32 devices in a mesh: seq: 8 (over z, x), head: 4 (over y, core).
Axes of the slice: x: 2, y: 2, z: 4, core: 2. Of those that a mesh axis runs over, the one named last changes fastest.
Arguments:
- inputs: bfloat16 [1, 2048, 1024], P(None, 'seq'), may hold values from -6 to 6
- cotangent: bfloat16 [1, 2048, 1024], P(None, 'seq'), may hold values from -6 to 6
- query_weight: bfloat16 [1024, 1024], P(None, 'head'), may hold values from -0.1875 to 0.1875
- key_weight: bfloat16 [1024, 1024], P(None, 'head'), may hold values from -0.1875 to 0.1875
- value_weight: bfloat16 [1024, 1024], P(None, 'head'), may hold values from -0.1875 to 0.1875
- output_weight: bfloat16 [1024, 1024], P('head'), may hold values from -1.5 to 1.5
- up_weight: bfloat16 [1024, 4096], P(None, 'head'), may hold values from -0.1875 to 0.1875
- down_weight: bfloat16 [4096, 1024], P('head'), may hold values from -0.09375 to 0.09375
- first_gain: float32 [1024], replicated, may hold values from 0.5 to 1.5
- second_gain: float32 [1024], replicated, may hold values from 0.5 to 1.5
- position_bias: float32 [8, 32], P('head'), may hold values from -3 to 3
- gate_bias: float32 [8], P('head'), may hold values from -2 to 2
- memory_table: bfloat16 [65536, 8, 256], P('seq', 'head'), may hold values from -6 to 6
- retrieved: int32 [1, 2048, 8, 32], P(None, 'seq', 'head'), may hold values from 0 to 65535, as said below
- lengths: int32 [1, 4], replicated, may hold values from 1 to 1024, 2048 in all within a row
Outputs:
- layer_out: bfloat16 [1, 2048, 1024], P(None, 'seq')
- input_grad: float32 [1, 2048, 1024], P(None, 'seq')
- query_grad: float32 [1024, 1024], P('seq', 'head')
- key_grad: float32 [1024, 1024], P('seq', 'head')
- value_grad: float32 [1024, 1024], P('seq', 'head')
- output_grad: float32 [1024, 1024], P('head', 'seq')
- up_grad: float32 [1024, 4096], P('seq', 'head')
- down_grad: float32 [4096, 1024], P('head', 'seq')
- first_gain_grad: float32 [1024], P('seq')
- second_gain_grad: float32 [1024], P('seq')
- position_grad: float32 [8, 32], P('head')
- gate_grad: float32 [8], P('head')
- rms_values: float32 [3], replicated
The draws below stay inside these ranges and needn't reach their ends.
Inputs may be any that keep to these rules, and one draw needn't show every extreme that they name: `retrieved`: for every stream, head and aligned block of 256 positions, each range of 8192 consecutive slots (starting at a multiple of 8192) holds exactly 1024 of the block's recalled slots. `lengths`: each row sums to 2048.
All inputs are finite; a program needn't handle non-finite values.
Results may differ from the reference program's by a relative error of at most 0.018.
Values may be sent and summed in bfloat16 or wider, within the bound.
A program may use at most 320 MiB of HBM per device.

```python
import math
import jax
import jax.numpy as jnp
import numpy as np
from jax import lax

D = 1024
HEADS = 8
DH = 128
FF = 4096
NB = 32
W = 512
TOPK = 32
MEM = 65536
BLK = 256
BATCH = 1
STREAM = 2048
MAXLEN = 1024
NDOC = 4
N_SEQ = 8


def draw_retrieved(key, part):
    key = jax.random.fold_in(key, 7)
    owner_key, slot_key = jax.random.split(key)
    base_list = jnp.repeat(jnp.arange(N_SEQ, dtype=jnp.int32), BLK * TOPK // N_SEQ)
    group_keys = jax.random.split(owner_key, BATCH * N_SEQ * HEADS)
    owners = jax.vmap(lambda group_key: jax.random.permutation(group_key, base_list))(group_keys)
    owners = owners.reshape(BATCH, N_SEQ, HEADS, BLK, TOPK).transpose(0, 1, 3, 2, 4).reshape(BATCH, N_SEQ * BLK, HEADS, TOPK)
    slot_local = jax.random.randint(slot_key, owners.shape, 0, MEM // N_SEQ, dtype=jnp.int32)
    return owners * (MEM // N_SEQ) + slot_local


def level_of(key, dims, shards, smallest, high):
    factor_of, own = 1.0, jax.random.fold_in(key, 6)
    for position, parts in shards:
        steps = jnp.exp(jax.random.uniform(jax.random.fold_in(own, position), (parts,), jnp.float32, smallest / len(shards), high / len(shards)))
        factor_of = factor_of * jnp.repeat(steps, dims[position] // parts).reshape([-1 if axis == position else 1 for axis in range(len(dims))])
    return factor_of


def length_profile(count, total, most, lean):
    loads = [(1 << 20) // math.isqrt(rank ** lean) + 1 for rank in range(2, count + 1)]
    spare, holding = total - most - (count - 1), [1] * (count - 1)
    while spare > 0:
        movable = [i for i in range(count - 1) if holding[i] < most]
        pool, budget = sum([loads[i] for i in movable]), spare
        for i in movable:
            more = min(most - holding[i], max(1, budget * loads[i] // pool), spare)
            holding[i] = holding[i] + more
            spare = spare - more
    return np.array([most] + holding)


def ragged(own_key, count, total, limit, lean):
    if count == 2:
        one = jax.random.randint(own_key, (), max(1, total - limit), min(limit, total - 1) + 1)
        return jnp.stack([one, total - one])
    sizes = jnp.asarray(length_profile(count, total, limit, lean), jnp.int32)
    twos = (count - 1) // 2
    giver, taker = sizes[1:1 + 2 * twos:2], sizes[2:2 + 2 * twos:2]
    room = jnp.minimum(giver - 1, limit - taker)
    shifted = jax.random.randint(jax.random.fold_in(own_key, 1), (twos,), 0, 1 << 20) % (room + 1)
    sizes = sizes.at[1:1 + 2 * twos:2].set(giver - shifted).at[2:2 + 2 * twos:2].set(taker + shifted)
    return sizes[jax.random.permutation(jax.random.fold_in(own_key, 2), count)]


def scatter_about(rng, shape, deviation, limit, cuts=(), kind=jnp.bfloat16):
    factor_of = level_of(rng, shape, cuts, -0.22, 0.18) if cuts else 1.0
    values = jax.random.normal(rng, shape, jnp.float32) * deviation * factor_of
    return jnp.minimum(jnp.maximum(values, -limit), limit).astype(kind)


def setup_inputs(seed: int = 0) -> dict:
    splits = jax.random.split(jax.random.key(seed), 16)
    inputs = scatter_about(splits[0], (BATCH, STREAM, D), 1.0, 6.0, ((1, 8),))
    cotangent = scatter_about(splits[1], (BATCH, STREAM, D), 1.0, 6.0, ((1, 8),))
    query_weight = scatter_about(splits[2], (D, HEADS * DH), D ** -0.5, 0.1875, ((1, 4),))
    key_weight = scatter_about(splits[3], (D, HEADS * DH), D ** -0.5, 0.1875, ((1, 4),))
    value_weight = scatter_about(splits[4], (D, HEADS * DH), D ** -0.5, 0.1875, ((1, 4),))
    output_weight = scatter_about(splits[5], (HEADS * DH, D), (HEADS * DH // 64) ** -0.5, 1.5, ((0, 4),))
    up_weight = scatter_about(splits[6], (D, FF), D ** -0.5, 0.1875, ((1, 4),))
    down_weight = scatter_about(splits[7], (FF, D), FF ** -0.5, 0.09375, ((0, 4),))
    first_gain = jnp.clip(1.0 + 0.1 * jax.random.normal(splits[8], (D,), jnp.float32), 0.5, 1.5)
    second_gain = jnp.clip(1.0 + 0.1 * jax.random.normal(splits[9], (D,), jnp.float32), 0.5, 1.5)
    position_bias = scatter_about(splits[10], (HEADS, NB), 0.5, 3.0, ((0, 4),), jnp.float32)
    gate_bias = jnp.clip(jax.random.uniform(splits[11], (HEADS,), jnp.float32, -2.0, 2.0) * level_of(splits[11], (HEADS,), ((0, 4),), -0.4, 0.0), -2.0, 2.0)
    memory_table = scatter_about(splits[12], (MEM, HEADS, 2 * DH), 1.0, 6.0, ((0, 8), (1, 4)))
    retrieved = draw_retrieved(jax.random.fold_in(splits[15], 71), 0)
    lengths = jax.vmap(lambda own: ragged(own, NDOC, STREAM, MAXLEN, 2))(jax.random.split(splits[14], BATCH)).reshape((BATCH, NDOC)).astype(jnp.int32)
    return dict(inputs=inputs, cotangent=cotangent, query_weight=query_weight, key_weight=key_weight, value_weight=value_weight, output_weight=output_weight, up_weight=up_weight, down_weight=down_weight, first_gain=first_gain, second_gain=second_gain, position_bias=position_bias, gate_bias=gate_bias, memory_table=memory_table, retrieved=retrieved, lengths=lengths)


eps = 1e-06
exact_span = 16
far_distance = 128
highest = lax.Precision.HIGHEST

@jax.custom_vjp
def low(v):
    return lax.optimization_barrier(v.astype(jnp.bfloat16)).astype(jnp.float32)

@jax.custom_vjp
def low_back(v):
    return v

def low_keep(v):
    return (low(v), None)

def low_pass(kept, grad):
    return (grad,)

def back_keep(v):
    return (v, None)

def back_low(kept, grad):
    return (low(grad),)
low.defvjp(low_keep, low_pass)
low_back.defvjp(back_keep, back_low)

def bucket_table(key_span, bucket_total):
    found = []
    for distance in range(key_span):
        if distance < exact_span:
            found.append(distance)
        else:
            scaled = math.log(distance / exact_span) / math.log(far_distance / exact_span)
            found.append(min(bucket_total - 1, exact_span + math.floor(scaled * (bucket_total - exact_span))))
    return np.asarray(found)

def window_layout(block_len, window_len, bucket_total):
    key_span = window_len + block_len
    delta = np.arange(block_len)[:, None] + window_len - np.arange(key_span)[None, :]
    in_window = (delta >= 0) & (delta < window_len)
    table = bucket_table(key_span, bucket_total)
    return (table[np.clip(delta, 0, key_span - 1)], in_window)

def rms_norm(values, gain):
    return values * lax.rsqrt(lax.optimization_barrier(jnp.mean(values * values, axis=-1, keepdims=True)) + eps) * gain

def softmax_rows(scores):
    top_score = lax.optimization_barrier(jnp.max(scores, axis=-1, keepdims=True))
    raised = jnp.exp(scores - top_score)
    return raised / lax.optimization_barrier(jnp.sum(raised, axis=-1, keepdims=True))

def reference(inputs, cotangent, query_weight, key_weight, value_weight, output_weight, up_weight, down_weight, first_gain, second_gain, position_bias, gate_bias, memory_table, retrieved, lengths):
    score_scale = DH ** (-0.5)
    bucket_index, in_window = window_layout(BLK, W, NB)
    positions = jnp.arange(STREAM, dtype=jnp.int32)
    doc_ends = jnp.cumsum(lengths, axis=-1).astype(jnp.int32)
    documents = lax.optimization_barrier(jnp.sum((doc_ends[:, None, :] <= positions[None, :, None]).astype(jnp.int32), axis=-1)).astype(jnp.int32)
    key_docs = jnp.pad(documents, ((0, 0), (W, 0)), constant_values=-1)
    head_index = jnp.arange(HEADS, dtype=jnp.int32)[None, None, :, None]

    def forward(tokens, w_query, w_key, w_value, w_output, w_up, w_down, gain_one, gain_two, bias_table, gate_logit):

        def project(left, weight):
            return jnp.einsum('bsd,de->bse', left, weight, precision=highest)
        normed_one = low(rms_norm(tokens, gain_one))
        queries = low_back(low(project(normed_one, w_query))).reshape(BATCH, STREAM, HEADS, DH)
        keys_all = low_back(low(project(normed_one, w_key))).reshape(BATCH, STREAM, HEADS, DH)
        values_all = low_back(low(project(normed_one, w_value))).reshape(BATCH, STREAM, HEADS, DH)
        keys_pad = jnp.pad(keys_all, ((0, 0), (W, 0), (0, 0), (0, 0)))
        values_pad = jnp.pad(values_all, ((0, 0), (W, 0), (0, 0), (0, 0)))
        bias_full = jnp.take(bias_table, jnp.asarray(bucket_index), axis=1)
        gate_values = jax.nn.sigmoid(gate_logit)[:, None]
        window_mask = jnp.asarray(in_window)[None, None]

        def block_out(index):
            start = index * BLK
            query_blk = lax.dynamic_slice_in_dim(queries, start, BLK, 1)
            key_blk = lax.dynamic_slice_in_dim(keys_pad, start, W + BLK, 1)
            value_blk = lax.dynamic_slice_in_dim(values_pad, start, W + BLK, 1)
            doc_query = lax.dynamic_slice_in_dim(documents, start, BLK, 1)
            doc_key = lax.dynamic_slice_in_dim(key_docs, start, W + BLK, 1)
            chosen = lax.dynamic_slice_in_dim(retrieved, start, BLK, 1)
            scores = jnp.einsum('bihd,bjhd->bhij', query_blk, key_blk, precision=highest) * score_scale + bias_full[None]
            scores = low_back(scores)
            allowed = window_mask & (doc_query[:, None, :, None] == doc_key[:, None, None, :])
            window_weights = softmax_rows(jnp.where(allowed, scores, -1e+30))
            local_out = jnp.einsum('bhij,bjhd->bihd', low(window_weights), value_blk, precision=highest)
            fetched = memory_table[chosen, head_index].astype(jnp.float32)
            recall_scores = jnp.einsum('bihd,bihkd->bihk', query_blk, fetched[..., :DH], precision=highest) * score_scale
            recall_weights = softmax_rows(low_back(recall_scores))
            recalled = jnp.einsum('bihk,bihkd->bihd', low(recall_weights), fetched[..., DH:], precision=highest)
            mixed = gate_values * recalled + (1.0 - gate_values) * local_out
            return mixed.reshape(BATCH, BLK, HEADS * DH)
        blocks = lax.map(jax.checkpoint(block_out), jnp.arange(N_SEQ, dtype=jnp.int32))
        attended = jnp.transpose(blocks, (1, 0, 2, 3)).reshape(BATCH, STREAM, HEADS * DH)
        attended = low_back(low(attended))
        branch_attn = low_back(project(attended, w_output))
        middle = tokens + branch_attn
        normed_two = low(rms_norm(middle, gain_two))
        hidden = low(jax.nn.gelu(low_back(project(normed_two, w_up))))
        branch_feed = low_back(project(hidden, w_down))
        return (middle + branch_feed, (branch_attn, branch_feed))
    primals = [array_in.astype(jnp.float32) for array_in in (inputs, query_weight, key_weight, value_weight, output_weight, up_weight, down_weight)]
    layer_sum, pullback, branches = jax.vjp(forward, *primals, first_gain, second_gain, position_bias, gate_bias, has_aux=True)
    grads = pullback(cotangent.astype(jnp.float32))
    branch_attn, branch_feed = branches
    rms_values = jnp.stack([jnp.sqrt(jnp.mean(layer_sum * layer_sum)), jnp.sqrt(jnp.mean(branch_attn * branch_attn)), jnp.sqrt(jnp.mean(branch_feed * branch_feed))])
    return (layer_sum.astype(jnp.bfloat16), grads[0], grads[1], grads[2], grads[3], grads[4], grads[5], grads[6], grads[7], grads[8], grads[9], grads[10], rms_values)
```

```python
import functools
import math

import jax
import jax.numpy as jnp
import numpy as np
from jax import lax
from jax.experimental import pallas as pl
from jax.experimental.pallas import tpu as pltpu
from jax.sharding import PartitionSpec as P

W = 512
eps = 1e-06
exact_span = 16
far_distance = 128
highest = lax.Precision.HIGHEST
f32 = jnp.float32
bf16 = jnp.bfloat16
NEG = -1e30
MIB = 2**20


def bucket_table(key_span, bucket_total):
    found = []
    for distance in range(key_span):
        if distance < exact_span:
            found.append(distance)
        else:
            scaled = math.log(distance / exact_span) / math.log(far_distance / exact_span)
            found.append(
                min(bucket_total - 1, exact_span + math.floor(scaled * (bucket_total - exact_span)))
            )
    return np.asarray(found)


def diagonal_buckets(block_len, bucket_total):
    span = W + block_len
    table = bucket_table(W, bucket_total)
    hot = np.zeros((bucket_total, span), np.float32)
    for u in range(1, W + 1):
        hot[table[W - u], u] = 1.0
    outside = np.where(hot.sum(0) > 0, 0.0, NEG).astype(np.float32)
    return hot, outside


def nt(a, b):
    return lax.dot_general(a, b, (((1,), (1,)), ((), ())), preferred_element_type=f32)


def nn(a, b):
    return lax.dot_general(a, b, (((1,), (0,)), ((), ())), preferred_element_type=f32)


def tn(a, b):
    return lax.dot_general(a, b, (((0,), (0,)), ((), ())), preferred_element_type=f32)


def gather_kernel(codes_ref, table_ref, out_ref, wide, buf, *, rows, chunk, chunks, unroll, group):
    step = pl.program_id(0)
    part = 32

    @pl.when(step < chunks)
    def _():
        def widen(q, carry):
            x = table_ref[pl.ds(q * part, part)].astype(f32)
            base = step * chunk + q * part
            for r in range(part):
                wide[pl.ds(4 * (base + r), 2), :] = x[r, :, 0:128]
                wide[pl.ds(4 * (base + r) + 2, 2), :] = x[r, :, 128:256]
            return carry

        lax.fori_loop(0, chunk // part, widen, 0)

    @pl.when(step >= chunks)
    def _():
        head = (step - chunks) % 2

        def copy_rows(i, carry):
            base = i * unroll
            for g in range(0, unroll, group):
                found = [
                    wide[pl.ds(codes_ref[0, 0, 0, base + g + u] * 4 + head, 2, 2), :]
                    for u in range(group)
                ]
                for u in range(group):
                    buf[pl.ds(2 * (base + g + u), 2), :] = found[u]
            return carry

        lax.fori_loop(0, rows // unroll, copy_rows, 0)
        out_ref[0, 0, :, 0:128] = buf[pl.ds(0, rows, 2), :].astype(bf16)
        out_ref[0, 0, :, 128:256] = buf[pl.ds(1, rows, 2), :].astype(bf16)


def gather_rows(slots, table):
    parts, heads, rows = slots.shape
    total = table.shape[0]
    chunk = min(1024, total)
    chunks = total // chunk
    unroll = min(64, rows)

    def place(i):
        at = jnp.maximum(i - chunks, 0)
        return (at // 2, at % 2, 0, 0)

    return pl.pallas_call(
        functools.partial(
            gather_kernel, rows=rows, chunk=chunk, chunks=chunks, unroll=unroll, group=unroll // 2
        ),
        out_shape=jax.ShapeDtypeStruct((parts, heads, rows, 256), bf16),
        grid=(chunks + parts * heads,),
        in_specs=[
            pl.BlockSpec((1, 1, 1, rows), place, memory_space=pltpu.SMEM),
            pl.BlockSpec((chunk, 2, 256), lambda i: (jnp.minimum(i, chunks - 1), 0, 0)),
        ],
        out_specs=pl.BlockSpec((1, 1, rows, 256), place),
        scratch_shapes=[pltpu.VMEM((4 * total, 128), f32), pltpu.VMEM((2 * rows, 128), f32)],
        compiler_params=pltpu.CompilerParams(vmem_limit_bytes=40 * MIB),
        cost_estimate=pl.CostEstimate(flops=0, bytes_accessed=100 * MIB, transcendentals=0),
        name="gather_rows",
    )(slots.reshape(parts, heads, 1, rows), table)


def recall_fwd_kernel(q_ref, rows_ref, tok_ref, o_ref, st_ref, *, scale):
    count, rows = q_ref.shape[1], rows_ref.shape[2]
    ids = lax.broadcasted_iota(jnp.int32, (count, rows), 0)
    logs = []
    for h in range(2):
        cols = slice(h * 128, h * 128 + 128)
        keep = tok_ref[0, h : h + 1, :] == ids
        s = jnp.where(keep, nt(q_ref[0, :, cols], rows_ref[0, h, :, 0:128]) * scale, NEG)
        top = jnp.max(s, axis=1, keepdims=True)
        p = jnp.where(keep, jnp.exp(s - top), 0.0)
        total = jnp.sum(p, axis=1, keepdims=True)
        some = total > 0.0
        safe = jnp.where(some, total, 1.0)
        o = nn(p.astype(bf16), rows_ref[0, h, :, 128:256]) / safe
        o_ref[0, h] = o.astype(bf16)
        logs.append(jnp.where(some, top + jnp.log(safe), NEG))
    lane = lax.broadcasted_iota(jnp.int32, (count, 128), 1)
    st_ref[0] = jnp.where(lane == 0, logs[0], logs[1]).T[0:8]


def recall_fwd(q_all, rows, tok):
    parts, count, width = q_all.shape
    per = rows.shape[2]
    return pl.pallas_call(
        functools.partial(recall_fwd_kernel, scale=128**-0.5),
        out_shape=(
            jax.ShapeDtypeStruct((parts, 2, count, 128), bf16),
            jax.ShapeDtypeStruct((parts, 8, count), f32),
        ),
        grid=(parts,),
        in_specs=[
            pl.BlockSpec((1, count, width), lambda i: (i, 0, 0)),
            pl.BlockSpec((1, 2, per, 256), lambda i: (i, 0, 0, 0)),
            pl.BlockSpec((1, 2, per), lambda i: (i, 0, 0)),
        ],
        out_specs=(
            pl.BlockSpec((1, 2, count, 128), lambda i: (i, 0, 0, 0)),
            pl.BlockSpec((1, 8, count), lambda i: (i, 0, 0)),
        ),
        compiler_params=pltpu.CompilerParams(vmem_limit_bytes=40 * MIB),
        name="recall_fwd",
    )(q_all, rows, tok)


def recall_bwd_kernel(gate_ref, q_ref, g_ref, st_ref, rows_ref, tok_ref, dq_ref, *, scale):
    count, rows = q_ref.shape[1], rows_ref.shape[2]
    ids = lax.broadcasted_iota(jnp.int32, (count, rows), 0)
    stats = st_ref[0].T
    for h in range(2):
        cols = slice(h * 128, h * 128 + 128)
        keep = tok_ref[0, h : h + 1, :] == ids
        s = nt(q_ref[0, :, cols], rows_ref[0, h, :, 0:128]) * scale
        p = jnp.exp(jnp.where(keep, s - stats[:, h : h + 1], NEG))
        e = nt(g_ref[0, :, cols], rows_ref[0, h, :, 128:256]) * gate_ref[h]
        ds = (p * (e - stats[:, 2 + h : 3 + h])).astype(bf16)
        dq_ref[0, h] = (nn(ds, rows_ref[0, h, :, 0:128]) * scale).astype(bf16)


def recall_bwd(gate, q_all, g_all, stats, rows, tok):
    parts, count, width = q_all.shape
    per = rows.shape[2]
    return pl.pallas_call(
        functools.partial(recall_bwd_kernel, scale=128**-0.5),
        out_shape=jax.ShapeDtypeStruct((parts, 2, count, 128), bf16),
        grid=(parts,),
        in_specs=[
            pl.BlockSpec(memory_space=pltpu.SMEM),
            pl.BlockSpec((1, count, width), lambda i: (i, 0, 0)),
            pl.BlockSpec((1, count, width), lambda i: (i, 0, 0)),
            pl.BlockSpec((1, 8, count), lambda i: (i, 0, 0)),
            pl.BlockSpec((1, 2, per, 256), lambda i: (i, 0, 0, 0)),
            pl.BlockSpec((1, 2, per), lambda i: (i, 0, 0)),
        ],
        out_specs=pl.BlockSpec((1, 2, count, 128), lambda i: (i, 0, 0, 0)),
        compiler_params=pltpu.CompilerParams(vmem_limit_bytes=40 * MIB),
        name="recall_bwd",
    )(gate, q_all, g_all, stats, rows, tok)


def doc_starts(lengths_ref, first, count):
    place = first + lax.broadcasted_iota(jnp.int32, (count, 1), 0)
    start = jnp.zeros((count, 1), jnp.int32)
    end = jnp.int32(0)
    for c in range(lengths_ref.shape[0]):
        end = end + lengths_ref[c]
        start = jnp.where(end <= place, end, start)
    return start


def window_fwd_kernel(place_ref, lengths_ref, q_ref, k_ref, v_ref, bias_ref, o_ref, p_ref, *, scale):
    count, span = q_ref.shape[0], k_ref.shape[0]
    first = place_ref[0] * count
    start = doc_starts(lengths_ref, first, count)
    key_place = first - W + lax.broadcasted_iota(jnp.int32, (count, span), 1)
    seen = key_place >= start
    for h in range(2):
        cols = slice(h * 128, h * 128 + 128)
        bias = pltpu.roll(
            jnp.broadcast_to(bias_ref[h : h + 1, :], (count, span)), 0, 1, stride=1, stride_axis=0
        )
        s = nt(q_ref[:, cols], k_ref[:, cols]) * scale + bias
        s = jnp.where(seen, s, NEG)
        top = jnp.max(s, axis=1, keepdims=True)
        raised = jnp.exp(s - top)
        p = raised / jnp.sum(raised, axis=1, keepdims=True)
        p_ref[h] = p
        o_ref[:, cols] = nn(p.astype(bf16), v_ref[:, cols])


def window_fwd(place, lengths, q, k, v, bias):
    count, span = q.shape[0], k.shape[0]
    smem = pl.BlockSpec(memory_space=pltpu.SMEM)
    vmem = pl.BlockSpec(memory_space=pltpu.VMEM)
    return pl.pallas_call(
        functools.partial(window_fwd_kernel, scale=128**-0.5),
        out_shape=(
            jax.ShapeDtypeStruct((count, 256), f32),
            jax.ShapeDtypeStruct((2, count, span), f32),
        ),
        in_specs=[smem, smem, vmem, vmem, vmem, vmem],
        out_specs=(vmem, vmem),
        compiler_params=pltpu.CompilerParams(vmem_limit_bytes=40 * MIB),
        name="window_fwd",
    )(place, lengths, q, k, v, bias)


def window_bwd_kernel(gate_ref, p_ref, g_ref, q_ref, k_ref, v_ref, dq_ref, dk_ref, dv_ref, pos_ref, *, scale):
    count, span = q_ref.shape[0], k_ref.shape[0]
    for h in range(2):
        cols = slice(h * 128, h * 128 + 128)
        rest = 1.0 - gate_ref[h]
        p = p_ref[h]
        e = nt(g_ref[:, cols], v_ref[:, cols]) * rest
        delta = jnp.sum(p * e, axis=1, keepdims=True)
        ds = (p * (e - delta)).astype(bf16)
        dq_ref[:, cols] = nn(ds, k_ref[:, cols]) * scale
        dk_ref[:, cols] = tn(ds, q_ref[:, cols]) * scale
        dv_ref[:, cols] = tn(p.astype(bf16), g_ref[:, cols]) * rest
        low = ds.astype(f32)
        acc = low[0:8]
        for a in range(1, count // 8):
            acc = acc + pltpu.roll(low[8 * a : 8 * a + 8], (span - 8 * a) % span, 1)
        row = acc[0:1]
        for b in range(1, 8):
            row = row + pltpu.roll(acc[b : b + 1], span - b, 1)
        pos_ref[h : h + 1, :] = row


def window_bwd(gate, p, g, q, k, v):
    count, span = q.shape[0], k.shape[0]
    smem = pl.BlockSpec(memory_space=pltpu.SMEM)
    vmem = pl.BlockSpec(memory_space=pltpu.VMEM)
    return pl.pallas_call(
        functools.partial(window_bwd_kernel, scale=128**-0.5),
        out_shape=(
            jax.ShapeDtypeStruct((count, 256), f32),
            jax.ShapeDtypeStruct((span, 256), f32),
            jax.ShapeDtypeStruct((span, 256), f32),
            jax.ShapeDtypeStruct((2, span), f32),
        ),
        in_specs=[smem] + [vmem] * 5,
        out_specs=(vmem,) * 4,
        compiler_params=pltpu.CompilerParams(vmem_limit_bytes=40 * MIB),
        name="window_bwd",
    )(gate, p, g, q, k, v)


def from_behind(value, axis, steps):
    count = lax.axis_size(axis)
    first, last = (max(0, -steps), min(count, count - steps))
    return lax.ppermute(value, axis, [(source, source + steps) for source in range(first, last)])


def norm_stats(values):
    row_scale = lax.rsqrt(jnp.mean(values * values, axis=-1, keepdims=True) + eps)
    return (values * row_scale, row_scale)


def norm_back(grad_normed, gain, normed_hat, row_scale):
    grad_hat = grad_normed * gain
    inner = jnp.mean(grad_hat * normed_hat, axis=-1, keepdims=True)
    return row_scale * (grad_hat - normed_hat * inner)


def exchange(value):
    return lax.all_to_all(value, "seq", split_axis=0, concat_axis=0, tiled=True)


def head_sum(value):
    return lax.psum(value.astype(bf16), "head").astype(f32)


def per_device(
    inputs,
    cotangent,
    query_weight,
    key_weight,
    value_weight,
    output_weight,
    up_weight,
    down_weight,
    first_gain,
    second_gain,
    position_bias,
    gate_bias,
    memory_table,
    retrieved,
    lengths,
):
    _, block_len, model_width = inputs.shape
    bucket_total = position_bias.shape[1]
    hop_count = W // block_len
    seq_count = lax.axis_size("seq")
    place = lax.axis_index("seq").astype(jnp.int32).reshape(1)
    slot_count = memory_table.shape[0]

    wanted = jnp.transpose(retrieved[0], (1, 0, 2))
    token = jnp.arange(block_len, dtype=jnp.int32)[None, :, None]
    codes = (wanted // slot_count) * (block_len * slot_count) + token * slot_count + wanted % slot_count
    codes = lax.sort(codes.reshape(2, -1), dimension=1, is_stable=False)
    codes = jnp.transpose(codes.reshape(2, seq_count, -1), (1, 0, 2))
    codes = exchange(codes)
    slots = codes % slot_count
    tok = (codes // slot_count) % block_len
    rows = gather_rows(slots, memory_table)

    hot, outside = diagonal_buckets(block_len, bucket_total)
    bias_row = jnp.dot(position_bias, hot, precision=highest) + outside[None]

    tokens = inputs[0].astype(f32)
    cot = cotangent[0]
    hat_one, scale_one = norm_stats(tokens)
    normed_one = (hat_one * first_gain).astype(bf16)
    queries = nn(normed_one, query_weight).astype(bf16)
    keys = nn(normed_one, key_weight).astype(bf16)
    values = nn(normed_one, value_weight).astype(bf16)
    q_all = lax.all_gather(queries, "seq", axis=0)
    pair = jnp.stack((keys, values))
    pieces = [pair] + [from_behind(pair, "seq", hop) for hop in range(1, hop_count + 1)]
    pair_window = jnp.concatenate(pieces[::-1], axis=1)
    key_window, value_window = pair_window[0], pair_window[1]

    local_out, window_weights = window_fwd(place, lengths[0], queries, key_window, value_window, bias_row)

    part_out, part_log = recall_fwd(q_all, rows, tok)
    got_out = exchange(part_out)
    got_log = exchange(part_log)[:, 0:2]
    log_total = jax.nn.logsumexp(got_log, axis=0)
    shares = jnp.exp(got_log - log_total[None])
    recalled = jnp.sum(shares[..., None] * got_out.astype(f32), axis=0)
    recalled = jnp.transpose(recalled, (1, 0, 2)).reshape(block_len, 256)

    gate_flat = jax.nn.sigmoid(gate_bias)
    gate_wide = jnp.repeat(gate_flat, 128)[None]
    mixed = (gate_wide * recalled + (1.0 - gate_wide) * local_out).astype(bf16)
    branch_attn = head_sum(nn(mixed, output_weight))
    middle = tokens + branch_attn
    hat_two, scale_two = norm_stats(middle)
    normed_two = (hat_two * second_gain).astype(bf16)
    upward = nn(normed_two, up_weight)
    gelu_value, gelu_back = jax.vjp(jax.nn.gelu, upward)
    hidden = gelu_value.astype(bf16)
    branch_feed = head_sum(nn(hidden, down_weight))
    layer_sum = middle + branch_feed
    grad_upward = gelu_back(nt(cot, down_weight))[0].astype(bf16)
    grad_normed_two = head_sum(nt(grad_upward, up_weight))
    feed_grads = jnp.concatenate((tn(normed_two, grad_upward), tn(cot, hidden)), axis=1).astype(bf16)
    feed_grads = lax.psum_scatter(feed_grads, "seq", scatter_dimension=0, tiled=True).astype(f32)

    second_gain_part = jnp.sum(grad_normed_two * hat_two, axis=0)
    grad_middle = cot.astype(f32) + norm_back(grad_normed_two, second_gain, hat_two, scale_two)
    grad_branch = grad_middle.astype(bf16)
    grad_mixed = nt(grad_branch, output_weight).astype(bf16)
    grad_wide = grad_mixed.astype(f32)
    gate_part = jnp.sum((grad_wide * (recalled - local_out)).reshape(block_len, 2, 128), axis=(0, 2))
    gate_part = gate_part * gate_flat * (1.0 - gate_flat)
    delta = jnp.sum((grad_wide * gate_wide * recalled).reshape(block_len, 2, 128), axis=2).T
    stats = jnp.concatenate((log_total, delta, jnp.zeros((4, block_len), f32)), axis=0)
    g_all = lax.all_gather(grad_mixed, "seq", axis=0)
    stats_all = lax.all_gather(stats, "seq", axis=0)

    dq_window, dk_window, dv_window, pos_rows = window_bwd(
        gate_flat, window_weights, grad_mixed, queries, key_window, value_window
    )
    grad_pair = jnp.stack((dk_window, dv_window))
    own = grad_pair[:, W:]
    for hop in range(1, hop_count + 1):
        piece = grad_pair[:, W - hop * block_len : W - (hop - 1) * block_len].astype(bf16)
        own = own + from_behind(piece, "seq", -hop).astype(f32)
    grad_keys, grad_values = own[0].astype(bf16), own[1].astype(bf16)

    dq_parts = exchange(recall_bwd(gate_flat, q_all, g_all, stats_all, rows, tok))
    dq_recall = jnp.transpose(jnp.sum(dq_parts.astype(f32), axis=0), (1, 0, 2)).reshape(block_len, 256)
    grad_queries = (dq_window + dq_recall).astype(bf16)

    attn_grads = jnp.concatenate(
        (
            tn(normed_one, grad_queries),
            tn(normed_one, grad_keys),
            tn(normed_one, grad_values),
            tn(grad_branch, mixed),
        ),
        axis=1,
    ).astype(bf16)
    attn_grads = lax.psum_scatter(attn_grads, "seq", scatter_dimension=0, tiled=True).astype(f32)
    grad_normed_one = head_sum(
        nt(grad_queries, query_weight) + nt(grad_keys, key_weight) + nt(grad_values, value_weight)
    )
    first_gain_part = jnp.sum(grad_normed_one * hat_one, axis=0)
    input_grad = grad_middle + norm_back(grad_normed_one, first_gain, hat_one, scale_one)

    position_part = jnp.dot(pos_rows, hot.T, precision=highest)
    square_parts = jnp.stack(
        [
            jnp.sum(layer_sum * layer_sum),
            jnp.sum(branch_attn * branch_attn),
            jnp.sum(branch_feed * branch_feed),
        ]
    )
    position_grad, gate_grad, square_sums, gain_sums = lax.psum(
        (position_part, gate_part, square_parts, jnp.stack((first_gain_part, second_gain_part))), "seq"
    )
    entry_count = float(block_len * model_width * seq_count)
    share = model_width // seq_count
    own_gains = lax.dynamic_slice_in_dim(gain_sums, place[0] * share, share, 1)
    return (
        layer_sum.astype(bf16)[None],
        input_grad[None],
        attn_grads[:, 0:256],
        attn_grads[:, 256:512],
        attn_grads[:, 512:768],
        attn_grads[:, 768:1024].T,
        feed_grads[:, : up_weight.shape[1]],
        feed_grads[:, up_weight.shape[1] :].T,
        own_gains[0],
        own_gains[1],
        position_grad,
        gate_grad,
        jnp.sqrt(square_sums / entry_count),
    )


def solution(mesh):
    in_specs = (
        P(None, "seq", None),
        P(None, "seq", None),
        P(None, "head"),
        P(None, "head"),
        P(None, "head"),
        P("head", None),
        P(None, "head"),
        P("head", None),
        P(),
        P(),
        P("head", None),
        P("head"),
        P("seq", "head", None),
        P(None, "seq", "head", None),
        P(),
    )
    out_specs = (
        P(None, "seq", None),
        P(None, "seq", None),
        P("seq", "head"),
        P("seq", "head"),
        P("seq", "head"),
        P("head", "seq"),
        P("seq", "head"),
        P("head", "seq"),
        P("seq"),
        P("seq"),
        P("head", None),
        P("head"),
        P(),
    )
    return jax.shard_map(
        per_device, mesh=mesh, in_specs=in_specs, out_specs=out_specs, check_vma=False
    )
```

```python
import functools
import math

import jax
import jax.numpy as jnp
import numpy as np
from jax import lax
from jax.experimental import pallas as pl
from jax.experimental.pallas import tpu as pltpu
from jax.sharding import PartitionSpec as P

W = 512
eps = 1e-06
exact_span = 16
far_distance = 128
highest = lax.Precision.HIGHEST
f32 = jnp.float32
bf16 = jnp.bfloat16
NEG = -1e30
MIB = 2**20


def bucket_table(key_span, bucket_total):
    found = []
    for distance in range(key_span):
        if distance < exact_span:
            found.append(distance)
        else:
            scaled = math.log(distance / exact_span) / math.log(far_distance / exact_span)
            found.append(
                min(bucket_total - 1, exact_span + math.floor(scaled * (bucket_total - exact_span)))
            )
    return np.asarray(found)


def diagonal_buckets(block_len, bucket_total):
    span = W + block_len
    table = bucket_table(W, bucket_total)
    hot = np.zeros((bucket_total, span), np.float32)
    for u in range(1, W + 1):
        hot[table[W - u], u] = 1.0
    outside = np.where(hot.sum(0) > 0, 0.0, NEG).astype(np.float32)
    return hot, outside


def nt(a, b):
    return lax.dot_general(a, b, (((1,), (1,)), ((), ())), preferred_element_type=f32)


def nn(a, b):
    return lax.dot_general(a, b, (((1,), (0,)), ((), ())), preferred_element_type=f32)


def tn(a, b):
    return lax.dot_general(a, b, (((0,), (0,)), ((), ())), preferred_element_type=f32)


def gather_kernel(codes_ref, table_ref, out_ref, wide, buf, *, rows, chunk, chunks, unroll, group):
    step = pl.program_id(0)
    part = 32

    @pl.when(step < chunks)
    def _():
        def widen(q, carry):
            x = table_ref[pl.ds(q * part, part)].astype(f32)
            base = step * chunk + q * part
            for r in range(part):
                wide[pl.ds(4 * (base + r), 2), :] = x[r, :, 0:128]
                wide[pl.ds(4 * (base + r) + 2, 2), :] = x[r, :, 128:256]
            return carry

        lax.fori_loop(0, chunk // part, widen, 0)

    @pl.when(step >= chunks)
    def _():
        head = (step - chunks) % 2

        def copy_rows(i, carry):
            base = i * unroll
            for g in range(0, unroll, group):
                found = [
                    wide[pl.ds(codes_ref[0, 0, 0, base + g + u] * 4 + head, 2, 2), :]
                    for u in range(group)
                ]
                for u in range(group):
                    buf[pl.ds(2 * (base + g + u), 2), :] = found[u]
            return carry

        lax.fori_loop(0, rows // unroll, copy_rows, 0)
        out_ref[0, 0, :, 0:128] = buf[pl.ds(0, rows, 2), :].astype(bf16)
        out_ref[0, 0, :, 128:256] = buf[pl.ds(1, rows, 2), :].astype(bf16)


def gather_rows(slots, table):
    parts, heads, rows = slots.shape
    total = table.shape[0]
    chunk = min(1024, total)
    chunks = total // chunk
    unroll = min(64, rows)

    def place(i):
        at = jnp.maximum(i - chunks, 0)
        return (at // 2, at % 2, 0, 0)

    return pl.pallas_call(
        functools.partial(
            gather_kernel, rows=rows, chunk=chunk, chunks=chunks, unroll=unroll, group=unroll // 2
        ),
        out_shape=jax.ShapeDtypeStruct((parts, heads, rows, 256), bf16),
        grid=(chunks + parts * heads,),
        in_specs=[
            pl.BlockSpec((1, 1, 1, rows), place, memory_space=pltpu.SMEM),
            pl.BlockSpec((chunk, 2, 256), lambda i: (jnp.minimum(i, chunks - 1), 0, 0)),
        ],
        out_specs=pl.BlockSpec((1, 1, rows, 256), place),
        scratch_shapes=[pltpu.VMEM((4 * total, 128), f32), pltpu.VMEM((2 * rows, 128), f32)],
        compiler_params=pltpu.CompilerParams(vmem_limit_bytes=40 * MIB),
        cost_estimate=pl.CostEstimate(flops=0, bytes_accessed=100 * MIB, transcendentals=0),
        name="gather_rows",
    )(slots.reshape(parts, heads, 1, rows), table)


MESH = pl.DeviceIdType.MESH


def greet(**counts):
    barrier = pltpu.get_barrier_semaphore()
    for axis, count in counts.items():
        me = lax.axis_index(axis)

        def call(d, carry, axis=axis, count=count, me=me):
            peer = lax.rem(me + d, count)
            pl.semaphore_signal(barrier, inc=1, device_id={axis: peer}, device_id_type=MESH)
            return carry

        lax.fori_loop(1, count, call, 0)
    pl.semaphore_wait(barrier, sum(counts.values()) - len(counts))


def send(src, dst, send_sem, recv_sem, axis, peer):
    return pltpu.make_async_remote_copy(
        src_ref=src,
        dst_ref=dst,
        send_sem=send_sem,
        recv_sem=recv_sem,
        device_id={axis: peer},
        device_id_type=MESH,
    )


def doc_starts(lengths_ref, first, count):
    place = first + lax.broadcasted_iota(jnp.int32, (count, 1), 0)
    start = jnp.zeros((count, 1), jnp.int32)
    end = jnp.int32(0)
    for c in range(lengths_ref.shape[0]):
        end = end + lengths_ref[c]
        start = jnp.where(end <= place, end, start)
    return start


def head_cols(h):
    return slice(h * 128, h * 128 + 128)


def row_form(columns, count):
    lane = lax.broadcasted_iota(jnp.int32, (count, 128), 1)
    wide = jnp.zeros((count, 128), f32)
    for i, column in enumerate(columns):
        wide = jnp.where(lane == i, column, wide)
    return wide


def attend_kernel(
    lengths_ref,
    gate_ref,
    q_ref,
    k_ref,
    v_ref,
    bias_ref,
    q_all_ref,
    tok_ref,
    rows_hbm,
    mixed_ref,
    recalled_ref,
    local_ref,
    logs_ref,
    p_ref,
    pair_ref,
    rows,
    out_send,
    out_recv,
    log_send,
    log_recv,
    rows_sem,
    out_ss,
    out_rs,
    log_ss,
    log_rs,
    pair_ss,
    pair_rs,
    *,
    parts,
    scale,
):
    count, span = q_ref.shape[0], pair_ref.shape[1]
    hops = W // count
    per = tok_ref.shape[2]

    def fetch(d, j):
        return pltpu.make_async_copy(rows_hbm.at[j], rows.at[d], rows_sem.at[d])

    me = lax.axis_index("seq")

    def fetch_start(d, carry):
        fetch(d, lax.rem(me + d, parts)).start()
        return carry

    lax.fori_loop(1, parts, fetch_start, 0)
    fetch(0, me).start()
    pair_ref[0, W:, :] = k_ref[...]
    pair_ref[1, W:, :] = v_ref[...]
    greet(seq=parts)

    def hand_on(hop):
        return send(
            pair_ref.at[:, pl.ds(W, count)],
            pair_ref.at[:, pl.ds(W - hop * count, count)],
            pair_ss.at[hop - 1],
            pair_rs.at[hop - 1],
            "seq",
            lax.rem(me + hop, parts),
        )

    for hop in range(1, hops + 1):
        hand_on(hop).start()

    ids = lax.broadcasted_iota(jnp.int32, (count, per), 0)

    def owner_part(d, j, out, logs):
        fetch(d, j).wait()
        found = []
        for h in range(2):
            cols = head_cols(h)
            keep = tok_ref[j, h : h + 1, :] == ids
            s = jnp.where(keep, nt(q_all_ref[j, :, cols], rows[d, h, :, 0:128]) * scale, NEG)
            top = jnp.max(s, axis=1, keepdims=True)
            p = jnp.where(keep, jnp.exp(s - top), 0.0)
            total = jnp.sum(p, axis=1, keepdims=True)
            some = total > 0.0
            safe = jnp.where(some, total, 1.0)
            out[d, h] = (nn(p.astype(bf16), rows[d, h, :, 128:256]) / safe).astype(bf16)
            found.append(jnp.where(some, top + jnp.log(safe), NEG))
        logs[d] = row_form(found, count).T[0:8]

    def send_out(d):
        peer = lax.rem(me + d, parts)
        return send(out_send.at[d], out_recv.at[d], out_ss.at[d], out_rs.at[d], "seq", peer)

    def send_log(d):
        peer = lax.rem(me + d, parts)
        return send(log_send.at[d], log_recv.at[d], log_ss.at[d], log_rs.at[d], "seq", peer)

    def serve(d, carry):
        owner_part(d, lax.rem(me + d, parts), out_send, log_send)
        send_log(d).start()
        send_out(d).start()
        return carry

    lax.fori_loop(1, parts, serve, 0)
    owner_part(0, me, out_recv, log_recv)

    for hop in range(1, hops + 1):
        hand_on(hop).wait()
    first = me * count
    start = doc_starts(lengths_ref, first, count)
    key_place = first - W + lax.broadcasted_iota(jnp.int32, (count, span), 1)
    seen = key_place >= start
    for h in range(2):
        cols = head_cols(h)
        bias = pltpu.roll(
            jnp.broadcast_to(bias_ref[h : h + 1, :], (count, span)), 0, 1, stride=1, stride_axis=0
        )
        s = nt(q_ref[:, cols], pair_ref[0, :, cols]) * scale + bias
        s = jnp.where(seen, s, NEG)
        raised = jnp.exp(s - jnp.max(s, axis=1, keepdims=True))
        p = raised / jnp.sum(raised, axis=1, keepdims=True)
        p_ref[h] = p
        local_ref[:, cols] = nn(p.astype(bf16), pair_ref[1, :, cols])

    def wait_log(d, carry):
        send_log(d).wait()
        return carry

    lax.fori_loop(1, parts, wait_log, 0)

    def top_of(d, top):
        return jnp.maximum(top, log_recv[d])

    top = lax.fori_loop(1, parts, top_of, log_recv[0])

    def add_to(d, total):
        return total + jnp.exp(log_recv[d] - top)

    total = lax.fori_loop(1, parts, add_to, jnp.exp(log_recv[0] - top))
    logs = top + jnp.log(total)
    logs_ref[...] = logs

    def merge(d):
        share = jnp.exp(log_recv[d] - logs).T
        for h in range(2):
            cols = head_cols(h)
            recalled_ref[:, cols] += share[:, h : h + 1] * out_recv[d, h].astype(f32)

    recalled_ref[...] = jnp.zeros_like(recalled_ref)
    merge(0)

    def merge_next(d, carry):
        send_out(d).wait()
        merge(d)
        return carry

    lax.fori_loop(1, parts, merge_next, 0)
    for h in range(2):
        cols = head_cols(h)
        gate = gate_ref[h]
        mixed = gate * recalled_ref[:, cols] + (1.0 - gate) * local_ref[:, cols]
        mixed_ref[:, cols] = mixed.astype(bf16)


def attend(lengths, gate, q, k, v, bias, q_all, tok, rows):
    parts, count, width = q_all.shape
    span, hops = W + count, W // count
    smem = pl.BlockSpec(memory_space=pltpu.SMEM)
    vmem = pl.BlockSpec(memory_space=pltpu.VMEM)
    dma = pltpu.SemaphoreType.DMA
    return pl.pallas_call(
        functools.partial(attend_kernel, parts=parts, scale=128**-0.5),
        out_shape=(
            jax.ShapeDtypeStruct((count, width), bf16),
            jax.ShapeDtypeStruct((count, width), f32),
            jax.ShapeDtypeStruct((count, width), f32),
            jax.ShapeDtypeStruct((8, count), f32),
            jax.ShapeDtypeStruct((2, count, span), f32),
            jax.ShapeDtypeStruct((2, span, width), bf16),
        ),
        in_specs=[smem, smem] + [vmem] * 6 + [pl.BlockSpec(memory_space=pl.ANY)],
        out_specs=(vmem,) * 6,
        scratch_shapes=[
            pltpu.VMEM(rows.shape, bf16),
            pltpu.VMEM((parts, 2, count, 128), bf16),
            pltpu.VMEM((parts, 2, count, 128), bf16),
            pltpu.VMEM((parts, 8, count), f32),
            pltpu.VMEM((parts, 8, count), f32),
        ]
        + [dma((parts,))] * 5
        + [dma((hops,))] * 2,
        compiler_params=pltpu.CompilerParams(
            vmem_limit_bytes=56 * MIB, collective_id=1, has_side_effects=True
        ),
        cost_estimate=pl.CostEstimate(
            flops=3 * 10**9, bytes_accessed=100 * MIB, transcendentals=5 * 10**6
        ),
        name="attend",
    )(lengths, gate, q, k, v, bias, q_all, tok, rows)


class ScatterSum:
    def __init__(self, grads, sems, parts):
        self.grads, self.sems = grads, sems
        self.quarter = parts // 4
        self.own = grads[0][0].shape[0] // parts
        me = lax.axis_index("seq")
        self.x, self.b, self.a = lax.rem(me, 2), lax.rem(me // 2, 2), me // 4

    def place(self, da, side, x):
        b = self.b if side == 1 else 1 - self.b
        return 4 * lax.rem(self.a + da, self.quarter) + 2 * b + x

    def rows_of(self, place):
        return pl.ds(pl.multiple_of(place * self.own, self.own), self.own)

    def send_x(self, k, da, side):
        ss, rs = self.sems[0:2]
        return send(
            self.grads[k][0].at[self.rows_of(self.place(da, side, 1 - self.x))],
            self.grads[k][1].at[side, da],
            ss.at[k, side, da],
            rs.at[k, side, da],
            "seq",
            self.place(0, 1, 1 - self.x),
        )

    def send_pair(self, k, da):
        ss, rs = self.sems[2:4]
        grads, peer = self.grads[k], self.place(0, 0, self.x)
        return send(grads[2].at[da], grads[3].at[da], ss.at[k, da], rs.at[k, da], "seq", peer)

    def send_far(self, k, da):
        ss, rs = self.sems[4:6]
        grads, peer = self.grads[k], self.place(da, 1, self.x)
        return send(grads[4].at[da], grads[5].at[da], ss.at[k, da], rs.at[k, da], "seq", peer)

    def loop(self, first, last, step):
        def body(da, carry):
            for k in range(len(self.grads)):
                step(k, da)
            return carry

        lax.fori_loop(first, last, body, 0)

    def span(self, far):
        return (1, self.quarter) if far else (0, 1)

    def start(self, far, side):
        self.loop(*self.span(far), lambda k, da: self.send_x(k, da, side).start())

    def column(self, k, da, side):
        self.send_x(k, da, side).wait()
        mine = self.grads[k][0][self.rows_of(self.place(da, side, self.x)), :]
        return mine.astype(f32) + self.grads[k][1][side, da].astype(f32)

    def pair(self, far):
        def step(k, da):
            self.grads[k][2][da] = self.column(k, da, 0).astype(bf16)
            self.send_pair(k, da).start()

        self.loop(*self.span(far), step)

    def both(self, k, da):
        found = self.column(k, da, 1)
        self.send_pair(k, da).wait()
        return found + self.grads[k][3][da].astype(f32)

    def far(self):
        def step(k, da):
            self.grads[k][4][da] = self.both(k, da).astype(bf16)
            self.send_far(k, da).start()

        self.loop(*self.span(True), step)

    def settle(self, outs):
        for k, out in enumerate(outs):
            out[...] = self.both(k, 0)

        def step(k, da):
            self.send_far(k, da).wait()
            outs[k][...] += self.grads[k][5][da].astype(f32)

        self.loop(*self.span(True), step)

    @staticmethod
    def scratch(arrays, parts):
        quarter = parts // 4
        slots = []
        for a in arrays:
            piece = (a.shape[0] // parts, a.shape[1])
            slots.append(pltpu.VMEM((2, quarter) + piece, bf16))
            slots += [pltpu.VMEM((quarter,) + piece, bf16)] * 4
        dma = pltpu.SemaphoreType.DMA
        count = len(arrays)
        return slots, [dma((count, 2, quarter))] * 2 + [dma((count, quarter))] * 4


def attend_back_kernel(
    gate_ref,
    sum_ref,
    cot_ref,
    gain_ref,
    middle_ref,
    weight_ref,
    q_ref,
    recalled_ref,
    local_ref,
    logs_ref,
    p_ref,
    pair_ref,
    q_all_ref,
    tok_ref,
    up_ref,
    down_ref,
    rows_hbm,
    branch_ref,
    grad_middle_ref,
    line_ref,
    d_ref,
    pos_ref,
    gate_out_ref,
    up_out_ref,
    down_out_ref,
    sum_recv,
    rows,
    g_own,
    g_all,
    st_own,
    st_all,
    dq_xs,
    dq_xr,
    dq_zs,
    dq_zr,
    pair_send,
    pair_recv,
    dq_sum,
    pair_sum,
    up_a,
    up_b,
    up_c,
    up_d,
    up_e,
    down_a,
    down_b,
    down_c,
    down_d,
    down_e,
    down_sum,
    sum_ss,
    sum_rs,
    full_ss,
    full_rs,
    rows_sem,
    g_ss,
    g_rs,
    st_ss,
    st_rs,
    dx_ss,
    dx_rs,
    dz_ss,
    dz_rs,
    pair_ss,
    pair_rs,
    sem_a,
    sem_b,
    sem_c,
    sem_d,
    sem_e,
    sem_f,
    *,
    parts,
    peers,
    scale,
):
    count, span = q_ref.shape[0], pair_ref.shape[1]
    width = q_ref.shape[1]
    hops = W // count
    per = tok_ref.shape[2]
    half = parts // 2
    me, head = lax.axis_index("seq"), lax.axis_index("head")
    x, z = lax.rem(me, 2), me // 2
    partner = me + 1 - 2 * x

    def reader(c, dz):
        at = lax.rem(z + half - dz, half)
        return 2 * at + (x if c == 0 else 1 - x)

    def fetch(c, dz):
        return pltpu.make_async_copy(
            rows_hbm.at[reader(c, dz)], rows.at[c, dz], rows_sem.at[c, dz]
        )

    def fetch_start(dz, carry):
        fetch(0, dz).start()
        fetch(1, dz).start()
        return carry

    lax.fori_loop(0, half, fetch_start, 0)
    greet(seq=parts, head=peers)

    share = count // peers

    def share_of(peer):
        return pl.ds(pl.multiple_of(peer * share, share), share)

    def send_sum(d):
        peer = lax.rem(head + d, peers)
        return send(
            sum_ref.at[share_of(peer)], sum_recv.at[d], sum_ss.at[d], sum_rs.at[d], "head", peer
        )

    mine = share_of(head)

    def send_full(d):
        peer = lax.rem(head + d, peers)
        return send(
            branch_ref.at[mine], branch_ref.at[mine], full_ss.at[d], full_rs.at[d], "head", peer
        )

    for d in range(1, peers):
        send_sum(d).start()
    scatter = ScatterSum(
        ((up_ref, up_a, up_b, up_c, up_d, up_e), (down_ref, down_a, down_b, down_c, down_d, down_e)),
        (sem_a, sem_b, sem_c, sem_d, sem_e, sem_f),
        parts,
    )
    scatter.start(True, 0)
    scatter.start(True, 1)
    middle = middle_ref[...]
    row_scale = lax.rsqrt(row_mean(middle * middle) + eps)
    hat = middle * row_scale
    grad_normed = sum_ref[mine, :].astype(f32)
    for d in range(1, peers):
        send_sum(d).wait()
        grad_normed = grad_normed + sum_recv[d].astype(f32)
    scaled = grad_normed * gain_ref[...]
    grad_middle = cot_ref[mine, :].astype(f32) + row_scale * (scaled - hat * row_mean(scaled * hat))
    branch_ref[mine, :] = grad_middle.astype(bf16)
    for d in range(1, peers):
        send_full(d).start()
    grad_middle_ref[...] = grad_middle
    line_ref[...] = col_sum(grad_normed * hat)
    scatter.pair(True)
    for d in range(1, peers):
        send_full(d).wait()
    g_own[...] = nt(branch_ref[...], weight_ref[...]).astype(bf16)

    deltas = []
    for h in range(2):
        cols = head_cols(h)
        g = g_own[:, cols].astype(f32)
        gate_out_ref[h : h + 1, :] = col_sum(g * (recalled_ref[:, cols] - local_ref[:, cols]))
        both = jnp.sum(g * recalled_ref[:, cols], axis=1, keepdims=True)
        deltas.append(both * gate_ref[h])
    turned = row_form([jnp.zeros_like(deltas[0])] * 2 + deltas, count).T[0:8]
    row = lax.broadcasted_iota(jnp.int32, (8, count), 0)
    st_own[...] = jnp.where(row < 2, logs_ref[...], turned)

    def ask_z(dz):
        peer = 2 * lax.rem(z + dz, half) + x
        return (
            send(st_own, st_all.at[0, dz], st_ss.at[0, dz], st_rs.at[0, dz], "seq", peer),
            send(g_own, g_all.at[0, dz], g_ss.at[0, dz], g_rs.at[0, dz], "seq", peer),
        )

    def ask_x(dz, own=False):
        st, g = (st_own, g_own) if own else (st_all.at[0, dz], g_all.at[0, dz])
        return (
            send(st, st_all.at[1, dz], st_ss.at[1, dz], st_rs.at[1, dz], "seq", partner),
            send(g, g_all.at[1, dz], g_ss.at[1, dz], g_rs.at[1, dz], "seq", partner),
        )

    def ask(dz, carry):
        for copy in ask_z(dz):
            copy.start()
        return carry

    for copy in ask_x(0, own=True):
        copy.start()
    lax.fori_loop(1, half, ask, 0)

    for h in range(2):
        cols = head_cols(h)
        rest = 1.0 - gate_ref[h]
        p = p_ref[h]
        e = nt(g_own[:, cols], pair_ref[1, :, cols]) * rest
        delta = jnp.sum(p * e, axis=1, keepdims=True)
        ds = (p * (e - delta)).astype(bf16)
        dq_sum[:, cols] = nn(ds, pair_ref[0, :, cols]) * scale
        dk = tn(ds, q_ref[:, cols]) * scale
        dv = tn(p.astype(bf16), g_own[:, cols]) * rest
        pair_sum[0, :, cols] = dk[W:]
        pair_sum[1, :, cols] = dv[W:]
        pair_send[0, :, cols] = dk[:W].astype(bf16)
        pair_send[1, :, cols] = dv[:W].astype(bf16)
        low = ds.astype(f32)
        acc = low[0:8]
        for a in range(1, count // 8):
            acc = acc + pltpu.roll(low[8 * a : 8 * a + 8], (span - 8 * a) % span, 1)
        line = acc[0:1]
        for b in range(1, 8):
            line = line + pltpu.roll(acc[b : b + 1], span - b, 1)
        pos_ref[h : h + 1, :] = line

    def hand_back(hop):
        return send(
            pair_send.at[:, pl.ds(W - hop * count, count)],
            pair_recv.at[hop - 1],
            pair_ss.at[hop - 1],
            pair_rs.at[hop - 1],
            "seq",
            lax.rem(me + parts - hop, parts),
        )

    for hop in range(1, hops + 1):
        hand_back(hop).start()

    ids = lax.broadcasted_iota(jnp.int32, (count, per), 0)

    def owner_part(c, dz, g_at, st_at):
        fetch(c, dz).wait()
        j = reader(c, dz)
        stats = st_at[...].T
        found = []
        for h in range(2):
            cols = head_cols(h)
            keep = tok_ref[j, h : h + 1, :] == ids
            s = nt(q_all_ref[j, :, cols], rows[c, dz, h, :, 0:128]) * scale
            p = jnp.exp(jnp.where(keep, s - stats[:, h : h + 1], NEG))
            e = nt(g_at[:, cols], rows[c, dz, h, :, 128:256]) * gate_ref[h]
            ds = (p * (e - stats[:, 2 + h : 3 + h])).astype(bf16)
            found.append(nn(ds, rows[c, dz, h, :, 0:128]) * scale)
        return found

    def give_x(dz):
        return send(dq_xs.at[dz], dq_xr.at[dz], dx_ss.at[dz], dx_rs.at[dz], "seq", partner)

    def give_z(dz):
        peer = reader(0, dz)
        return send(dq_zs.at[dz], dq_zr.at[dz], dz_ss.at[dz], dz_rs.at[dz], "seq", peer)

    own = owner_part(0, 0, g_own, st_own)
    for h in range(2):
        dq_sum[:, head_cols(h)] += own[h]

    def column(dz, carry):
        for copy in ask_z(dz):
            copy.wait()
        for copy in ask_x(dz):
            copy.start()
        found = owner_part(0, dz, g_all.at[0, dz], st_all.at[0, dz])
        for h in range(2):
            dq_zs[dz, h] = found[h].astype(bf16)
        return carry

    lax.fori_loop(1, half, column, 0)
    scatter.start(False, 0)
    scatter.far()

    def neighbour(dz, copies):
        for copy in copies:
            copy.wait()
        found = owner_part(1, dz, g_all.at[1, dz], st_all.at[1, dz])
        for h in range(2):
            dq_xs[dz, h] = found[h].astype(bf16)
        give_x(dz).start()

    def neighbour_step(dz, carry):
        neighbour(dz, ask_x(dz))
        return carry

    lax.fori_loop(1, half, neighbour_step, 0)
    neighbour(0, ask_x(0, own=True))
    scatter.start(False, 1)

    def column_back(dz, carry):
        give_x(dz).wait()
        for h in range(2):
            both = dq_zs[dz, h].astype(f32) + dq_xr[dz, h].astype(f32)
            dq_zs[dz, h] = both.astype(bf16)
        give_z(dz).start()
        return carry

    lax.fori_loop(1, half, column_back, 0)
    scatter.pair(False)
    give_x(0).wait()
    for h in range(2):
        dq_sum[:, head_cols(h)] += dq_xr[0, h].astype(f32)
    for hop in range(1, hops + 1):
        hand_back(hop).wait()
        pair_sum[...] += pair_recv[hop - 1].astype(f32)
    d_ref[:, width : 2 * width] = pair_sum[0].astype(bf16)
    d_ref[:, 2 * width :] = pair_sum[1].astype(bf16)

    def merge(dz, carry):
        give_z(dz).wait()
        for h in range(2):
            dq_sum[:, head_cols(h)] += dq_zr[dz, h].astype(f32)
        return carry

    lax.fori_loop(1, half, merge, 0)
    d_ref[:, :width] = dq_sum[...].astype(bf16)
    scatter.settle((up_out_ref, down_sum))
    down_out_ref[...] = down_sum[...].T


def attend_back(
    gate, sums, cot, gain, middle, weight, q, recalled, local, logs, p, pair, q_all, tok, up, down, rows, peers
):
    parts, count, width = q_all.shape
    span, hops, half = W + count, W // count, parts // 2
    model = sums.shape[1]
    share, own = count // peers, up.shape[0] // parts
    smem = pl.BlockSpec(memory_space=pltpu.SMEM)
    vmem = pl.BlockSpec(memory_space=pltpu.VMEM)
    dma = pltpu.SemaphoreType.DMA
    slots, sems = ScatterSum.scratch((up, down), parts)
    return pl.pallas_call(
        functools.partial(attend_back_kernel, parts=parts, peers=peers, scale=128**-0.5),
        out_shape=(
            jax.ShapeDtypeStruct((count, model), bf16),
            jax.ShapeDtypeStruct((share, model), f32),
            jax.ShapeDtypeStruct((1, model), f32),
            jax.ShapeDtypeStruct((count, 3 * width), bf16),
            jax.ShapeDtypeStruct((2, span), f32),
            jax.ShapeDtypeStruct((2, 128), f32),
            jax.ShapeDtypeStruct((own, up.shape[1]), f32),
            jax.ShapeDtypeStruct((down.shape[1], own), f32),
        ),
        in_specs=[smem] + [vmem] * 15 + [pl.BlockSpec(memory_space=pl.ANY)],
        out_specs=(vmem,) * 8,
        scratch_shapes=[
            pltpu.VMEM((peers, share, model), bf16),
            pltpu.VMEM((2, half) + rows.shape[1:], bf16),
            pltpu.VMEM((count, width), bf16),
            pltpu.VMEM((2, half, count, width), bf16),
            pltpu.VMEM((8, count), f32),
            pltpu.VMEM((2, half, 8, count), f32),
        ]
        + [pltpu.VMEM((half, 2, count, 128), bf16)] * 4
        + [
            pltpu.VMEM((2, W, width), bf16),
            pltpu.VMEM((hops, 2, count, width), bf16),
            pltpu.VMEM((count, width), f32),
            pltpu.VMEM((2, count, width), f32),
        ]
        + slots
        + [pltpu.VMEM((own, down.shape[1]), f32)]
        + [dma((peers,))] * 4
        + [dma((2, half))] * 5
        + [dma((half,))] * 4
        + [dma((hops,))] * 2
        + sems,
        compiler_params=pltpu.CompilerParams(
            vmem_limit_bytes=(44 if parts <= 8 else 62) * MIB, collective_id=2, has_side_effects=True
        ),
        cost_estimate=pl.CostEstimate(
            flops=4 * 10**9, bytes_accessed=150 * MIB, transcendentals=5 * 10**6
        ),
        name="attend_back",
    )(gate, sums, cot, gain, middle, weight, q, recalled, local, logs, p, pair, q_all, tok, up, down, rows)


def close_kernel(*refs, body, n_sum, n_aux, n_full, n_own, peers):
    sums = refs[:n_sum]
    aux = refs[n_sum : n_sum + n_aux]
    at = n_sum + n_aux
    full, own = refs[at : at + n_full], refs[at + n_full : at + n_full + n_own]
    at += n_full + n_own
    recv = refs[at : at + n_sum]
    ss, rs, full_ss, full_rs = refs[at + n_sum :]
    count = sums[0].shape[0]
    share = count // peers
    me = lax.axis_index("head")
    greet(head=peers)

    def rows_of(peer):
        return pl.ds(pl.multiple_of(peer * share, share), share)

    def send_sum(i, d):
        peer = lax.rem(me + d, peers)
        return send(
            sums[i].at[rows_of(peer)], recv[i].at[d], ss.at[i, d], rs.at[i, d], "head", peer
        )

    def send_full(i, d):
        return send(
            full[i].at[rows_of(me)],
            full[i].at[rows_of(me)],
            full_ss.at[i, d],
            full_rs.at[i, d],
            "head",
            lax.rem(me + d, peers),
        )

    for i in range(n_sum):
        for d in range(1, peers):
            send_sum(i, d).start()
    mine = rows_of(me)

    def total(i):
        found = sums[i][mine, :].astype(f32)
        for d in range(1, peers):
            send_sum(i, d).wait()
            found = found + recv[i][d].astype(f32)
        return found

    def spread(i, value):
        full[i][mine, :] = value.astype(full[i].dtype)
        for d in range(1, peers):
            send_full(i, d).start()

    body(mine, total, spread, aux, own)
    for i in range(n_full):
        for d in range(1, peers):
            send_full(i, d).wait()


def close(name, collective_id, body, sums, aux, full, own, peers):
    count, width = sums[0].shape
    vmem = pl.BlockSpec(memory_space=pltpu.VMEM)
    dma = pltpu.SemaphoreType.DMA
    return pl.pallas_call(
        functools.partial(
            close_kernel,
            body=body,
            n_sum=len(sums),
            n_aux=len(aux),
            n_full=len(full),
            n_own=len(own),
            peers=peers,
        ),
        out_shape=tuple(full) + tuple(own),
        in_specs=[vmem] * (len(sums) + len(aux)),
        out_specs=(vmem,) * (len(full) + len(own)),
        scratch_shapes=[pltpu.VMEM((peers, count // peers, width), bf16) for _ in sums]
        + [dma((len(sums), peers))] * 2
        + [dma((len(full), peers))] * 2,
        compiler_params=pltpu.CompilerParams(
            vmem_limit_bytes=40 * MIB, collective_id=collective_id, has_side_effects=True
        ),
        cost_estimate=pl.CostEstimate(flops=10**6, bytes_accessed=30 * MIB, transcendentals=0),
        name=name,
    )(*sums, *aux)


def row_mean(x):
    return jnp.mean(x, axis=1, keepdims=True)


def col_sum(x):
    return jnp.sum(x, axis=0, keepdims=True)


def close_attn(mine, total, spread, aux, own):
    inputs_ref, gain_ref = aux
    middle_ref, small_ref = own
    branch = total(0)
    middle = inputs_ref[mine, :].astype(f32) + branch
    hat = middle * lax.rsqrt(row_mean(middle * middle) + eps)
    spread(0, hat * gain_ref[...])
    middle_ref[...] = middle
    small_ref[...] = col_sum(branch * branch)


def folded(line):
    return jnp.concatenate([line[:, 128 * i : 128 * i + 128] for i in range(8)], axis=0)


def fold_sum(line):
    return col_sum(folded(line))


def finish_kernel(
    back_ref,
    feed_ref,
    in_ref,
    gain_ref,
    grad_middle_ref,
    middle_ref,
    gain_line_ref,
    attn_line_ref,
    extra_ref,
    grad_a,
    grad_b,
    input_grad_ref,
    layer_ref,
    out_a,
    out_b,
    small_ref,
    back_recv,
    feed_recv,
    in_a,
    in_b,
    in_c,
    in_d,
    in_e,
    res_a,
    res_b,
    res_c,
    res_d,
    res_e,
    small_head,
    small_seq,
    small_send,
    sum_ss,
    sum_rs,
    full_ss,
    full_rs,
    sh_ss,
    sh_rs,
    sq_ss,
    sq_rs,
    sem_a,
    sem_b,
    sem_c,
    sem_d,
    sem_e,
    sem_f,
    *,
    parts,
    peers,
):
    count = back_ref.shape[0]
    share = count // peers
    me, head = lax.axis_index("seq"), lax.axis_index("head")
    greet(seq=parts, head=peers)

    def share_of(peer):
        return pl.ds(pl.multiple_of(peer * share, share), share)

    def send_sum(i, d):
        peer = lax.rem(head + d, peers)
        src, recv = ((back_ref, back_recv), (feed_ref, feed_recv))[i]
        return send(
            src.at[share_of(peer)], recv.at[d], sum_ss.at[i, d], sum_rs.at[i, d], "head", peer
        )

    for i in range(2):
        for d in range(1, peers):
            send_sum(i, d).start()

    scatter = ScatterSum(
        ((grad_a, in_a, in_b, in_c, in_d, in_e), (grad_b, res_a, res_b, res_c, res_d, res_e)),
        (sem_a, sem_b, sem_c, sem_d, sem_e, sem_f),
        parts,
    )
    for far in (True, False):
        for side in range(2):
            scatter.start(far, side)

    mine = share_of(head)

    def total(i):
        src, recv = ((back_ref, back_recv), (feed_ref, feed_recv))[i]
        found = src[mine, :].astype(f32)
        for d in range(1, peers):
            send_sum(i, d).wait()
            found = found + recv[d].astype(f32)
        return found

    def send_full(i, d):
        full = (input_grad_ref, layer_ref)[i]
        return send(
            full.at[mine],
            full.at[mine],
            full_ss.at[i, d],
            full_rs.at[i, d],
            "head",
            lax.rem(head + d, peers),
        )

    tokens = in_ref[mine, :].astype(f32)
    scale = lax.rsqrt(row_mean(tokens * tokens) + eps)
    hat = tokens * scale
    grad_normed = total(0)
    g = grad_normed * gain_ref[...]
    back = grad_middle_ref[...] + scale * (g - hat * row_mean(g * hat))
    input_grad_ref[mine, :] = back.astype(bf16)
    for d in range(1, peers):
        send_full(0, d).start()
    scatter.pair(True)
    small_send[0:8] = folded(col_sum(grad_normed * hat))
    small_send[8:16] = folded(gain_line_ref[...])
    branch = total(1)
    layer = middle_ref[...] + branch
    layer_ref[mine, :] = layer.astype(bf16)
    for d in range(1, peers):
        send_full(1, d).start()
    small_send[16:24] = extra_ref[...]
    small_send[16:17] = fold_sum(col_sum(layer * layer))
    small_send[17:18] = fold_sum(attn_line_ref[...])
    small_send[18:19] = fold_sum(col_sum(branch * branch))

    def send_head(d):
        peer = lax.rem(head + d, peers)
        return send(small_send, small_head.at[d], sh_ss.at[d], sh_rs.at[d], "head", peer)

    for d in range(1, peers):
        send_head(d).start()

    scatter.far()

    kept = lax.broadcasted_iota(jnp.int32, (24, 128), 0) < 19
    found = small_send[...]
    for d in range(1, peers):
        send_head(d).wait()
        found = found + jnp.where(kept, small_head[d], 0.0)
    small_seq[0] = found

    def send_seq(d):
        peer = lax.rem(me + d, parts)
        return send(small_seq.at[0], small_seq.at[d], sq_ss.at[d], sq_rs.at[d], "seq", peer)

    def start_seq(d, carry):
        send_seq(d).start()
        return carry

    lax.fori_loop(1, parts, start_seq, 0)

    scatter.pair(False)
    scatter.settle((out_a, out_b))
    small_ref[...] = small_seq[0]

    def add_seq(d, carry):
        send_seq(d).wait()
        small_ref[...] += small_seq[d]
        return carry

    lax.fori_loop(1, parts, add_seq, 0)
    for i in range(2):
        for d in range(1, peers):
            send_full(i, d).wait()


def finish(back, feed, x, gain, grad_middle, middle, gain_line, attn_line, extra, grad_a, grad_b, parts, peers):
    count, width = back.shape
    share, own = count // peers, grad_a.shape[0] // parts
    slots, sems = ScatterSum.scratch((grad_a, grad_b), parts)
    wide_a, wide_b = grad_a.shape[1], grad_b.shape[1]
    vmem = pl.BlockSpec(memory_space=pltpu.VMEM)
    dma = pltpu.SemaphoreType.DMA
    return pl.pallas_call(
        functools.partial(finish_kernel, parts=parts, peers=peers),
        out_shape=(
            jax.ShapeDtypeStruct((count, width), bf16),
            jax.ShapeDtypeStruct((count, width), bf16),
            jax.ShapeDtypeStruct((own, wide_a), f32),
            jax.ShapeDtypeStruct((own, wide_b), f32),
            jax.ShapeDtypeStruct((24, 128), f32),
        ),
        in_specs=[vmem] * 11,
        out_specs=(vmem,) * 5,
        scratch_shapes=[pltpu.VMEM((peers, share, width), bf16)] * 2
        + slots
        + [
            pltpu.VMEM((peers, 24, 128), f32),
            pltpu.VMEM((parts, 24, 128), f32),
            pltpu.VMEM((24, 128), f32),
        ]
        + [dma((2, peers))] * 4
        + [dma((peers,))] * 2
        + [dma((parts,))] * 2
        + sems,
        compiler_params=pltpu.CompilerParams(
            vmem_limit_bytes=40 * MIB, collective_id=5, has_side_effects=True
        ),
        cost_estimate=pl.CostEstimate(flops=10**7, bytes_accessed=100 * MIB, transcendentals=0),
        name="finish",
    )(back, feed, x, gain, grad_middle, middle, gain_line, attn_line, extra, grad_a, grad_b)


def norm_stats(values):
    row_scale = lax.rsqrt(jnp.mean(values * values, axis=-1, keepdims=True) + eps)
    return (values * row_scale, row_scale)


def exchange(value):
    return lax.all_to_all(value, "seq", split_axis=0, concat_axis=0, tiled=True)


def per_device(
    inputs,
    cotangent,
    query_weight,
    key_weight,
    value_weight,
    output_weight,
    up_weight,
    down_weight,
    first_gain,
    second_gain,
    position_bias,
    gate_bias,
    memory_table,
    retrieved,
    lengths,
):
    _, block_len, model_width = inputs.shape
    bucket_total = position_bias.shape[1]
    seq_count = lax.axis_size("seq")
    slot_count = memory_table.shape[0]

    wanted = jnp.transpose(retrieved[0], (1, 0, 2))
    token = jnp.arange(block_len, dtype=jnp.int32)[None, :, None]
    codes = (wanted // slot_count) * (block_len * slot_count) + token * slot_count + wanted % slot_count
    codes = lax.sort(codes.reshape(2, -1), dimension=1, is_stable=False)
    codes = jnp.transpose(codes.reshape(2, seq_count, -1), (1, 0, 2))
    codes = exchange(codes)
    slots = codes % slot_count
    tok = (codes // slot_count) % block_len
    rows = gather_rows(slots, memory_table)

    hot, outside = diagonal_buckets(block_len, bucket_total)
    bias_row = jnp.dot(position_bias, hot, precision=highest) + outside[None]

    x, cot = inputs[0], cotangent[0]
    peers = lax.axis_size("head")
    gain_one, gain_two = first_gain[None], second_gain[None]
    gate_flat = jax.nn.sigmoid(gate_bias)
    hat_one, _ = norm_stats(x.astype(f32))
    normed_one = (hat_one * first_gain).astype(bf16)
    queries = nn(normed_one, query_weight).astype(bf16)
    keys = nn(normed_one, key_weight).astype(bf16)
    values = nn(normed_one, value_weight).astype(bf16)
    q_all = lax.all_gather(queries, "seq", axis=0)

    mixed, recalled, local_out, logs, window_weights, pair = attend(
        lengths[0], gate_flat, queries, keys, values, bias_row, q_all, tok, rows
    )

    def whole(dtype):
        return jax.ShapeDtypeStruct((block_len, model_width), dtype)

    def lines(count):
        return jax.ShapeDtypeStruct((count, model_width), f32)

    chunk = lines(block_len // peers)
    normed_two, middle, attn_line = close(
        "close_attn",
        3,
        close_attn,
        [nn(mixed, output_weight).astype(bf16)],
        [x, gain_two],
        [whole(bf16)],
        [chunk, lines(1)],
        peers,
    )
    upward = nn(normed_two, up_weight)
    gelu_value, gelu_back = jax.vjp(jax.nn.gelu, upward)
    hidden = gelu_value.astype(bf16)
    grad_upward = gelu_back(nt(cot, down_weight))[0].astype(bf16)
    grad_branch, grad_middle, gain_line, grad_heads, pos_rows, gate_rows, up_grad, down_grad = attend_back(
        gate_flat,
        nt(grad_upward, up_weight).astype(bf16),
        cot,
        gain_two,
        middle,
        output_weight,
        queries,
        recalled,
        local_out,
        logs,
        window_weights,
        pair,
        q_all,
        tok,
        tn(normed_two, grad_upward).astype(bf16),
        tn(cot, hidden).astype(bf16),
        rows,
        peers,
    )
    feed = nn(hidden, down_weight).astype(bf16)
    gate_part = jnp.sum(gate_rows, axis=1) * gate_flat * (1.0 - gate_flat)
    position_part = jnp.dot(pos_rows, hot.T, precision=highest)
    extra = jnp.zeros((8, 128), f32)
    extra = extra.at[3:5, :bucket_total].set(position_part).at[5, :2].set(gate_part)
    back = (
        nt(grad_heads[:, :256], query_weight)
        + nt(grad_heads[:, 256:512], key_weight)
        + nt(grad_heads[:, 512:], value_weight)
    )
    input_grad, layer_out, grads_in, grads_out, small = finish(
        back.astype(bf16),
        feed,
        x,
        gain_one,
        grad_middle,
        middle,
        gain_line,
        attn_line,
        extra,
        tn(normed_one, grad_heads).astype(bf16),
        tn(grad_branch, mixed).astype(bf16),
        seq_count,
        peers,
    )
    entry_count = float(block_len * model_width * seq_count)
    share = model_width // seq_count
    gains = small[:16].reshape(2, model_width)
    own_gains = lax.dynamic_slice_in_dim(gains, lax.axis_index("seq") * share, share, 1)
    return (
        layer_out[None],
        input_grad.astype(f32)[None],
        grads_in[:, 0:256],
        grads_in[:, 256:512],
        grads_in[:, 512:768],
        grads_out.T,
        up_grad,
        down_grad,
        own_gains[0],
        own_gains[1],
        small[19:21, :bucket_total],
        small[21, :2],
        jnp.sqrt(jnp.sum(small[16:19], axis=1) / entry_count),
    )


def solution(mesh):
    in_specs = (
        P(None, "seq", None),
        P(None, "seq", None),
        P(None, "head"),
        P(None, "head"),
        P(None, "head"),
        P("head", None),
        P(None, "head"),
        P("head", None),
        P(),
        P(),
        P("head", None),
        P("head"),
        P("seq", "head", None),
        P(None, "seq", "head", None),
        P(),
    )
    out_specs = (
        P(None, "seq", None),
        P(None, "seq", None),
        P("seq", "head"),
        P("seq", "head"),
        P("seq", "head"),
        P("head", "seq"),
        P("seq", "head"),
        P("head", "seq"),
        P("seq"),
        P("seq"),
        P("head", None),
        P("head"),
        P(),
    )
    return jax.shard_map(
        per_device, mesh=mesh, in_specs=in_specs, out_specs=out_specs, check_vma=False
    )
```

```python
import functools
import math

import jax
import jax.numpy as jnp
import numpy as np
from jax import lax
from jax.experimental import pallas as pl
from jax.experimental.pallas import tpu as pltpu
from jax.sharding import PartitionSpec as P

W = 512
eps = 1e-06
exact_span = 16
far_distance = 128
highest = lax.Precision.HIGHEST
f32 = jnp.float32
bf16 = jnp.bfloat16
NEG = -1e30
MIB = 2**20


def bucket_table(key_span, bucket_total):
    found = []
    for distance in range(key_span):
        if distance < exact_span:
            found.append(distance)
        else:
            scaled = math.log(distance / exact_span) / math.log(far_distance / exact_span)
            found.append(
                min(bucket_total - 1, exact_span + math.floor(scaled * (bucket_total - exact_span)))
            )
    return np.asarray(found)


def diagonal_buckets(block_len, bucket_total):
    span = W + block_len
    table = bucket_table(W, bucket_total)
    hot = np.zeros((bucket_total, span), np.float32)
    for u in range(1, W + 1):
        hot[table[W - u], u] = 1.0
    outside = np.where(hot.sum(0) > 0, 0.0, NEG).astype(np.float32)
    return hot, outside


def nt(a, b):
    return lax.dot_general(a, b, (((1,), (1,)), ((), ())), preferred_element_type=f32)


def nn(a, b):
    return lax.dot_general(a, b, (((1,), (0,)), ((), ())), preferred_element_type=f32)


def tn(a, b):
    return lax.dot_general(a, b, (((0,), (0,)), ((), ())), preferred_element_type=f32)


def widen_kernel(table_hbm, wide_ref, buf, sem, *, chunk, part):
    chunks = table_hbm.shape[0] // chunk

    def fetch(i):
        return pltpu.make_async_copy(
            table_hbm.at[pl.ds(i * chunk, chunk)], buf.at[i % 2], sem.at[i % 2]
        )

    fetch(0).start()
    for i in range(chunks):
        fetch(i).wait()
        if i + 1 < chunks:
            fetch(i + 1).start()

        def widen(q, carry, i=i):
            x = buf[i % 2, pl.ds(q * part, part)].astype(f32)
            base = i * chunk + q * part
            for r in range(part):
                wide_ref[pl.ds(4 * (base + r), 2), :] = x[r, :, 0:128]
                wide_ref[pl.ds(4 * (base + r) + 2, 2), :] = x[r, :, 128:256]
            return carry

        lax.fori_loop(0, chunk // part, widen, 0)


def widen(table):
    total = table.shape[0]
    chunk = min(1024, total)
    return pl.pallas_call(
        functools.partial(widen_kernel, chunk=chunk, part=32),
        out_shape=jax.ShapeDtypeStruct((4 * total, 128), f32),
        in_specs=[pl.BlockSpec(memory_space=pl.ANY)],
        out_specs=pl.BlockSpec(memory_space=pltpu.VMEM),
        scratch_shapes=[pltpu.VMEM((2, chunk, 2, 256), bf16), pltpu.SemaphoreType.DMA((2,))],
        compiler_params=pltpu.CompilerParams(vmem_limit_bytes=24 * MIB),
        cost_estimate=pl.CostEstimate(flops=0, bytes_accessed=40 * MIB, transcendentals=0),
        name="widen",
    )(table)


def gather_kernel(at_ref, wide_ref, out_ref, buf, *, unroll, group):
    groups, rows = out_ref.shape[0], out_ref.shape[1]

    def one(i, carry):
        def copy_rows(q, carry):
            base = q * unroll
            for g in range(0, unroll, group):
                found = [
                    wide_ref[pl.ds(at_ref[i * rows + base + g + u], 2, 2), :] for u in range(group)
                ]
                for u in range(group):
                    buf[pl.ds(2 * (base + g + u), 2), :] = found[u]
            return carry

        lax.fori_loop(0, rows // unroll, copy_rows, 0)
        out_ref[i, :, 0:128] = buf[pl.ds(0, rows, 2), :].astype(bf16)
        out_ref[i, :, 128:256] = buf[pl.ds(1, rows, 2), :].astype(bf16)
        return carry

    lax.fori_loop(0, groups, one, 0)


def gather_rows(places, wide):
    parts, heads, rows = places.shape
    unroll = min(64, rows)
    vmem = pl.BlockSpec(memory_space=pltpu.VMEM)
    found = pl.pallas_call(
        functools.partial(gather_kernel, unroll=unroll, group=unroll // 2),
        out_shape=jax.ShapeDtypeStruct((parts * heads, rows, 256), bf16),
        in_specs=[pl.BlockSpec(memory_space=pltpu.SMEM), vmem],
        out_specs=vmem,
        scratch_shapes=[pltpu.VMEM((2 * rows, 128), f32)],
        compiler_params=pltpu.CompilerParams(vmem_limit_bytes=32 * MIB),
        cost_estimate=pl.CostEstimate(flops=0, bytes_accessed=100 * MIB, transcendentals=0),
        name="gather_rows",
    )(places.reshape(-1), wide)
    return found.reshape(parts, heads, rows, 256)


MESH = pl.DeviceIdType.MESH


def greet(**counts):
    barrier = pltpu.get_barrier_semaphore()
    for axis, count in counts.items():
        me = lax.axis_index(axis)

        def call(d, carry, axis=axis, count=count, me=me):
            peer = lax.rem(me + d, count)
            pl.semaphore_signal(barrier, inc=1, device_id={axis: peer}, device_id_type=MESH)
            return carry

        lax.fori_loop(1, count, call, 0)
    pl.semaphore_wait(barrier, sum(counts.values()) - len(counts))


def send(src, dst, send_sem, recv_sem, axis, peer):
    return pltpu.make_async_remote_copy(
        src_ref=src,
        dst_ref=dst,
        send_sem=send_sem,
        recv_sem=recv_sem,
        device_id={axis: peer},
        device_id_type=MESH,
    )


def doc_starts(lengths_ref, first, count):
    place = first + lax.broadcasted_iota(jnp.int32, (count, 1), 0)
    start = jnp.zeros((count, 1), jnp.int32)
    end = jnp.int32(0)
    for c in range(lengths_ref.shape[0]):
        end = end + lengths_ref[c]
        start = jnp.where(end <= place, end, start)
    return start


def head_cols(h):
    return slice(h * 128, h * 128 + 128)


def row_form(columns, count):
    lane = lax.broadcasted_iota(jnp.int32, (count, 128), 1)
    wide = jnp.zeros((count, 128), f32)
    for i, column in enumerate(columns):
        wide = jnp.where(lane == i, column, wide)
    return wide


def request_kernel(codes_ref, place_ref, tok_ref, got, own_sem, ss, rs, *, parts, slots, tokens):
    rows = codes_ref.shape[1] // parts
    me = lax.axis_index("seq")

    def part(owner):
        return codes_ref.at[:, pl.ds(pl.multiple_of(owner * rows, 128), rows)]

    keep = pltpu.make_async_copy(part(me), got.at[0], own_sem)
    keep.start()
    greet(seq=parts)

    def ask(d):
        peer = lax.rem(me + d, parts)
        return send(part(peer), got.at[d], ss.at[d], rs.at[d], "seq", peer)

    def start(d, carry):
        ask(d).start()
        return carry

    lax.fori_loop(1, parts, start, 0)
    shift = slots.bit_length() - 1
    head = lax.broadcasted_iota(jnp.int32, (2, rows), 0)

    def read(d, j):
        code = got[d]
        place_ref[j] = (code & (slots - 1)) * 4 + head
        tok_ref[j] = (code >> shift) & (tokens - 1)

    keep.wait()
    read(0, me)

    def arrive(d, carry):
        ask(d).wait()
        read(d, lax.rem(me + parts - d, parts))
        return carry

    lax.fori_loop(1, parts, arrive, 0)


def request(codes, parts, slots, tokens):
    rows = codes.shape[1] // parts
    vmem = pl.BlockSpec(memory_space=pltpu.VMEM)
    dma = pltpu.SemaphoreType.DMA
    shape = (parts, 2, rows)
    return pl.pallas_call(
        functools.partial(request_kernel, parts=parts, slots=slots, tokens=tokens),
        out_shape=(jax.ShapeDtypeStruct(shape, jnp.int32),) * 2,
        in_specs=[vmem],
        out_specs=(vmem,) * 2,
        scratch_shapes=[pltpu.VMEM(shape, jnp.int32), dma, dma((parts,)), dma((parts,))],
        compiler_params=pltpu.CompilerParams(
            vmem_limit_bytes=8 * MIB, collective_id=6, has_side_effects=True
        ),
        name="request",
    )(codes)


class HeadSum:
    def __init__(self, src, scratch, sems, full=None, full_sems=None):
        self.src, self.full = src, full
        self.core_recv, self.side_send, self.side_recv = scratch
        self.core_ss, self.core_rs, self.side_ss, self.side_rs = sems
        self.full_sems = full_sems
        head = lax.axis_index("head")
        self.y, self.c = head // 2, lax.rem(head, 2)
        self.share = src.shape[0] // 4
        self.core = 2 * self.y + 1 - self.c
        self.side = 2 * (1 - self.y) + self.c
        self.mine = self.rows_of(head)

    def rows_of(self, place):
        return pl.ds(pl.multiple_of(place * self.share, self.share), self.share)

    def to_core(self, i):
        y = self.y if i == 0 else 1 - self.y
        src = self.src.at[self.rows_of(2 * y + 1 - self.c)]
        return send(src, self.core_recv.at[i], self.core_ss.at[i], self.core_rs.at[i], "head", self.core)

    def to_side(self):
        return send(self.side_send, self.side_recv, self.side_ss, self.side_rs, "head", self.side)

    def start(self):
        self.to_core(1).start()
        self.to_core(0).start()

    def relay(self):
        self.to_core(1).wait()
        other = self.src[self.rows_of(self.side), :].astype(f32)
        self.side_send[...] = (other + self.core_recv[1].astype(f32)).astype(bf16)
        self.to_side().start()

    def total(self):
        self.to_core(0).wait()
        found = self.src[self.mine, :].astype(f32) + self.core_recv[0].astype(f32)
        self.to_side().wait()
        return found + self.side_recv[...].astype(f32)

    def back(self, i):
        rows = self.rows_of(self.side) if i == 2 else self.mine
        peer = self.side if i == 1 else self.core
        ss, rs = self.full_sems
        return send(self.full.at[rows], self.full.at[rows], ss.at[i], rs.at[i], "head", peer)

    def spread(self, value):
        self.full[self.mine, :] = value.astype(self.full.dtype)
        self.back(1).start()
        self.back(0).start()

    def forward(self):
        self.back(1).wait()
        self.back(2).start()

    def settle(self):
        self.back(0).wait()
        self.back(2).wait()

    @staticmethod
    def scratch(count, width):
        piece = (count // 4, width)
        return [pltpu.VMEM((2,) + piece, bf16), pltpu.VMEM(piece, bf16), pltpu.VMEM(piece, bf16)]

    @staticmethod
    def sems():
        dma = pltpu.SemaphoreType.DMA
        return [dma((2,)), dma((2,)), dma, dma]

    @staticmethod
    def full_scratch():
        return [pltpu.SemaphoreType.DMA((3,))] * 2


def attend_kernel(
    lengths_ref,
    gate_ref,
    q_ref,
    k_ref,
    v_ref,
    bias_ref,
    q_all_ref,
    tok_ref,
    rows_ref,
    mixed_ref,
    recalled_ref,
    local_ref,
    logs_ref,
    p_ref,
    pair_ref,
    out_xs,
    out_xr,
    out_zs,
    out_zr,
    log_xs,
    log_xr,
    log_zs,
    log_zr,
    ox_ss,
    ox_rs,
    oz_ss,
    oz_rs,
    lx_ss,
    lx_rs,
    lz_ss,
    lz_rs,
    pair_ss,
    pair_rs,
    *,
    parts,
    scale,
):
    count, span = q_ref.shape[0], pair_ref.shape[1]
    hops = W // count
    per = tok_ref.shape[2]
    half = parts // 2
    me = lax.axis_index("seq")
    x, z = lax.rem(me, 2), me // 2
    partner = me + 1 - 2 * x

    def reader(c, dz):
        at = lax.rem(z + half - dz, half)
        return 2 * at + (x if c == 0 else 1 - x)

    pair_ref[0, W:, :] = k_ref[...]
    pair_ref[1, W:, :] = v_ref[...]
    greet(seq=parts)

    def hand_on(hop):
        return send(
            pair_ref.at[:, pl.ds(W, count)],
            pair_ref.at[:, pl.ds(W - hop * count, count)],
            pair_ss.at[hop - 1],
            pair_rs.at[hop - 1],
            "seq",
            lax.rem(me + hop, parts),
        )

    for hop in range(1, hops + 1):
        hand_on(hop).start()

    ids = lax.broadcasted_iota(jnp.int32, (count, per), 0)

    def owner_part(j):
        outs, logs = [], []
        for h in range(2):
            cols = head_cols(h)
            keep = tok_ref[j, h : h + 1, :] == ids
            s = jnp.where(keep, nt(q_all_ref[j, :, cols], rows_ref[j, h, :, 0:128]), NEG)
            top = jnp.max(s, axis=1, keepdims=True)
            p = jnp.where(keep, jnp.exp((s - top) * scale), 0.0)
            total = jnp.sum(p, axis=1, keepdims=True)
            some = total > 0.0
            safe = jnp.where(some, total, 1.0)
            outs.append(nn(p.astype(bf16), rows_ref[j, h, :, 128:256]) / safe)
            logs.append(jnp.where(some, top * scale + jnp.log(safe), NEG))
        return outs, logs

    def give_x(dz):
        return (
            send(log_xs.at[dz], log_xr.at[dz], lx_ss.at[dz], lx_rs.at[dz], "seq", partner),
            send(out_xs.at[dz], out_xr.at[dz], ox_ss.at[dz], ox_rs.at[dz], "seq", partner),
        )

    def log_z(dz):
        return send(
            log_zs.at[dz], log_zr.at[dz], lz_ss.at[dz], lz_rs.at[dz], "seq", reader(0, dz)
        )

    def out_z(dz):
        return send(
            out_zs.at[dz], out_zr.at[dz], oz_ss.at[dz], oz_rs.at[dz], "seq", reader(0, dz)
        )

    def neighbour(dz):
        outs, logs = owner_part(reader(1, dz))
        for h in range(2):
            out_xs[dz, h] = outs[h].astype(bf16)
        log_xs[dz] = row_form(logs, count).T[0:8]
        for copy in give_x(dz):
            copy.start()

    def join(outs, logs, dz):
        for copy in give_x(dz):
            copy.wait()
        other = log_xr[dz].T
        joined = []
        for h in range(2):
            theirs = other[:, h : h + 1]
            top = jnp.maximum(logs[h], theirs)
            a, b = jnp.exp(logs[h] - top), jnp.exp(theirs - top)
            total = a + b
            outs[h] = outs[h] * (a / total) + out_xr[dz, h].astype(f32) * (b / total)
            joined.append(top + jnp.log(total))
        return outs, joined

    def neighbour_step(dz, carry):
        neighbour(dz)
        return carry

    lax.fori_loop(1, half, neighbour_step, 0)
    neighbour(0)

    def column_step(dz, carry):
        outs, logs = owner_part(reader(0, dz))
        outs, logs = join(outs, logs, dz)
        for h in range(2):
            out_zs[dz, h] = outs[h].astype(bf16)
        log_zs[dz] = row_form(logs, count).T[0:8]
        log_z(dz).start()
        out_z(dz).start()
        return carry

    lax.fori_loop(1, half, column_step, 0)
    outs, logs = owner_part(me)
    outs, logs = join(outs, logs, 0)
    log_zr[0] = row_form(logs, count).T[0:8]
    for h in range(2):
        recalled_ref[:, head_cols(h)] = outs[h]

    for hop in range(1, hops + 1):
        hand_on(hop).wait()
    first = me * count
    start = doc_starts(lengths_ref, first, count)
    key_place = first - W + lax.broadcasted_iota(jnp.int32, (count, span), 1)
    seen = key_place >= start
    for h in range(2):
        cols = head_cols(h)
        bias = pltpu.roll(
            jnp.broadcast_to(bias_ref[h : h + 1, :], (count, span)), 0, 1, stride=1, stride_axis=0
        )
        s = nt(q_ref[:, cols], pair_ref[0, :, cols]) * scale + bias
        s = jnp.where(seen, s, NEG)
        raised = jnp.exp(s - jnp.max(s, axis=1, keepdims=True))
        p = raised / jnp.sum(raised, axis=1, keepdims=True)
        p_ref[h] = p
        local_ref[:, cols] = nn(p.astype(bf16), pair_ref[1, :, cols])

    def wait_log(dz, top):
        log_z(dz).wait()
        return jnp.maximum(top, log_zr[dz])

    top = lax.fori_loop(1, half, wait_log, log_zr[0])

    def add_to(dz, total):
        return total + jnp.exp(log_zr[dz] - top)

    logs = top + jnp.log(lax.fori_loop(0, half, add_to, jnp.zeros_like(top)))
    logs_ref[...] = logs
    share = jnp.exp(log_zr[0] - logs).T
    for h in range(2):
        recalled_ref[:, head_cols(h)] *= share[:, h : h + 1]

    def merge(dz, carry):
        share = jnp.exp(log_zr[dz] - logs).T
        out_z(dz).wait()
        for h in range(2):
            recalled_ref[:, head_cols(h)] += share[:, h : h + 1] * out_zr[dz, h].astype(f32)
        return carry

    lax.fori_loop(1, half, merge, 0)
    for h in range(2):
        cols = head_cols(h)
        gate = gate_ref[h]
        mixed = gate * recalled_ref[:, cols] + (1.0 - gate) * local_ref[:, cols]
        mixed_ref[:, cols] = mixed.astype(bf16)


def attend(lengths, gate, q, k, v, bias, q_all, tok, rows):
    parts, count, width = q_all.shape
    span, hops, half = W + count, W // count, parts // 2
    smem = pl.BlockSpec(memory_space=pltpu.SMEM)
    vmem = pl.BlockSpec(memory_space=pltpu.VMEM)
    dma = pltpu.SemaphoreType.DMA
    return pl.pallas_call(
        functools.partial(attend_kernel, parts=parts, scale=128**-0.5),
        out_shape=(
            jax.ShapeDtypeStruct((count, width), bf16),
            jax.ShapeDtypeStruct((count, width), f32),
            jax.ShapeDtypeStruct((count, width), f32),
            jax.ShapeDtypeStruct((8, count), f32),
            jax.ShapeDtypeStruct((2, count, span), f32),
            jax.ShapeDtypeStruct((2, span, width), bf16),
        ),
        in_specs=[smem, smem] + [vmem] * 7,
        out_specs=(vmem,) * 6,
        scratch_shapes=[pltpu.VMEM((half, 2, count, 128), bf16)] * 4
        + [pltpu.VMEM((half, 8, count), f32)] * 4
        + [dma((half,))] * 8
        + [dma((hops,))] * 2,
        compiler_params=pltpu.CompilerParams(
            vmem_limit_bytes=(28 if parts <= 8 else 56) * MIB, collective_id=1, has_side_effects=True
        ),
        cost_estimate=pl.CostEstimate(
            flops=3 * 10**9, bytes_accessed=100 * MIB, transcendentals=5 * 10**6
        ),
        name="attend",
    )(lengths, gate, q, k, v, bias, q_all, tok, rows)


class ScatterSum:
    def __init__(self, grads, sems, parts):
        self.grads, self.sems = grads, sems
        self.quarter = parts // 4
        self.own = grads[0][0].shape[0] // parts
        me = lax.axis_index("seq")
        self.x, self.b, self.a = lax.rem(me, 2), lax.rem(me // 2, 2), me // 4

    def place(self, da, side, x):
        b = self.b if side == 1 else 1 - self.b
        return 4 * lax.rem(self.a + da, self.quarter) + 2 * b + x

    def rows_of(self, place):
        return pl.ds(pl.multiple_of(place * self.own, self.own), self.own)

    def send_x(self, k, da, side):
        ss, rs = self.sems[0:2]
        return send(
            self.grads[k][0].at[self.rows_of(self.place(da, side, 1 - self.x))],
            self.grads[k][1].at[side, da],
            ss.at[k, side, da],
            rs.at[k, side, da],
            "seq",
            self.place(0, 1, 1 - self.x),
        )

    def send_pair(self, k, da):
        ss, rs = self.sems[2:4]
        grads, peer = self.grads[k], self.place(0, 0, self.x)
        return send(grads[2].at[da], grads[3].at[da], ss.at[k, da], rs.at[k, da], "seq", peer)

    def send_far(self, k, da):
        ss, rs = self.sems[4:6]
        grads, peer = self.grads[k], self.place(da, 1, self.x)
        return send(grads[4].at[da], grads[5].at[da], ss.at[k, da], rs.at[k, da], "seq", peer)

    def loop(self, first, last, step):
        def body(da, carry):
            for k in range(len(self.grads)):
                step(k, da)
            return carry

        lax.fori_loop(first, last, body, 0)

    def span(self, far):
        return (1, self.quarter) if far else (0, 1)

    def start(self, far, side):
        self.loop(*self.span(far), lambda k, da: self.send_x(k, da, side).start())

    def column(self, k, da, side):
        self.send_x(k, da, side).wait()
        mine = self.grads[k][0][self.rows_of(self.place(da, side, self.x)), :]
        return mine.astype(f32) + self.grads[k][1][side, da].astype(f32)

    def pair(self, far):
        def step(k, da):
            self.grads[k][2][da] = self.column(k, da, 0).astype(bf16)
            self.send_pair(k, da).start()

        self.loop(*self.span(far), step)

    def both(self, k, da):
        found = self.column(k, da, 1)
        self.send_pair(k, da).wait()
        return found + self.grads[k][3][da].astype(f32)

    def far(self):
        def step(k, da):
            self.grads[k][4][da] = self.both(k, da).astype(bf16)
            self.send_far(k, da).start()

        self.loop(*self.span(True), step)

    def settle(self, outs):
        for k, out in enumerate(outs):
            out[...] = self.both(k, 0)

        def step(k, da):
            self.send_far(k, da).wait()
            outs[k][...] += self.grads[k][5][da].astype(f32)

        self.loop(*self.span(True), step)

    @staticmethod
    def scratch(arrays, parts):
        quarter = parts // 4
        slots = []
        for a in arrays:
            piece = (a.shape[0] // parts, a.shape[1])
            slots.append(pltpu.VMEM((2, quarter) + piece, bf16))
            slots += [pltpu.VMEM((quarter,) + piece, bf16)] * 4
        dma = pltpu.SemaphoreType.DMA
        count = len(arrays)
        return slots, [dma((count, 2, quarter))] * 2 + [dma((count, quarter))] * 4


def attend_back_kernel(
    gate_ref,
    sum_ref,
    cot_ref,
    gain_ref,
    middle_ref,
    weight_ref,
    q_ref,
    recalled_ref,
    local_ref,
    logs_ref,
    p_ref,
    pair_ref,
    q_all_ref,
    tok_ref,
    up_ref,
    down_ref,
    rows_ref,
    branch_ref,
    grad_middle_ref,
    line_ref,
    d_ref,
    pos_ref,
    gate_out_ref,
    up_out_ref,
    down_out_ref,
    core_recv,
    side_send,
    side_recv,
    g_own,
    g_all,
    st_own,
    st_all,
    dq_xs,
    dq_xr,
    dq_zs,
    dq_zr,
    pair_send,
    pair_recv,
    dq_sum,
    pair_sum,
    up_a,
    up_b,
    up_c,
    up_d,
    up_e,
    down_a,
    down_b,
    down_c,
    down_d,
    down_e,
    down_sum,
    core_ss,
    core_rs,
    side_ss,
    side_rs,
    full_ss,
    full_rs,
    g_ss,
    g_rs,
    st_ss,
    st_rs,
    dx_ss,
    dx_rs,
    dz_ss,
    dz_rs,
    pair_ss,
    pair_rs,
    sem_a,
    sem_b,
    sem_c,
    sem_d,
    sem_e,
    sem_f,
    *,
    parts,
    peers,
    scale,
):
    count, span = q_ref.shape[0], pair_ref.shape[1]
    width = q_ref.shape[1]
    hops = W // count
    per = tok_ref.shape[2]
    half = parts // 2
    me = lax.axis_index("seq")
    x, z = lax.rem(me, 2), me // 2
    partner = me + 1 - 2 * x

    def reader(c, dz):
        at = lax.rem(z + half - dz, half)
        return 2 * at + (x if c == 0 else 1 - x)

    greet(seq=parts, head=peers)

    sums = HeadSum(
        sum_ref,
        (core_recv, side_send, side_recv),
        (core_ss, core_rs, side_ss, side_rs),
        branch_ref,
        (full_ss, full_rs),
    )
    sums.start()
    scatter = ScatterSum(
        ((up_ref, up_a, up_b, up_c, up_d, up_e), (down_ref, down_a, down_b, down_c, down_d, down_e)),
        (sem_a, sem_b, sem_c, sem_d, sem_e, sem_f),
        parts,
    )
    scatter.start(True, 0)
    scatter.start(True, 1)
    middle = middle_ref[...]
    row_scale = lax.rsqrt(row_mean(middle * middle) + eps)
    hat = middle * row_scale
    sums.relay()
    grad_normed = sums.total()
    scaled = grad_normed * gain_ref[...]
    grad_middle = cot_ref[sums.mine, :].astype(f32) + row_scale * (
        scaled - hat * row_mean(scaled * hat)
    )
    sums.spread(grad_middle)
    grad_middle_ref[...] = grad_middle
    line_ref[...] = col_sum(grad_normed * hat)
    scatter.pair(True)
    sums.forward()
    sums.settle()
    g_own[...] = nt(branch_ref[...], weight_ref[...]).astype(bf16)

    deltas = []
    for h in range(2):
        cols = head_cols(h)
        g = g_own[:, cols].astype(f32)
        gate_out_ref[h : h + 1, :] = col_sum(g * (recalled_ref[:, cols] - local_ref[:, cols]))
        both = jnp.sum(g * recalled_ref[:, cols], axis=1, keepdims=True)
        deltas.append(both * gate_ref[h])
    turned = row_form([jnp.zeros_like(deltas[0])] * 2 + deltas, count).T[0:8]
    row = lax.broadcasted_iota(jnp.int32, (8, count), 0)
    st_own[...] = jnp.where(row < 2, logs_ref[...], turned)

    def ask_z(dz):
        peer = 2 * lax.rem(z + dz, half) + x
        return (
            send(st_own, st_all.at[0, dz], st_ss.at[0, dz], st_rs.at[0, dz], "seq", peer),
            send(g_own, g_all.at[0, dz], g_ss.at[0, dz], g_rs.at[0, dz], "seq", peer),
        )

    def ask_x(dz, own=False):
        st, g = (st_own, g_own) if own else (st_all.at[0, dz], g_all.at[0, dz])
        return (
            send(st, st_all.at[1, dz], st_ss.at[1, dz], st_rs.at[1, dz], "seq", partner),
            send(g, g_all.at[1, dz], g_ss.at[1, dz], g_rs.at[1, dz], "seq", partner),
        )

    def ask(dz, carry):
        for copy in ask_z(dz):
            copy.start()
        return carry

    for copy in ask_x(0, own=True):
        copy.start()
    lax.fori_loop(1, half, ask, 0)

    for h in range(2):
        cols = head_cols(h)
        rest = 1.0 - gate_ref[h]
        p = p_ref[h]
        e = nt(g_own[:, cols], pair_ref[1, :, cols]) * rest
        delta = jnp.sum(p * e, axis=1, keepdims=True)
        ds = (p * (e - delta)).astype(bf16)
        dq_sum[:, cols] = nn(ds, pair_ref[0, :, cols]) * scale
        dk = tn(ds, q_ref[:, cols]) * scale
        dv = tn(p.astype(bf16), g_own[:, cols]) * rest
        pair_sum[0, :, cols] = dk[W:]
        pair_sum[1, :, cols] = dv[W:]
        pair_send[0, :, cols] = dk[:W].astype(bf16)
        pair_send[1, :, cols] = dv[:W].astype(bf16)
        low = ds.astype(f32)
        acc = low[0:8]
        for a in range(1, count // 8):
            acc = acc + pltpu.roll(low[8 * a : 8 * a + 8], (span - 8 * a) % span, 1)
        line = acc[0:1]
        for b in range(1, 8):
            line = line + pltpu.roll(acc[b : b + 1], span - b, 1)
        pos_ref[h : h + 1, :] = line

    def hand_back(hop):
        return send(
            pair_send.at[:, pl.ds(W - hop * count, count)],
            pair_recv.at[hop - 1],
            pair_ss.at[hop - 1],
            pair_rs.at[hop - 1],
            "seq",
            lax.rem(me + parts - hop, parts),
        )

    for hop in range(1, hops + 1):
        hand_back(hop).start()

    ids = lax.broadcasted_iota(jnp.int32, (count, per), 0)

    def owner_part(c, dz, g_at, st_at):
        j = reader(c, dz)
        stats = st_at[...].T
        found = []
        for h in range(2):
            cols = head_cols(h)
            keep = tok_ref[j, h : h + 1, :] == ids
            s = nt(q_all_ref[j, :, cols], rows_ref[j, h, :, 0:128]) * scale
            p = jnp.exp(jnp.where(keep, s - stats[:, h : h + 1], NEG))
            e = nt(g_at[:, cols], rows_ref[j, h, :, 128:256]) * gate_ref[h]
            ds = (p * (e - stats[:, 2 + h : 3 + h])).astype(bf16)
            found.append(nn(ds, rows_ref[j, h, :, 0:128]) * scale)
        return found

    def give_x(dz):
        return send(dq_xs.at[dz], dq_xr.at[dz], dx_ss.at[dz], dx_rs.at[dz], "seq", partner)

    def give_z(dz):
        peer = reader(0, dz)
        return send(dq_zs.at[dz], dq_zr.at[dz], dz_ss.at[dz], dz_rs.at[dz], "seq", peer)

    own = owner_part(0, 0, g_own, st_own)
    for h in range(2):
        dq_sum[:, head_cols(h)] += own[h]

    def column(dz, carry):
        for copy in ask_z(dz):
            copy.wait()
        for copy in ask_x(dz):
            copy.start()
        found = owner_part(0, dz, g_all.at[0, dz], st_all.at[0, dz])
        for h in range(2):
            dq_zs[dz, h] = found[h].astype(bf16)
        return carry

    lax.fori_loop(1, half, column, 0)
    scatter.start(False, 0)
    scatter.far()

    def neighbour(dz, copies):
        for copy in copies:
            copy.wait()
        found = owner_part(1, dz, g_all.at[1, dz], st_all.at[1, dz])
        for h in range(2):
            dq_xs[dz, h] = found[h].astype(bf16)
        give_x(dz).start()

    def neighbour_step(dz, carry):
        neighbour(dz, ask_x(dz))
        return carry

    lax.fori_loop(1, half, neighbour_step, 0)
    neighbour(0, ask_x(0, own=True))
    scatter.start(False, 1)

    def column_back(dz, carry):
        give_x(dz).wait()
        for h in range(2):
            both = dq_zs[dz, h].astype(f32) + dq_xr[dz, h].astype(f32)
            dq_zs[dz, h] = both.astype(bf16)
        give_z(dz).start()
        return carry

    lax.fori_loop(1, half, column_back, 0)
    scatter.pair(False)
    give_x(0).wait()
    for h in range(2):
        dq_sum[:, head_cols(h)] += dq_xr[0, h].astype(f32)
    for hop in range(1, hops + 1):
        hand_back(hop).wait()
        pair_sum[...] += pair_recv[hop - 1].astype(f32)
    d_ref[:, width : 2 * width] = pair_sum[0].astype(bf16)
    d_ref[:, 2 * width :] = pair_sum[1].astype(bf16)

    def merge(dz, carry):
        give_z(dz).wait()
        for h in range(2):
            dq_sum[:, head_cols(h)] += dq_zr[dz, h].astype(f32)
        return carry

    lax.fori_loop(1, half, merge, 0)
    d_ref[:, :width] = dq_sum[...].astype(bf16)
    scatter.settle((up_out_ref, down_sum))
    down_out_ref[...] = down_sum[...].T


def attend_back(
    gate, sums, cot, gain, middle, weight, q, recalled, local, logs, p, pair, q_all, tok, up, down, rows, peers
):
    parts, count, width = q_all.shape
    span, hops, half = W + count, W // count, parts // 2
    model = sums.shape[1]
    share, own = count // peers, up.shape[0] // parts
    smem = pl.BlockSpec(memory_space=pltpu.SMEM)
    vmem = pl.BlockSpec(memory_space=pltpu.VMEM)
    dma = pltpu.SemaphoreType.DMA
    slots, sems = ScatterSum.scratch((up, down), parts)
    return pl.pallas_call(
        functools.partial(attend_back_kernel, parts=parts, peers=peers, scale=128**-0.5),
        out_shape=(
            jax.ShapeDtypeStruct((count, model), bf16),
            jax.ShapeDtypeStruct((share, model), f32),
            jax.ShapeDtypeStruct((1, model), f32),
            jax.ShapeDtypeStruct((count, 3 * width), bf16),
            jax.ShapeDtypeStruct((2, span), f32),
            jax.ShapeDtypeStruct((2, 128), f32),
            jax.ShapeDtypeStruct((own, up.shape[1]), f32),
            jax.ShapeDtypeStruct((down.shape[1], own), f32),
        ),
        in_specs=[smem] + [vmem] * 16,
        out_specs=(vmem,) * 8,
        scratch_shapes=HeadSum.scratch(count, model)
        + [
            pltpu.VMEM((count, width), bf16),
            pltpu.VMEM((2, half, count, width), bf16),
            pltpu.VMEM((8, count), f32),
            pltpu.VMEM((2, half, 8, count), f32),
        ]
        + [pltpu.VMEM((half, 2, count, 128), bf16)] * 4
        + [
            pltpu.VMEM((2, W, width), bf16),
            pltpu.VMEM((hops, 2, count, width), bf16),
            pltpu.VMEM((count, width), f32),
            pltpu.VMEM((2, count, width), f32),
        ]
        + slots
        + [pltpu.VMEM((own, down.shape[1]), f32)]
        + HeadSum.sems()
        + HeadSum.full_scratch()
        + [dma((2, half))] * 4
        + [dma((half,))] * 4
        + [dma((hops,))] * 2
        + sems,
        compiler_params=pltpu.CompilerParams(
            vmem_limit_bytes=(36 if parts <= 8 else 62) * MIB, collective_id=2, has_side_effects=True
        ),
        cost_estimate=pl.CostEstimate(
            flops=4 * 10**9, bytes_accessed=150 * MIB, transcendentals=5 * 10**6
        ),
        name="attend_back",
    )(gate, sums, cot, gain, middle, weight, q, recalled, local, logs, p, pair, q_all, tok, up, down, rows)


def close_attn_kernel(
    sum_ref, in_ref, gain_ref, full_ref, middle_ref, line_ref, a, b, c, ss_a, rs_a, ss_b, rs_b, ss_f, rs_f
):
    greet(head=4)
    sums = HeadSum(sum_ref, (a, b, c), (ss_a, rs_a, ss_b, rs_b), full_ref, (ss_f, rs_f))
    sums.start()
    sums.relay()
    branch = sums.total()
    middle = in_ref[sums.mine, :].astype(f32) + branch
    hat = middle * lax.rsqrt(row_mean(middle * middle) + eps)
    sums.spread(hat * gain_ref[...])
    middle_ref[...] = middle
    line_ref[...] = col_sum(branch * branch)
    sums.forward()
    sums.settle()


def close_attn(sums, x, gain):
    count, width = sums.shape
    vmem = pl.BlockSpec(memory_space=pltpu.VMEM)
    return pl.pallas_call(
        close_attn_kernel,
        out_shape=(
            jax.ShapeDtypeStruct((count, width), bf16),
            jax.ShapeDtypeStruct((count // 4, width), f32),
            jax.ShapeDtypeStruct((1, width), f32),
        ),
        in_specs=[vmem] * 3,
        out_specs=(vmem,) * 3,
        scratch_shapes=HeadSum.scratch(count, width) + HeadSum.sems() + HeadSum.full_scratch(),
        compiler_params=pltpu.CompilerParams(
            vmem_limit_bytes=16 * MIB, collective_id=3, has_side_effects=True
        ),
        cost_estimate=pl.CostEstimate(flops=10**6, bytes_accessed=30 * MIB, transcendentals=0),
        name="close_attn",
    )(sums, x, gain)


def row_mean(x):
    return jnp.mean(x, axis=1, keepdims=True)


def col_sum(x):
    return jnp.sum(x, axis=0, keepdims=True)


def folded(line):
    return jnp.concatenate([line[:, 128 * i : 128 * i + 128] for i in range(8)], axis=0)


def fold_sum(line):
    return col_sum(folded(line))


def finish_kernel(
    back_ref,
    feed_ref,
    in_ref,
    gain_ref,
    grad_middle_ref,
    middle_ref,
    gain_line_ref,
    attn_line_ref,
    extra_ref,
    grad_a,
    grad_b,
    input_grad_ref,
    layer_ref,
    out_a,
    out_b,
    small_ref,
    back_a,
    back_b,
    back_c,
    feed_a,
    feed_b,
    feed_c,
    in_a,
    in_b,
    in_c,
    in_d,
    in_e,
    res_a,
    res_b,
    res_c,
    res_d,
    res_e,
    small_head,
    small_seq,
    small_send,
    bs_a,
    bs_b,
    bs_c,
    bs_d,
    fs_a,
    fs_b,
    fs_c,
    fs_d,
    bf_ss,
    bf_rs,
    ff_ss,
    ff_rs,
    sh_ss,
    sh_rs,
    sq_ss,
    sq_rs,
    sem_a,
    sem_b,
    sem_c,
    sem_d,
    sem_e,
    sem_f,
    *,
    parts,
    peers,
):
    count = back_ref.shape[0]
    me, head = lax.axis_index("seq"), lax.axis_index("head")
    greet(seq=parts, head=peers)
    backs = HeadSum(
        back_ref, (back_a, back_b, back_c), (bs_a, bs_b, bs_c, bs_d), input_grad_ref, (bf_ss, bf_rs)
    )
    feeds = HeadSum(
        feed_ref, (feed_a, feed_b, feed_c), (fs_a, fs_b, fs_c, fs_d), layer_ref, (ff_ss, ff_rs)
    )
    backs.start()
    feeds.start()
    scatter = ScatterSum(
        ((grad_a, in_a, in_b, in_c, in_d, in_e), (grad_b, res_a, res_b, res_c, res_d, res_e)),
        (sem_a, sem_b, sem_c, sem_d, sem_e, sem_f),
        parts,
    )
    for far in (True, False):
        for side in range(2):
            scatter.start(far, side)

    backs.relay()
    feeds.relay()
    tokens = in_ref[backs.mine, :].astype(f32)
    scale = lax.rsqrt(row_mean(tokens * tokens) + eps)
    hat = tokens * scale
    grad_normed = backs.total()
    g = grad_normed * gain_ref[...]
    backs.spread(grad_middle_ref[...] + scale * (g - hat * row_mean(g * hat)))
    branch = feeds.total()
    layer = middle_ref[...] + branch
    feeds.spread(layer)
    scatter.pair(True)
    small_send[0:8] = folded(col_sum(grad_normed * hat))
    small_send[8:16] = folded(gain_line_ref[...])
    small_send[16:24] = extra_ref[...]
    small_send[16:17] = fold_sum(col_sum(layer * layer))
    small_send[17:18] = fold_sum(attn_line_ref[...])
    small_send[18:19] = fold_sum(col_sum(branch * branch))

    def send_head(d):
        peer = lax.rem(head + d, peers)
        return send(small_send, small_head.at[d], sh_ss.at[d], sh_rs.at[d], "head", peer)

    for d in range(1, peers):
        send_head(d).start()

    scatter.far()
    backs.forward()
    feeds.forward()

    kept = lax.broadcasted_iota(jnp.int32, (24, 128), 0) < 19
    found = small_send[...]
    for d in range(1, peers):
        send_head(d).wait()
        found = found + jnp.where(kept, small_head[d], 0.0)
    small_seq[0] = found

    def send_seq(d):
        peer = lax.rem(me + d, parts)
        return send(small_seq.at[0], small_seq.at[d], sq_ss.at[d], sq_rs.at[d], "seq", peer)

    def start_seq(d, carry):
        send_seq(d).start()
        return carry

    lax.fori_loop(1, parts, start_seq, 0)

    scatter.pair(False)
    scatter.settle((out_a, out_b))
    small_ref[...] = small_seq[0]

    def add_seq(d, carry):
        send_seq(d).wait()
        small_ref[...] += small_seq[d]
        return carry

    lax.fori_loop(1, parts, add_seq, 0)
    backs.settle()
    feeds.settle()


def finish(back, feed, x, gain, grad_middle, middle, gain_line, attn_line, extra, grad_a, grad_b, parts, peers):
    count, width = back.shape
    own = grad_a.shape[0] // parts
    slots, sems = ScatterSum.scratch((grad_a, grad_b), parts)
    wide_a, wide_b = grad_a.shape[1], grad_b.shape[1]
    vmem = pl.BlockSpec(memory_space=pltpu.VMEM)
    dma = pltpu.SemaphoreType.DMA
    return pl.pallas_call(
        functools.partial(finish_kernel, parts=parts, peers=peers),
        out_shape=(
            jax.ShapeDtypeStruct((count, width), bf16),
            jax.ShapeDtypeStruct((count, width), bf16),
            jax.ShapeDtypeStruct((own, wide_a), f32),
            jax.ShapeDtypeStruct((own, wide_b), f32),
            jax.ShapeDtypeStruct((24, 128), f32),
        ),
        in_specs=[vmem] * 11,
        out_specs=(vmem,) * 5,
        scratch_shapes=HeadSum.scratch(count, width) * 2
        + slots
        + [
            pltpu.VMEM((peers, 24, 128), f32),
            pltpu.VMEM((parts, 24, 128), f32),
            pltpu.VMEM((24, 128), f32),
        ]
        + HeadSum.sems() * 2
        + HeadSum.full_scratch() * 2
        + [dma((peers,))] * 2
        + [dma((parts,))] * 2
        + sems,
        compiler_params=pltpu.CompilerParams(
            vmem_limit_bytes=40 * MIB, collective_id=5, has_side_effects=True
        ),
        cost_estimate=pl.CostEstimate(flops=10**7, bytes_accessed=100 * MIB, transcendentals=0),
        name="finish",
    )(back, feed, x, gain, grad_middle, middle, gain_line, attn_line, extra, grad_a, grad_b)


def norm_stats(values):
    row_scale = lax.rsqrt(jnp.mean(values * values, axis=-1, keepdims=True) + eps)
    return (values * row_scale, row_scale)


def per_device(
    inputs,
    cotangent,
    query_weight,
    key_weight,
    value_weight,
    output_weight,
    up_weight,
    down_weight,
    first_gain,
    second_gain,
    position_bias,
    gate_bias,
    memory_table,
    retrieved,
    lengths,
):
    _, block_len, model_width = inputs.shape
    bucket_total = position_bias.shape[1]
    seq_count = lax.axis_size("seq")
    slot_count = memory_table.shape[0]

    wanted = jnp.transpose(retrieved[0], (1, 0, 2))
    token = jnp.arange(block_len, dtype=jnp.int32)[None, :, None]
    codes = (wanted // slot_count) * (block_len * slot_count) + token * slot_count + wanted % slot_count
    codes = lax.sort(codes.reshape(2, -1), dimension=1, is_stable=False)
    places, tok = request(codes, seq_count, slot_count, block_len)
    rows = gather_rows(places, widen(memory_table))

    hot, outside = diagonal_buckets(block_len, bucket_total)
    bias_row = jnp.dot(position_bias, hot, precision=highest) + outside[None]

    x, cot = inputs[0], cotangent[0]
    peers = lax.axis_size("head")
    gain_one, gain_two = first_gain[None], second_gain[None]
    gate_flat = jax.nn.sigmoid(gate_bias)
    hat_one, _ = norm_stats(x.astype(f32))
    normed_one = (hat_one * first_gain).astype(bf16)
    queries = nn(normed_one, query_weight).astype(bf16)
    keys = nn(normed_one, key_weight).astype(bf16)
    values = nn(normed_one, value_weight).astype(bf16)
    q_all = lax.all_gather(queries, "seq", axis=0)

    mixed, recalled, local_out, logs, window_weights, pair = attend(
        lengths[0], gate_flat, queries, keys, values, bias_row, q_all, tok, rows
    )

    normed_two, middle, attn_line = close_attn(nn(mixed, output_weight).astype(bf16), x, gain_two)
    upward = nn(normed_two, up_weight)
    gelu_value, gelu_back = jax.vjp(jax.nn.gelu, upward)
    hidden = gelu_value.astype(bf16)
    grad_upward = gelu_back(nt(cot, down_weight))[0].astype(bf16)
    grad_branch, grad_middle, gain_line, grad_heads, pos_rows, gate_rows, up_grad, down_grad = attend_back(
        gate_flat,
        nt(grad_upward, up_weight).astype(bf16),
        cot,
        gain_two,
        middle,
        output_weight,
        queries,
        recalled,
        local_out,
        logs,
        window_weights,
        pair,
        q_all,
        tok,
        tn(normed_two, grad_upward).astype(bf16),
        tn(cot, hidden).astype(bf16),
        rows,
        peers,
    )
    feed = nn(hidden, down_weight).astype(bf16)
    gate_part = jnp.sum(gate_rows, axis=1) * gate_flat * (1.0 - gate_flat)
    position_part = jnp.dot(pos_rows, hot.T, precision=highest)
    extra = jnp.zeros((8, 128), f32)
    extra = extra.at[3:5, :bucket_total].set(position_part).at[5, :2].set(gate_part)
    back = (
        nt(grad_heads[:, :256], query_weight)
        + nt(grad_heads[:, 256:512], key_weight)
        + nt(grad_heads[:, 512:], value_weight)
    )
    input_grad, layer_out, grads_in, grads_out, small = finish(
        back.astype(bf16),
        feed,
        x,
        gain_one,
        grad_middle,
        middle,
        gain_line,
        attn_line,
        extra,
        tn(normed_one, grad_heads).astype(bf16),
        tn(grad_branch, mixed).astype(bf16),
        seq_count,
        peers,
    )
    entry_count = float(block_len * model_width * seq_count)
    share = model_width // seq_count
    gains = small[:16].reshape(2, model_width)
    own_gains = lax.dynamic_slice_in_dim(gains, lax.axis_index("seq") * share, share, 1)
    return (
        layer_out[None],
        input_grad.astype(f32)[None],
        grads_in[:, 0:256],
        grads_in[:, 256:512],
        grads_in[:, 512:768],
        grads_out.T,
        up_grad,
        down_grad,
        own_gains[0],
        own_gains[1],
        small[19:21, :bucket_total],
        small[21, :2],
        jnp.sqrt(jnp.sum(small[16:19], axis=1) / entry_count),
    )


def solution(mesh):
    in_specs = (
        P(None, "seq", None),
        P(None, "seq", None),
        P(None, "head"),
        P(None, "head"),
        P(None, "head"),
        P("head", None),
        P(None, "head"),
        P("head", None),
        P(),
        P(),
        P("head", None),
        P("head"),
        P("seq", "head", None),
        P(None, "seq", "head", None),
        P(),
    )
    out_specs = (
        P(None, "seq", None),
        P(None, "seq", None),
        P("seq", "head"),
        P("seq", "head"),
        P("seq", "head"),
        P("head", "seq"),
        P("seq", "head"),
        P("head", "seq"),
        P("seq"),
        P("seq"),
        P("head", None),
        P("head"),
        P(),
    )
    return jax.shard_map(
        per_device, mesh=mesh, in_specs=in_specs, out_specs=out_specs, check_vma=False
    )
```

```python
import functools
import math
import types

import jax
import jax.numpy as jnp
import numpy as np
from jax import lax
from jax.experimental import pallas as pl
from jax.experimental.pallas import tpu as pltpu
from jax.sharding import PartitionSpec as P

W = 512
eps = 1e-06
exact_span = 16
far_distance = 128
highest = lax.Precision.HIGHEST
f32 = jnp.float32
bf16 = jnp.bfloat16
NEG = -1e30
MIB = 2**20


def bucket_table(key_span, bucket_total):
    found = []
    for distance in range(key_span):
        if distance < exact_span:
            found.append(distance)
        else:
            scaled = math.log(distance / exact_span) / math.log(far_distance / exact_span)
            found.append(
                min(bucket_total - 1, exact_span + math.floor(scaled * (bucket_total - exact_span)))
            )
    return np.asarray(found)


def diagonal_buckets(block_len, bucket_total):
    span = W + block_len
    table = bucket_table(W, bucket_total)
    hot = np.zeros((bucket_total, span), np.float32)
    for u in range(1, W + 1):
        hot[table[W - u], u] = 1.0
    outside = np.where(hot.sum(0) > 0, 0.0, NEG).astype(np.float32)
    return hot, outside


def nt(a, b):
    return lax.dot_general(a, b, (((1,), (1,)), ((), ())), preferred_element_type=f32)


def nn(a, b):
    return lax.dot_general(a, b, (((1,), (0,)), ((), ())), preferred_element_type=f32)


def tn(a, b):
    return lax.dot_general(a, b, (((0,), (0,)), ((), ())), preferred_element_type=f32)


def widen_kernel(table_hbm, wide_hbm, buf, out, sem, out_sem, *, chunk, part):
    chunks = table_hbm.shape[0] // chunk

    def fetch(i):
        return pltpu.make_async_copy(
            table_hbm.at[pl.ds(i * chunk, chunk)], buf.at[i % 2], sem.at[i % 2]
        )

    def store(i):
        return pltpu.make_async_copy(
            out.at[i % 2], wide_hbm.at[:, pl.ds(2 * i * chunk, 2 * chunk)], out_sem.at[i % 2]
        )

    fetch(0).start()
    for i in range(chunks):
        fetch(i).wait()
        if i + 1 < chunks:
            fetch(i + 1).start()
        if i > 1:
            store(i - 2).wait()

        def widen(q, carry, i=i):
            x = buf[i % 2, pl.ds(q * part, part)].astype(f32)
            for r in range(part):
                for h in range(2):
                    place = pl.ds(2 * (q * part + r), 1)
                    out[i % 2, h, place, :] = x[r, h : h + 1, 0:128]
                    place = pl.ds(2 * (q * part + r) + 1, 1)
                    out[i % 2, h, place, :] = x[r, h : h + 1, 128:256]
            return carry

        lax.fori_loop(0, chunk // part, widen, 0)
        store(i).start()
    for i in range(max(0, chunks - 2), chunks):
        store(i).wait()


def widen(table):
    total = table.shape[0]
    chunk = min(1024, total)
    hbm = pl.BlockSpec(memory_space=pltpu.HBM)
    dma = pltpu.SemaphoreType.DMA
    return pl.pallas_call(
        functools.partial(widen_kernel, chunk=chunk, part=32),
        out_shape=jax.ShapeDtypeStruct((2, 2 * total, 128), f32),
        in_specs=[hbm],
        out_specs=hbm,
        scratch_shapes=[
            pltpu.VMEM((2, chunk, 2, 256), bf16),
            pltpu.VMEM((2, 2, 2 * chunk, 128), f32),
            dma((2,)),
            dma((2,)),
        ],
        compiler_params=pltpu.CompilerParams(vmem_limit_bytes=58 * MIB),
        cost_estimate=pl.CostEstimate(flops=0, bytes_accessed=40 * MIB, transcendentals=0),
        name="widen",
    )(table)


def gather_kernel(at_ref, wide_hbm, out_hbm, wide, buf, low, wide_sem, out_sem, *, unroll, group):
    parts, rows = out_hbm.shape[0], out_hbm.shape[2]

    def fetch(h):
        return pltpu.make_async_copy(wide_hbm.at[h], wide.at[h], wide_sem.at[h])

    def store(j, h, slot):
        return pltpu.make_async_copy(low.at[slot], out_hbm.at[j, h], out_sem.at[slot])

    for h in range(2):
        fetch(h).start()
    for h in range(2):
        fetch(h).wait()

        def one(j, carry, h=h):
            slot = lax.rem(j, 2)
            first = (2 * j + h) * rows

            def copy_rows(q, carry):
                base = q * unroll
                for g in range(0, unroll, group):
                    found = [
                        wide[h, pl.ds(at_ref[first + base + g + u], 2), :] for u in range(group)
                    ]
                    for u in range(group):
                        buf[pl.ds(2 * (base + g + u), 2), :] = found[u]
                return carry

            lax.fori_loop(0, rows // unroll, copy_rows, 0)

            if h == 0:

                @pl.when(j > 1)
                def _():
                    store(j, h, slot).wait()

            else:
                store(j, h, slot).wait()

            low[slot, :, 0:128] = buf[pl.ds(0, rows, 2), :].astype(bf16)
            low[slot, :, 128:256] = buf[pl.ds(1, rows, 2), :].astype(bf16)
            store(j, h, slot).start()
            return carry

        lax.fori_loop(0, parts, one, 0)
    store(0, 1, 0).wait()
    store(1, 1, 1).wait()


def gather_rows(places, wide):
    parts, heads, rows = places.shape
    unroll = min(64, rows)
    hbm = pl.BlockSpec(memory_space=pltpu.HBM)
    dma = pltpu.SemaphoreType.DMA
    return pl.pallas_call(
        functools.partial(gather_kernel, unroll=unroll, group=unroll // 2),
        out_shape=jax.ShapeDtypeStruct((parts, heads, rows, 256), bf16),
        in_specs=[pl.BlockSpec(memory_space=pltpu.SMEM), hbm],
        out_specs=hbm,
        scratch_shapes=[
            pltpu.VMEM(wide.shape, f32),
            pltpu.VMEM((2 * rows, 128), f32),
            pltpu.VMEM((2, rows, 256), bf16),
            dma((2,)),
            dma((2,)),
        ],
        compiler_params=pltpu.CompilerParams(vmem_limit_bytes=58 * MIB),
        cost_estimate=pl.CostEstimate(flops=0, bytes_accessed=100 * MIB, transcendentals=0),
        name="gather_rows",
    )(places.reshape(-1), wide)


MESH = pl.DeviceIdType.MESH


def greet(**counts):
    barrier = pltpu.get_barrier_semaphore()
    for axis, count in counts.items():
        me = lax.axis_index(axis)

        def call(d, carry, axis=axis, count=count, me=me):
            peer = lax.rem(me + d, count)
            pl.semaphore_signal(barrier, inc=1, device_id={axis: peer}, device_id_type=MESH)
            return carry

        lax.fori_loop(1, count, call, 0)
    pl.semaphore_wait(barrier, sum(counts.values()) - len(counts))


def send(src, dst, send_sem, recv_sem, axis, peer):
    return pltpu.make_async_remote_copy(
        src_ref=src,
        dst_ref=dst,
        send_sem=send_sem,
        recv_sem=recv_sem,
        device_id={axis: peer},
        device_id_type=MESH,
    )


def doc_starts(lengths_ref, first, count):
    place = first + lax.broadcasted_iota(jnp.int32, (count, 1), 0)
    start = jnp.zeros((count, 1), jnp.int32)
    end = jnp.int32(0)
    for c in range(lengths_ref.shape[0]):
        end = end + lengths_ref[c]
        start = jnp.where(end <= place, end, start)
    return start


def head_cols(h):
    return slice(h * 128, h * 128 + 128)


def row_form(columns, count):
    lane = lax.broadcasted_iota(jnp.int32, (count, 128), 1)
    wide = jnp.zeros((count, 128), f32)
    for i, column in enumerate(columns):
        wide = jnp.where(lane == i, column, wide)
    return wide


def request_kernel(codes_ref, place_ref, tok_ref, got, own_sem, ss, rs, *, parts, slots, tokens):
    rows = codes_ref.shape[1] // parts
    me = lax.axis_index("seq")

    def part(owner):
        return codes_ref.at[:, pl.ds(pl.multiple_of(owner * rows, 128), rows)]

    keep = pltpu.make_async_copy(part(me), got.at[0], own_sem)
    keep.start()
    greet(seq=parts)

    def ask(d):
        peer = lax.rem(me + d, parts)
        return send(part(peer), got.at[d], ss.at[d], rs.at[d], "seq", peer)

    def start(d, carry):
        ask(d).start()
        return carry

    lax.fori_loop(1, parts, start, 0)
    shift = slots.bit_length() - 1

    def read(d, j):
        code = got[d]
        place_ref[j] = (code & (slots - 1)) * 2
        tok_ref[j] = (code >> shift) & (tokens - 1)

    keep.wait()
    read(0, me)

    def arrive(d, carry):
        ask(d).wait()
        read(d, lax.rem(me + parts - d, parts))
        return carry

    lax.fori_loop(1, parts, arrive, 0)


def request(codes, parts, slots, tokens):
    rows = codes.shape[1] // parts
    vmem = pl.BlockSpec(memory_space=pltpu.VMEM)
    dma = pltpu.SemaphoreType.DMA
    shape = (parts, 2, rows)
    return pl.pallas_call(
        functools.partial(request_kernel, parts=parts, slots=slots, tokens=tokens),
        out_shape=(jax.ShapeDtypeStruct(shape, jnp.int32),) * 2,
        in_specs=[vmem],
        out_specs=(vmem,) * 2,
        scratch_shapes=[pltpu.VMEM(shape, jnp.int32), dma, dma((parts,)), dma((parts,))],
        compiler_params=pltpu.CompilerParams(
            vmem_limit_bytes=8 * MIB, collective_id=6, has_side_effects=True
        ),
        name="request",
    )(codes)


class HeadSum:
    def __init__(self, src, scratch, sems, full=None, full_sems=None):
        self.src, self.full = src, full
        self.core_recv, self.side_send, self.side_recv = scratch
        self.core_ss, self.core_rs, self.side_ss, self.side_rs = sems
        self.full_sems = full_sems
        head = lax.axis_index("head")
        self.y, self.c = head // 2, lax.rem(head, 2)
        self.share = src.shape[0] // 4
        self.core = 2 * self.y + 1 - self.c
        self.side = 2 * (1 - self.y) + self.c
        self.mine = self.rows_of(head)

    def rows_of(self, place):
        return pl.ds(pl.multiple_of(place * self.share, self.share), self.share)

    def to_core(self, i):
        y = self.y if i == 0 else 1 - self.y
        src = self.src.at[self.rows_of(2 * y + 1 - self.c)]
        return send(src, self.core_recv.at[i], self.core_ss.at[i], self.core_rs.at[i], "head", self.core)

    def to_side(self):
        return send(self.side_send, self.side_recv, self.side_ss, self.side_rs, "head", self.side)

    def start(self):
        self.to_core(1).start()
        self.to_core(0).start()

    def relay(self):
        self.to_core(1).wait()
        other = self.src[self.rows_of(self.side), :].astype(f32)
        self.side_send[...] = (other + self.core_recv[1].astype(f32)).astype(bf16)
        self.to_side().start()

    def total(self):
        self.to_core(0).wait()
        found = self.src[self.mine, :].astype(f32) + self.core_recv[0].astype(f32)
        self.to_side().wait()
        return found + self.side_recv[...].astype(f32)

    def back(self, i):
        rows = self.rows_of(self.side) if i == 2 else self.mine
        peer = self.side if i == 1 else self.core
        ss, rs = self.full_sems
        return send(self.full.at[rows], self.full.at[rows], ss.at[i], rs.at[i], "head", peer)

    def spread(self, value):
        self.full[self.mine, :] = value.astype(self.full.dtype)
        self.back(1).start()
        self.back(0).start()

    def forward(self):
        self.back(1).wait()
        self.back(2).start()

    def settle(self):
        self.back(0).wait()
        self.back(2).wait()

    @staticmethod
    def scratch(count, width):
        piece = (count // 4, width)
        return [pltpu.VMEM((2,) + piece, bf16), pltpu.VMEM(piece, bf16), pltpu.VMEM(piece, bf16)]

    @staticmethod
    def sems():
        dma = pltpu.SemaphoreType.DMA
        return [dma((2,)), dma((2,)), dma, dma]

    @staticmethod
    def full_scratch():
        return [pltpu.SemaphoreType.DMA((3,))] * 2


class Held:
    def __init__(self, arrays, parts):
        self.arrays, self.parts = arrays, parts
        self.all = arrays[0][1].shape[0] == parts

    def fetch(self, i, j):
        hbm, place, sem = self.arrays[i]
        slot = j if self.all else 0
        return pltpu.make_async_copy(hbm.at[j], place.at[slot], sem.at[slot])

    def ahead(self):
        if self.all:

            def start(j, carry):
                for i in range(len(self.arrays)):
                    self.fetch(i, j).start()
                return carry

            lax.fori_loop(0, self.parts, start, 0)

    def get(self, j):
        for i in range(len(self.arrays)):
            if not self.all:
                self.fetch(i, j).start()
            self.fetch(i, j).wait()
        return [place.at[j if self.all else 0] for _, place, _ in self.arrays]

    @staticmethod
    def scratch(arrays, parts):
        slots = parts if parts <= 8 else 1
        places = [pltpu.VMEM((slots,) + a.shape[1:], a.dtype) for a in arrays]
        return places + [pltpu.SemaphoreType.DMA((slots,))] * len(arrays)


def attend_kernel(
    lengths_ref,
    gate_ref,
    q_ref,
    k_ref,
    v_ref,
    bias_ref,
    tok_ref,
    q_all_hbm,
    rows_hbm,
    mixed_ref,
    recalled_ref,
    local_ref,
    logs_ref,
    p_ref,
    pair_ref,
    out_xs,
    out_xr,
    out_zs,
    out_zr,
    log_xs,
    log_xr,
    log_zs,
    log_zr,
    q_all,
    rows,
    q_sem,
    rows_sem,
    ox_ss,
    ox_rs,
    oz_ss,
    oz_rs,
    lx_ss,
    lx_rs,
    lz_ss,
    lz_rs,
    pair_ss,
    pair_rs,
    *,
    parts,
    scale,
):
    count, span = q_ref.shape[0], pair_ref.shape[1]
    per = tok_ref.shape[2]
    half = parts // 2
    me = lax.axis_index("seq")
    x, z = lax.rem(me, 2), me // 2
    partner = me + 1 - 2 * x

    def reader(c, dz):
        at = lax.rem(z + half - dz, half)
        return 2 * at + (x if c == 0 else 1 - x)

    held = Held(((q_all_hbm, q_all, q_sem), (rows_hbm, rows, rows_sem)), parts)
    held.ahead()
    pair_ref[0, W:, :] = k_ref[...]
    pair_ref[1, W:, :] = v_ref[...]

    @pl.when(z == 0)
    def _():
        pair_ref[:, :count] = jnp.zeros_like(pair_ref[:, :count])

    @pl.when(me == 0)
    def _():
        pair_ref[:, count:W] = jnp.zeros_like(pair_ref[:, count:W])

    greet(seq=parts)

    def pair_rows(first):
        return pair_ref.at[:, pl.ds(first, count)]

    def hand_on(i, source, target, peer):
        return send(
            pair_rows(source), pair_rows(target), pair_ss.at[i], pair_rs.at[i], "seq", peer
        )

    next_one = hand_on(0, W, count, partner)
    next_two = hand_on(1, W, 0, me + 2)
    passed_on = hand_on(2, 0, count, partner)

    @pl.when(z < half - 1)
    def _():
        next_two.start()

    @pl.when(x == 0)
    def _():
        next_one.start()

    ids = lax.broadcasted_iota(jnp.int32, (count, per), 0)

    def owner_part(j):
        q_at, rows_at = held.get(j)
        outs, logs = [], []
        for h in range(2):
            cols = head_cols(h)
            keep = tok_ref[j, h : h + 1, :] == ids
            s = jnp.where(keep, nt(q_at[:, cols], rows_at[h, :, 0:128]), NEG)
            top = jnp.max(s, axis=1, keepdims=True)
            p = jnp.where(keep, jnp.exp((s - top) * scale), 0.0)
            total = jnp.sum(p, axis=1, keepdims=True)
            some = total > 0.0
            safe = jnp.where(some, total, 1.0)
            outs.append(nn(p.astype(bf16), rows_at[h, :, 128:256]) / safe)
            logs.append(jnp.where(some, top * scale + jnp.log(safe), NEG))
        return outs, logs

    def give_x(dz):
        return (
            send(log_xs.at[dz], log_xr.at[dz], lx_ss.at[dz], lx_rs.at[dz], "seq", partner),
            send(out_xs.at[dz], out_xr.at[dz], ox_ss.at[dz], ox_rs.at[dz], "seq", partner),
        )

    def log_z(dz):
        return send(
            log_zs.at[dz], log_zr.at[dz], lz_ss.at[dz], lz_rs.at[dz], "seq", reader(0, dz)
        )

    def out_z(dz):
        return send(
            out_zs.at[dz], out_zr.at[dz], oz_ss.at[dz], oz_rs.at[dz], "seq", reader(0, dz)
        )

    def neighbour(dz):
        outs, logs = owner_part(reader(1, dz))
        for h in range(2):
            out_xs[dz, h] = outs[h].astype(bf16)
        log_xs[dz] = row_form(logs, count).T[0:8]
        for copy in give_x(dz):
            copy.start()

    def join(outs, logs, dz):
        for copy in give_x(dz):
            copy.wait()
        other = log_xr[dz].T
        joined = []
        for h in range(2):
            theirs = other[:, h : h + 1]
            top = jnp.maximum(logs[h], theirs)
            a, b = jnp.exp(logs[h] - top), jnp.exp(theirs - top)
            total = a + b
            outs[h] = outs[h] * (a / total) + out_xr[dz, h].astype(f32) * (b / total)
            joined.append(top + jnp.log(total))
        return outs, joined

    def neighbour_step(dz, carry):
        neighbour(dz)
        return carry

    lax.fori_loop(1, half, neighbour_step, 0)
    neighbour(0)

    @pl.when(z > 0)
    def _():
        hand_on(1, W, 0, partner).wait_recv()

        @pl.when(x == 1)
        def _():
            passed_on.start()

    def column_step(dz, carry):
        outs, logs = owner_part(reader(0, dz))
        outs, logs = join(outs, logs, dz)
        for h in range(2):
            out_zs[dz, h] = outs[h].astype(bf16)
        log_zs[dz] = row_form(logs, count).T[0:8]
        log_z(dz).start()
        out_z(dz).start()
        return carry

    lax.fori_loop(1, half, column_step, 0)
    outs, logs = owner_part(me)
    outs, logs = join(outs, logs, 0)
    log_zr[0] = row_form(logs, count).T[0:8]
    for h in range(2):
        recalled_ref[:, head_cols(h)] = outs[h]

    @pl.when(x == 0)
    def _():
        next_one.wait_send()

        @pl.when(z > 0)
        def _():
            passed_on.wait_recv()

    @pl.when(x == 1)
    def _():
        next_one.wait_recv()

        @pl.when(z > 0)
        def _():
            passed_on.wait_send()

    @pl.when(z < half - 1)
    def _():
        next_two.wait_send()

    first = me * count
    start = doc_starts(lengths_ref, first, count)
    key_place = first - W + lax.broadcasted_iota(jnp.int32, (count, span), 1)
    seen = key_place >= start
    for h in range(2):
        cols = head_cols(h)
        bias = pltpu.roll(
            jnp.broadcast_to(bias_ref[h : h + 1, :], (count, span)), 0, 1, stride=1, stride_axis=0
        )
        s = nt(q_ref[:, cols], pair_ref[0, :, cols]) * scale + bias
        s = jnp.where(seen, s, NEG)
        raised = jnp.exp(s - jnp.max(s, axis=1, keepdims=True))
        p = raised / jnp.sum(raised, axis=1, keepdims=True)
        p_ref[h] = p
        local_ref[:, cols] = nn(p.astype(bf16), pair_ref[1, :, cols])

    def wait_log(dz, top):
        log_z(dz).wait()
        return jnp.maximum(top, log_zr[dz])

    top = lax.fori_loop(1, half, wait_log, log_zr[0])

    def add_to(dz, total):
        return total + jnp.exp(log_zr[dz] - top)

    logs = top + jnp.log(lax.fori_loop(0, half, add_to, jnp.zeros_like(top)))
    logs_ref[...] = logs
    share = jnp.exp(log_zr[0] - logs).T
    for h in range(2):
        recalled_ref[:, head_cols(h)] *= share[:, h : h + 1]

    def merge(dz, carry):
        share = jnp.exp(log_zr[dz] - logs).T
        out_z(dz).wait()
        for h in range(2):
            recalled_ref[:, head_cols(h)] += share[:, h : h + 1] * out_zr[dz, h].astype(f32)
        return carry

    lax.fori_loop(1, half, merge, 0)
    for h in range(2):
        cols = head_cols(h)
        gate = gate_ref[h]
        mixed = gate * recalled_ref[:, cols] + (1.0 - gate) * local_ref[:, cols]
        mixed_ref[:, cols] = mixed.astype(bf16)


def attend(lengths, gate, q, k, v, bias, q_all, tok, rows):
    parts, count, width = q_all.shape
    span, half = W + count, parts // 2
    smem = pl.BlockSpec(memory_space=pltpu.SMEM)
    vmem = pl.BlockSpec(memory_space=pltpu.VMEM)
    hbm = pl.BlockSpec(memory_space=pltpu.HBM)
    dma = pltpu.SemaphoreType.DMA
    return pl.pallas_call(
        functools.partial(attend_kernel, parts=parts, scale=128**-0.5),
        out_shape=(
            jax.ShapeDtypeStruct((count, width), bf16),
            jax.ShapeDtypeStruct((count, width), f32),
            jax.ShapeDtypeStruct((count, width), f32),
            jax.ShapeDtypeStruct((8, count), f32),
            jax.ShapeDtypeStruct((2, count, span), f32),
            jax.ShapeDtypeStruct((2, span, width), bf16),
        ),
        in_specs=[smem, smem] + [vmem] * 5 + [hbm] * 2,
        out_specs=(vmem,) * 6,
        scratch_shapes=[pltpu.VMEM((half, 2, count, 128), bf16)] * 4
        + [pltpu.VMEM((half, 8, count), f32)] * 4
        + Held.scratch((q_all, rows), parts)
        + [dma((half,))] * 8
        + [dma((3,))] * 2,
        compiler_params=pltpu.CompilerParams(
            vmem_limit_bytes=58 * MIB, collective_id=1, has_side_effects=True
        ),
        cost_estimate=pl.CostEstimate(
            flops=3 * 10**9, bytes_accessed=100 * MIB, transcendentals=5 * 10**6
        ),
        name="attend",
    )(lengths, gate, q, k, v, bias, tok, q_all, rows)


class ScatterSum:
    def __init__(self, grads, sems, parts):
        self.grads, self.sems = grads, sems
        self.quarter = parts // 4
        self.own = grads[0][0].shape[0] // parts
        me = lax.axis_index("seq")
        self.x, self.b, self.a = lax.rem(me, 2), lax.rem(me // 2, 2), me // 4

    def place(self, da, side, x):
        b = self.b if side == 1 else 1 - self.b
        return 4 * lax.rem(self.a + da, self.quarter) + 2 * b + x

    def rows_of(self, place):
        return pl.ds(pl.multiple_of(place * self.own, self.own), self.own)

    def send_x(self, k, da, side):
        ss, rs = self.sems[0:2]
        return send(
            self.grads[k][0].at[self.rows_of(self.place(da, side, 1 - self.x))],
            self.grads[k][1].at[side, da],
            ss.at[k, side, da],
            rs.at[k, side, da],
            "seq",
            self.place(0, 1, 1 - self.x),
        )

    def send_pair(self, k, da):
        ss, rs = self.sems[2:4]
        grads, peer = self.grads[k], self.place(0, 0, self.x)
        return send(grads[2].at[da], grads[3].at[da], ss.at[k, da], rs.at[k, da], "seq", peer)

    def send_far(self, k, da):
        ss, rs = self.sems[4:6]
        grads, peer = self.grads[k], self.place(da, 1, self.x)
        return send(grads[4].at[da], grads[5].at[da], ss.at[k, da], rs.at[k, da], "seq", peer)

    def loop(self, first, last, step):
        def body(da, carry):
            for k in range(len(self.grads)):
                step(k, da)
            return carry

        lax.fori_loop(first, last, body, 0)

    def span(self, far):
        return (1, self.quarter) if far else (0, 1)

    def start(self, far, side):
        self.loop(*self.span(far), lambda k, da: self.send_x(k, da, side).start())

    def start_one(self, k):
        for far in (True, False):
            for side in range(2):

                def body(da, carry, side=side):
                    self.send_x(k, da, side).start()
                    return carry

                lax.fori_loop(*self.span(far), body, 0)

    def column(self, k, da, side):
        self.send_x(k, da, side).wait()
        mine = self.grads[k][0][self.rows_of(self.place(da, side, self.x)), :]
        return mine.astype(f32) + self.grads[k][1][side, da].astype(f32)

    def pair(self, far):
        def step(k, da):
            self.grads[k][2][da] = self.column(k, da, 0).astype(bf16)
            self.send_pair(k, da).start()

        self.loop(*self.span(far), step)

    def both(self, k, da):
        found = self.column(k, da, 1)
        self.send_pair(k, da).wait()
        return found + self.grads[k][3][da].astype(f32)

    def far(self):
        def step(k, da):
            self.grads[k][4][da] = self.both(k, da).astype(bf16)
            self.send_far(k, da).start()

        self.loop(*self.span(True), step)

    def settle(self, outs):
        for k, out in enumerate(outs):
            out[...] = self.both(k, 0)

        def step(k, da):
            self.send_far(k, da).wait()
            outs[k][...] += self.grads[k][5][da].astype(f32)

        self.loop(*self.span(True), step)

    @staticmethod
    def scratch(shapes, parts):
        quarter = parts // 4
        slots = []
        for rows, columns in shapes:
            piece = (rows // parts, columns)
            slots.append(pltpu.VMEM((2, quarter) + piece, bf16))
            slots += [pltpu.VMEM((quarter,) + piece, bf16)] * 4
        dma = pltpu.SemaphoreType.DMA
        count = len(shapes)
        return slots, [dma((count, 2, quarter))] * 2 + [dma((count, quarter))] * 4


def close_attn_kernel(*refs, names, parts):
    r = types.SimpleNamespace(**dict(zip(names, refs, strict=True)))
    greet(seq=parts, head=4)
    sums = HeadSum(
        r.sum, (r.a, r.b, r.c), (r.ss_a, r.rs_a, r.ss_b, r.rs_b), r.full, (r.ss_full, r.rs_full)
    )
    sums.start()
    copies = []
    if hasattr(r, "cot_other"):
        crossed = (
            ("cot", "z", r.cot, r.cot_other),
            ("normed", "x", r.normed, r.normed_other),
        )
        for name, first, left, other in crossed:
            joined = JoinedSum([(left, other, left, left)], [None] * 4, parts, first)
            sems = getattr(r, f"{name}_ss"), getattr(r, f"{name}_rs")
            copies += joined.cross_blocks(0, sems)
        sems = (r.mixed_ss, r.mixed_rs)
        joined = JoinedSum([(r.normed, r.normed, r.mixed, r.mixed_other)], [None] * 4, parts, "x")
        copies += joined.cross(0, sems)
        for copy in copies:
            copy.start()
    sums.relay()
    branch = sums.total()
    middle = r.inputs[sums.mine, :].astype(f32) + branch
    hat = middle * lax.rsqrt(row_mean(middle * middle) + eps)
    sums.spread(hat * r.gain[...])
    r.middle[...] = middle
    r.line[...] = col_sum(branch * branch)
    sums.forward()
    sums.settle()
    for copy in copies:
        copy.wait()


def close_attn(inputs, parts):
    count, width = inputs["sum"].shape
    vmem = pl.BlockSpec(memory_space=pltpu.VMEM)
    dma = pltpu.SemaphoreType.DMA
    outputs = dict(
        full=jax.ShapeDtypeStruct((count, width), bf16),
        middle=jax.ShapeDtypeStruct((count // 4, width), f32),
        line=jax.ShapeDtypeStruct((1, width), f32),
    )
    scratch = dict(zip("abc", HeadSum.scratch(count, width), strict=True))
    scratch |= dict(zip(("ss_a", "rs_a", "ss_b", "rs_b"), HeadSum.sems(), strict=True))
    scratch |= dict(zip(("ss_full", "rs_full"), HeadSum.full_scratch(), strict=True))
    if width // parts % 128 == 0:
        for name in ("cot", "normed"):
            outputs[f"{name}_other"] = jax.ShapeDtypeStruct((count, width // 2), bf16)
            scratch |= {f"{name}_{end}": dma((parts // 2,)) for end in ("ss", "rs")}
        outputs["mixed_other"] = jax.ShapeDtypeStruct(inputs["mixed"].shape, bf16)
        scratch |= {f"mixed_{end}": dma((1,)) for end in ("ss", "rs")}
    found = pl.pallas_call(
        functools.partial(close_attn_kernel, names=(*inputs, *outputs, *scratch), parts=parts),
        out_shape=tuple(outputs.values()),
        in_specs=[vmem] * len(inputs),
        out_specs=(vmem,) * len(outputs),
        scratch_shapes=list(scratch.values()),
        compiler_params=pltpu.CompilerParams(
            vmem_limit_bytes=16 * MIB, collective_id=3, has_side_effects=True
        ),
        cost_estimate=pl.CostEstimate(flops=10**6, bytes_accessed=30 * MIB, transcendentals=0),
        name="close_attn",
    )(*inputs.values())
    return dict(zip(outputs, found, strict=True))


def row_mean(x):
    return jnp.mean(x, axis=1, keepdims=True)


def col_sum(x):
    return jnp.sum(x, axis=0, keepdims=True)


def folded(line):
    return jnp.concatenate([line[:, 128 * i : 128 * i + 128] for i in range(8)], axis=0)


def fold_sum(line):
    return col_sum(folded(line))


class JoinedSum(ScatterSum):
    def __init__(self, grads, sems, parts, first):
        super().__init__([(g[0], *g[4:]) for g in grads], sems, parts)
        self.own = grads[0][0].shape[1] // parts
        self.operands = [g[0:4] for g in grads]
        self.first = first

    def side_of(self, first, second):
        return 2 * first + second if self.first == "z" else 2 * second + first

    def mine(self):
        return (self.b, self.x) if self.first == "z" else (self.x, self.b)

    def place(self, da, side, flip=0):
        first, second = self.mine()
        first = 1 - first if flip else first
        second = second if side == 1 else 1 - second
        return 4 * lax.rem(self.a + da, self.quarter) + self.side_of(first, second)

    def partner(self):
        return self.place(0, 1, 1)

    def columns(self, place):
        return pl.ds(pl.multiple_of(place * self.own, self.own), self.own)

    def cross_blocks(self, k, sems):
        left, slots = self.operands[k][0:2]
        first, _ = self.mine()
        copies = []
        for block in range(2 * self.quarter):
            place = 4 * (block // 2) + self.side_of(1 - first, block % 2)
            copies.append(
                send(
                    left.at[:, self.columns(place)],
                    slots.at[:, pl.ds(block * self.own, self.own)],
                    sems[0].at[block],
                    sems[1].at[block],
                    "seq",
                    self.partner(),
                )
            )
        return copies

    def cross(self, k, sems):
        right, slots = self.operands[k][2:4]
        return [send(right, slots, sems[0].at[0], sems[1].at[0], "seq", self.partner())]

    def send_pair(self, k, da):
        ss, rs = self.sems[0:2]
        grads, peer = self.grads[k], self.place(0, 0)
        return send(grads[1].at[da], grads[2].at[da], ss.at[k, da], rs.at[k, da], "seq", peer)

    def send_far(self, k, da):
        ss, rs = self.sems[2:4]
        grads, peer = self.grads[k], self.place(da, 1)
        return send(grads[3].at[da], grads[4].at[da], ss.at[k, da], rs.at[k, da], "seq", peer)

    def column(self, k, da, side):
        left, left_other, right, right_other = self.operands[k]
        _, second = self.mine()
        second = second if side == 1 else 1 - second
        block = 2 * lax.rem(self.a + da, self.quarter) + second
        found = tn(left[:, self.columns(self.place(da, side))], right[...])
        return found + tn(left_other[:, self.columns(block)], right_other[...])

    def pair(self, far):
        def step(k, da):
            self.grads[k][1][da] = self.column(k, da, 0).astype(bf16)
            self.send_pair(k, da).start()

        self.loop(*self.span(far), step)

    def both(self, k, da):
        found = self.column(k, da, 1)
        self.send_pair(k, da).wait()
        return found + self.grads[k][2][da].astype(f32)

    def far(self):
        def step(k, da):
            self.grads[k][3][da] = self.both(k, da).astype(bf16)
            self.send_far(k, da).start()

        self.loop(*self.span(True), step)

    def settle(self, outs):
        for k, out in enumerate(outs):
            out[...] = self.both(k, 0)

        def step(k, da):
            self.send_far(k, da).wait()
            outs[k][...] += self.grads[k][4][da].astype(f32)

        self.loop(*self.span(True), step)

    @staticmethod
    def scratch(shapes, parts):
        quarter = parts // 4
        slots = []
        for rows, columns in shapes:
            slots += [pltpu.VMEM((quarter, rows // parts, columns), bf16)] * 4
        return slots, [pltpu.SemaphoreType.DMA((len(shapes), quarter))] * 4


class Product:
    def __init__(self, r, name, left, right, parts, first, left_other=None, right_other=None):
        self.left, self.right = left, right
        self.joined = left.shape[1] // parts % 128 == 0

        def own(part):
            return getattr(r, f"{name}_{part}")

        if self.joined:
            left_slots = own("left") if left_other is None else left_other
            right_slots = own("right") if right_other is None else right_other
            grads = (left, left_slots, right, right_slots, *(own(i) for i in range(4)))
            self.sum = JoinedSum([grads], [own(f"sem_{i}") for i in range(4)], parts, first)
            self.lefts, self.rights = [], []
            if left_other is None:
                self.lefts = self.sum.cross_blocks(0, (own("left_ss"), own("left_rs")))
            if right_other is None:
                self.rights = self.sum.cross(0, (own("right_ss"), own("right_rs")))
        else:
            self.whole = own("whole")
            grads = (self.whole, *(own(i) for i in range(5)))
            self.sum = ScatterSum([grads], [own(f"sem_{i}") for i in range(6)], parts)
        self.pair, self.far = self.sum.pair, self.sum.far

    def begin_left(self):
        if self.joined:
            for copy in self.lefts:
                copy.start()

    def begin(self):
        if self.joined:
            for copy in self.rights:
                copy.start()
        else:
            for b in range(self.left.shape[1] // 256):
                block = slice(256 * b, 256 * b + 256)
                self.whole[block, :] = tn(self.left[:, block], self.right[...]).astype(bf16)
            self.sum.start_one(0)

    def ready(self):
        if self.joined:
            for copy in self.lefts + self.rights:
                copy.wait()

    def settle(self, out):
        self.sum.settle((out,))

    @staticmethod
    def scratch(name, count, model, columns, parts, left=True, right=True):
        own, dma = model // parts, pltpu.SemaphoreType.DMA
        found = {}
        if own % 128 == 0:
            slots, sems = JoinedSum.scratch([(model, columns)], parts)
            if left:
                found["left"] = pltpu.VMEM((count, model // 2), bf16)
                found |= {f"left_{end}": dma((parts // 2,)) for end in ("ss", "rs")}
            if right:
                found["right"] = pltpu.VMEM((count, columns), bf16)
                found |= {f"right_{end}": dma((1,)) for end in ("ss", "rs")}
        else:
            slots, sems = ScatterSum.scratch([(model, columns)], parts)
            found["whole"] = pltpu.VMEM((model, columns), bf16)
        found |= {str(i): s for i, s in enumerate(slots)}
        found |= {f"sem_{i}": s for i, s in enumerate(sems)}
        return {f"{name}_{part}": spec for part, spec in found.items()}


def back_kernel(*refs, names, parts, peers, scale):
    r = types.SimpleNamespace(**dict(zip(names, refs, strict=True)))
    count, width = r.q.shape
    span, model = r.pair.shape[1], r.cot.shape[1]
    per = r.tok.shape[2]
    half = parts // 2
    me = lax.axis_index("seq")
    x, z = lax.rem(me, 2), me // 2
    partner = me + 1 - 2 * x

    def at(o, c):
        return 2 * o + (x if c == 0 else 1 - x)

    held = Held(((r.q_all_hbm, r.q_all, r.q_sem), (r.rows_hbm, r.rows, r.rows_sem)), parts)
    held.ahead()
    greet(seq=parts, head=peers)

    def head_sum(name, source, full):
        return HeadSum(
            source,
            [getattr(r, f"{name}_{i}") for i in range(3)],
            [getattr(r, f"{name}_sem_{i}") for i in range(4)],
            full,
            [getattr(r, f"{name}_full_{i}") for i in range(2)],
        )

    sums = head_sum("sum", r.sum, r.branch)
    feeds = head_sum("feed", r.feed_in, r.layer)
    cot_other = getattr(r, "cot_other", None)
    normed_other = getattr(r, "normed_other", None)
    mixed_other = getattr(r, "mixed_other", None)
    p_down = Product(r, "down", r.cot, r.hidden, parts, "z", left_other=cot_other)
    p_up = Product(r, "up", r.normed_two, r.grad_upward, parts, "x")
    p_o = Product(r, "o", r.branch, r.mixed, parts, "x", right_other=mixed_other)
    p_kv = Product(r, "kv", r.normed, r.d_kv, parts, "x", left_other=normed_other)
    p_q = Product(r, "q", r.normed, r.d_q, parts, "x", left_other=normed_other)

    sums.start()
    p_down.begin()
    p_up.begin_left()
    p_up.begin()
    feeds.start()
    middle = r.middle[...]
    row_scale = lax.rsqrt(row_mean(middle * middle) + eps)
    hat = middle * row_scale
    sums.relay()
    grad_normed = sums.total()
    scaled = grad_normed * r.gain_two[...]
    grad_middle = r.cot[sums.mine, :].astype(f32) + row_scale * (
        scaled - hat * row_mean(scaled * hat)
    )
    sums.spread(grad_middle)
    r.grad_middle[...] = grad_middle
    r.small_send[8:16] = folded(col_sum(grad_normed * hat))
    feeds.relay()
    sums.forward()
    sums.settle()
    g_own = nt(r.branch[...], r.w_o[...]).astype(bf16)
    r.g_all[0, z] = g_own

    deltas = []
    for h in range(2):
        cols = head_cols(h)
        g = g_own[:, cols].astype(f32)
        r.small_send[19 + h : 20 + h] = col_sum(g * (r.recalled[:, cols] - r.local[:, cols]))
        both = jnp.sum(g * r.recalled[:, cols], axis=1, keepdims=True)
        deltas.append(both * r.gate[h])
    turned = row_form([jnp.zeros_like(deltas[0])] * 2 + deltas, count).T[0:8]
    row = lax.broadcasted_iota(jnp.int32, (8, count), 0)
    r.st_all[0, z] = jnp.where(row < 2, r.logs[...], turned)

    def ask(c, o, way, peer):
        return (
            send(
                r.st_all.at[0, o], r.st_all.at[c, o], r.st_ss.at[way, o], r.st_rs.at[c, o], "seq", peer
            ),
            send(r.g_all.at[0, o], r.g_all.at[c, o], r.g_ss.at[way, o], r.g_rs.at[c, o], "seq", peer),
        )

    def start(copies):
        for copy in copies:
            copy.start()

    def up(o):
        return ask(0, o, 0, me + 2)

    def down(o):
        return ask(0, o, 1, me - 2)

    def across(o):
        return ask(1, o, 2, partner)

    def arrived(c, o):
        for copy in ask(c, o, 2, partner):
            copy.wait_recv()

    def sent(copies):
        for copy in copies:
            copy.wait_send()

    @pl.when(z < half - 1)
    def _():
        start(up(z))

    @pl.when(z > 0)
    def _():
        start(down(z))

    start(across(z))
    p_down.ready()
    p_down.pair(True)

    dq = []
    for h in range(2):
        cols = head_cols(h)
        rest = 1.0 - r.gate[h]
        g = r.g_all[0, z, :, cols]
        p = r.p[h]
        e = nt(g, r.pair[1, :, cols])
        delta = jnp.sum(p * e, axis=1, keepdims=True)
        ds = (p * ((e - delta) * rest)).astype(bf16)
        r.dq_sum[:, cols] = nn(ds, r.pair[0, :, cols]) * scale
        dk = tn(ds, r.q[:, cols]) * scale
        dv = tn(p.astype(bf16), g) * rest
        r.pair_sum[0, :, cols] = dk[W:]
        r.pair_sum[1, :, cols] = dv[W:]
        r.pair_send[0, :, cols] = dk[:W].astype(bf16)
        r.pair_send[1, :, cols] = dv[:W].astype(bf16)
        low = ds.astype(f32)
        acc = low[0:8]
        for a in range(1, count // 8):
            acc = acc + pltpu.roll(low[8 * a : 8 * a + 8], (span - 8 * a) % span, 1)
        line = acc[0:1]
        for b in range(1, 8):
            line = line + pltpu.roll(acc[b : b + 1], span - b, 1)
        lines = span // 128
        for i in range(lines):
            r.small_send[24 + h * lines + i : 25 + h * lines + i] = line[:, 128 * i : 128 * i + 128]

    halo_x = send(
        r.pair_send.at[:, pl.ds(count, count)], r.halo_x, r.halo_ss.at[0], r.halo_rs.at[0], "seq", partner
    )
    halo_z = send(r.halo_send, r.halo_z, r.halo_ss.at[1], r.halo_rs.at[1], "seq", me - 2)
    halo_x.start()

    ids = lax.broadcasted_iota(jnp.int32, (count, per), 0)

    def owner_part(c, o):
        j = at(o, c)
        q_at, rows_at = held.get(j)
        stats = r.st_all[c, o].T
        found = []
        for h in range(2):
            cols = head_cols(h)
            keep = r.tok[j, h : h + 1, :] == ids
            s = nt(q_at[:, cols], rows_at[h, :, 0:128]) * scale
            p = jnp.exp(jnp.where(keep, s - stats[:, h : h + 1], NEG))
            e = nt(r.g_all[c, o, :, cols], rows_at[h, :, 128:256]) * r.gate[h]
            ds = (p * (e - stats[:, 2 + h : 3 + h])).astype(bf16)
            found.append(nn(ds, rows_at[h, :, 0:128]) * scale)
        return found

    own = owner_part(0, z)
    for h in range(2):
        r.dq_sum[:, head_cols(h)] += own[h]

    halo_x.wait()
    passing = x.astype(f32)
    r.halo_send[...] = (
        r.pair_send[:, :count].astype(f32) + r.halo_x[...].astype(f32) * passing
    ).astype(bf16)
    r.pair_sum[...] += r.halo_x[...].astype(f32) * (1.0 - passing)

    @pl.when(z > 0)
    def _():
        halo_z.start()

    def give_x(o):
        return send(r.dq_xs.at[o], r.dq_xr.at[o], r.dx_ss.at[o], r.dx_rs.at[o], "seq", partner)

    def give_z(o):
        return send(r.dq_zs.at[o], r.dq_zr.at[z], r.dz_ss.at[o], r.dz_rs.at[z], "seq", at(o, 0))

    def got_z(o):
        return send(r.dq_zs.at[o], r.dq_zr.at[o], r.dz_ss.at[o], r.dz_rs.at[o], "seq", partner)

    def neighbour(o):
        arrived(1, o)
        found = owner_part(1, o)
        for h in range(2):
            r.dq_xs[o, h] = found[h].astype(bf16)
        give_x(o).start()

    def column(o):
        found = owner_part(0, o)
        for h in range(2):
            r.dq_zs[o, h] = found[h].astype(bf16)

    def near(body):
        def step(t, carry):
            @pl.when(z - t >= 0)
            def _():
                body(z - t, True)

            @pl.when(z + t < half)
            def _():
                body(z + t, False)

            return carry

        lax.fori_loop(1, half, step, 0)

    neighbour(z)

    def relay(o, below):
        arrived(0, o)
        start(across(o))
        if below:

            @pl.when(z < half - 1)
            def _():
                start(up(o))

        else:

            @pl.when(z > 0)
            def _():
                start(down(o))

    def relay_step(t, carry):
        @pl.when(z - t >= 0)
        def _():
            relay(z - t, True)

        @pl.when(z + t < half)
        def _():
            relay(z + t, False)

        @pl.when(z - t >= 0)
        def _():
            column(z - t)

        @pl.when(z + t < half)
        def _():
            column(z + t)

        return carry

    lax.fori_loop(1, half, relay_step, 0)
    p_up.ready()
    p_up.pair(True)
    feed_sum = feeds.total()
    layer = r.middle[...] + feed_sum
    feeds.spread(layer)
    r.small_send[16:17] = fold_sum(col_sum(layer * layer))
    r.small_send[17:18] = fold_sum(r.attn_line[...])
    r.small_send[18:19] = fold_sum(col_sum(feed_sum * feed_sum))
    near(lambda o, below: neighbour(o))
    p_down.pair(False)
    p_o.begin_left()
    p_o.begin()
    p_up.pair(False)

    @pl.when(z > 0)
    def _():
        halo_z.wait_send()

    @pl.when(z < half - 1)
    def _():
        send(r.halo_send, r.halo_z, r.halo_ss.at[1], r.halo_rs.at[1], "seq", partner).wait_recv()
        r.pair_sum[...] += r.halo_z[...].astype(f32)

    def join(o, below):
        give_x(o).wait()
        for h in range(2):
            both = r.dq_zs[o, h].astype(f32) + r.dq_xr[o, h].astype(f32)
            r.dq_zs[o, h] = both.astype(bf16)
        give_z(o).start()

    near(join)
    r.d_kv[:, :width] = r.pair_sum[0].astype(bf16)
    r.d_kv[:, width:] = r.pair_sum[1].astype(bf16)
    p_kv.begin()
    feeds.forward()
    p_down.far()
    p_up.far()
    give_x(z).wait()
    for h in range(2):
        r.dq_sum[:, head_cols(h)] += r.dq_xr[z, h].astype(f32)

    def merge(o, below):
        got_z(o).wait_recv()
        for h in range(2):
            r.dq_sum[:, head_cols(h)] += r.dq_zr[o, h].astype(f32)

    near(merge)

    r.d_q[...] = r.dq_sum[...].astype(bf16)
    p_q.begin()
    for b in range(model // 256):
        block = slice(256 * b, 256 * b + 256)
        r.back[:, block] = (
            nt(r.d_q[...], r.w_q[block, :])
            + nt(r.d_kv[:, :width], r.w_k[block, :])
            + nt(r.d_kv[:, width:], r.w_v[block, :])
        ).astype(bf16)
    backs = head_sum("back", r.back, r.input_grad)
    backs.start()
    backs.relay()
    p_o.ready()
    p_o.pair(True)
    p_kv.ready()
    p_kv.pair(True)
    tokens = r.inputs[backs.mine, :].astype(f32)
    in_scale = lax.rsqrt(row_mean(tokens * tokens) + eps)
    in_hat = tokens * in_scale
    back_sum = backs.total()
    g = back_sum * r.gain_one[...]
    backs.spread(r.grad_middle[...] + in_scale * (g - in_hat * row_mean(g * in_hat)))
    r.small_send[0:8] = folded(col_sum(back_sum * in_hat))
    r.small_send[21:24] = jnp.zeros((3, 128), f32)
    r.small_send[36:40] = jnp.zeros((4, 128), f32)

    def small_heads(d):
        peer = lax.rem(lax.axis_index("head") + d, peers)
        return send(r.small_send, r.small_head.at[d], r.sh_ss.at[d], r.sh_rs.at[d], "head", peer)

    for d in range(1, peers):
        small_heads(d).start()
    p_q.ready()
    p_q.pair(True)
    backs.forward()
    p_o.far()
    p_kv.far()

    kept = lax.broadcasted_iota(jnp.int32, r.small_send.shape, 0) < 19
    found = r.small_send[...]
    for d in range(1, peers):
        small_heads(d).wait()
        found = found + jnp.where(kept, r.small_head[d], 0.0)
    r.small_seq[0] = found

    def small_seqs(d):
        peer = lax.rem(me + d, parts)
        return send(r.small_seq.at[0], r.small_seq.at[d], r.sq_ss.at[d], r.sq_rs.at[d], "seq", peer)

    def small_start(d, carry):
        small_seqs(d).start()
        return carry

    lax.fori_loop(1, parts, small_start, 0)
    p_o.pair(False)
    p_kv.pair(False)
    p_q.far()
    p_q.pair(False)
    p_down.settle(r.down_sum)
    r.down_out[...] = r.down_sum[...].T
    p_up.settle(r.up_out)
    p_o.settle(r.o_sum)
    p_kv.settle(r.kv_sum)
    r.k_out[...] = r.kv_sum[:, :width]
    r.v_out[...] = r.kv_sum[:, width:]
    r.o_out[...] = r.o_sum[...].T
    p_q.settle(r.q_out)
    r.small[...] = r.small_seq[0]

    def small_add(d, carry):
        small_seqs(d).wait()
        r.small[...] += r.small_seq[d]
        return carry

    lax.fori_loop(1, parts, small_add, 0)
    feeds.settle()
    backs.settle()

    sent(across(z))

    @pl.when(z < half - 1)
    def _():
        sent(up(z))

    @pl.when(z > 0)
    def _():
        sent(down(z))

    def drain(o, below):
        sent(across(o))
        give_z(o).wait_send()
        if below:

            @pl.when(z < half - 1)
            def _():
                sent(up(o))

        else:

            @pl.when(z > 0)
            def _():
                sent(down(o))

    near(drain)


def back(inputs, parts, peers):
    count, width = inputs["q"].shape
    model, span = inputs["cot"].shape[1], W + count
    half, own = parts // 2, model // parts
    smem = pl.BlockSpec(memory_space=pltpu.SMEM)
    vmem = pl.BlockSpec(memory_space=pltpu.VMEM)
    hbm = pl.BlockSpec(memory_space=pltpu.HBM)
    dma = pltpu.SemaphoreType.DMA
    wide = inputs["hidden"].shape[1]
    outputs = dict(
        input_grad=((count, model), bf16),
        layer=((count, model), bf16),
        q_out=((own, width), f32),
        k_out=((own, width), f32),
        v_out=((own, width), f32),
        o_out=((width, own), f32),
        up_out=((own, wide), f32),
        down_out=((wide, own), f32),
        small=((40, 128), f32),
    )
    outputs = {name: jax.ShapeDtypeStruct(*spec) for name, spec in outputs.items()}
    held = Held.scratch((inputs["q_all_hbm"], inputs["rows_hbm"]), parts)
    scratch = dict(zip(("q_all", "rows", "q_sem", "rows_sem"), held, strict=True))
    for name, spec in dict(
        branch=((count, model), bf16),
        back=((count, model), bf16),
        grad_middle=((count // peers, model), f32),
        g_all=((2, half, count, width), bf16),
        st_all=((2, half, 8, count), f32),
        dq_xs=((half, 2, count, 128), bf16),
        dq_xr=((half, 2, count, 128), bf16),
        dq_zs=((half, 2, count, 128), bf16),
        dq_zr=((half, 2, count, 128), bf16),
        pair_send=((2, W, width), bf16),
        pair_sum=((2, count, width), f32),
        halo_x=((2, count, width), bf16),
        halo_send=((2, count, width), bf16),
        halo_z=((2, count, width), bf16),
        dq_sum=((count, width), f32),
        d_kv=((count, 2 * width), bf16),
        d_q=((count, width), bf16),
        kv_sum=((own, 2 * width), f32),
        o_sum=((own, width), f32),
        down_sum=((own, wide), f32),
        small_send=((40, 128), f32),
        small_head=((peers, 40, 128), f32),
        small_seq=((parts, 40, 128), f32),
    ).items():
        scratch[name] = pltpu.VMEM(*spec)
    for name, shape in dict(
        st_ss=(3, half),
        st_rs=(2, half),
        g_ss=(3, half),
        g_rs=(2, half),
        dx_ss=(half,),
        dx_rs=(half,),
        dz_ss=(half,),
        dz_rs=(half,),
        halo_ss=(2,),
        halo_rs=(2,),
        sh_ss=(peers,),
        sh_rs=(peers,),
        sq_ss=(parts,),
        sq_rs=(parts,),
    ).items():
        scratch[name] = dma(shape)
    for name in ("sum", "feed", "back"):
        scratch |= {f"{name}_{i}": s for i, s in enumerate(HeadSum.scratch(count, model))}
        scratch |= {f"{name}_sem_{i}": s for i, s in enumerate(HeadSum.sems())}
        scratch |= {f"{name}_full_{i}": s for i, s in enumerate(HeadSum.full_scratch())}
    for name, columns, left, right in (
        ("down", wide, False, True),
        ("up", wide, True, True),
        ("o", width, True, False),
        ("kv", 2 * width, False, True),
        ("q", width, False, True),
    ):
        scratch |= Product.scratch(name, count, model, columns, parts, left, right)
    spaces = dict(gate=smem, q_all_hbm=hbm, rows_hbm=hbm)
    found = pl.pallas_call(
        functools.partial(
            back_kernel,
            names=(*inputs, *outputs, *scratch),
            parts=parts,
            peers=peers,
            scale=128**-0.5,
        ),
        out_shape=tuple(outputs.values()),
        in_specs=[spaces.get(name, vmem) for name in inputs],
        out_specs=(vmem,) * len(outputs),
        scratch_shapes=list(scratch.values()),
        compiler_params=pltpu.CompilerParams(
            vmem_limit_bytes=(40 if parts <= 8 else 62) * MIB, collective_id=2, has_side_effects=True
        ),
        cost_estimate=pl.CostEstimate(
            flops=4 * 10**9, bytes_accessed=150 * MIB, transcendentals=5 * 10**6
        ),
        name="back",
    )(*inputs.values())
    return dict(zip(outputs, found, strict=True))


def norm_stats(values):
    row_scale = lax.rsqrt(jnp.mean(values * values, axis=-1, keepdims=True) + eps)
    return (values * row_scale, row_scale)


def per_device(
    inputs,
    cotangent,
    query_weight,
    key_weight,
    value_weight,
    output_weight,
    up_weight,
    down_weight,
    first_gain,
    second_gain,
    position_bias,
    gate_bias,
    memory_table,
    retrieved,
    lengths,
):
    _, block_len, model_width = inputs.shape
    bucket_total = position_bias.shape[1]
    seq_count = lax.axis_size("seq")
    slot_count = memory_table.shape[0]

    wanted = jnp.transpose(retrieved[0], (1, 0, 2))
    token = jnp.arange(block_len, dtype=jnp.int32)[None, :, None]
    codes = (wanted // slot_count) * (block_len * slot_count) + token * slot_count + wanted % slot_count
    codes = lax.sort(codes.reshape(2, -1), dimension=1, is_stable=False)
    places, tok = request(codes, seq_count, slot_count, block_len)
    rows = gather_rows(places, widen(memory_table))

    hot, outside = diagonal_buckets(block_len, bucket_total)
    bias_row = jnp.dot(position_bias, hot, precision=highest) + outside[None]

    x, cot = inputs[0], cotangent[0]
    peers = lax.axis_size("head")
    gain_one, gain_two = first_gain[None], second_gain[None]
    gate_flat = jax.nn.sigmoid(gate_bias)
    hat_one, _ = norm_stats(x.astype(f32))
    normed_one = (hat_one * first_gain).astype(bf16)
    queries = nn(normed_one, query_weight).astype(bf16)
    keys = nn(normed_one, key_weight).astype(bf16)
    values = nn(normed_one, value_weight).astype(bf16)
    q_all = lax.all_gather(queries, "seq", axis=0)

    mixed, recalled, local_out, logs, window_weights, pair = attend(
        lengths[0], gate_flat, queries, keys, values, bias_row, q_all, tok, rows
    )

    closed = close_attn(
        dict(
            sum=nn(mixed, output_weight).astype(bf16),
            inputs=x,
            gain=gain_two,
            cot=cot,
            normed=normed_one,
            mixed=mixed,
        ),
        seq_count,
    )
    normed_two, middle, attn_line = closed.pop("full"), closed.pop("middle"), closed.pop("line")
    others = closed
    upward = nn(normed_two, up_weight)
    gelu_value, gelu_back = jax.vjp(jax.nn.gelu, upward)
    hidden = gelu_value.astype(bf16)
    grad_upward = gelu_back(nt(cot, down_weight))[0].astype(bf16)
    done = back(
        dict(
            gate=gate_flat,
            sum=nt(grad_upward, up_weight).astype(bf16),
            feed_in=nn(hidden, down_weight).astype(bf16),
            hidden=hidden,
            grad_upward=grad_upward,
            normed_two=normed_two,
            **others,
            cot=cot,
            inputs=x,
            gain_one=gain_one,
            gain_two=gain_two,
            middle=middle,
            attn_line=attn_line,
            w_o=output_weight,
            w_q=query_weight,
            w_k=key_weight,
            w_v=value_weight,
            normed=normed_one,
            mixed=mixed,
            q=queries,
            recalled=recalled,
            local=local_out,
            logs=logs,
            p=window_weights,
            pair=pair,
            tok=tok,
            q_all_hbm=q_all,
            rows_hbm=rows,
        ),
        seq_count,
        peers,
    )
    small = done["small"]
    entry_count = float(block_len * model_width * seq_count)
    share = model_width // seq_count
    gains = small[:16].reshape(2, model_width)
    own_gains = lax.dynamic_slice_in_dim(gains, lax.axis_index("seq") * share, share, 1)
    position_grad = jnp.dot(small[24:36].reshape(2, -1), hot.T, precision=highest)
    gate_grad = jnp.sum(small[19:21], axis=1) * gate_flat * (1.0 - gate_flat)
    return (
        done["layer"][None],
        done["input_grad"].astype(f32)[None],
        done["q_out"],
        done["k_out"],
        done["v_out"],
        done["o_out"],
        done["up_out"],
        done["down_out"],
        own_gains[0],
        own_gains[1],
        position_grad,
        gate_grad,
        jnp.sqrt(jnp.sum(small[16:19], axis=1) / entry_count),
    )


def solution(mesh):
    in_specs = (
        P(None, "seq", None),
        P(None, "seq", None),
        P(None, "head"),
        P(None, "head"),
        P(None, "head"),
        P("head", None),
        P(None, "head"),
        P("head", None),
        P(),
        P(),
        P("head", None),
        P("head"),
        P("seq", "head", None),
        P(None, "seq", "head", None),
        P(),
    )
    out_specs = (
        P(None, "seq", None),
        P(None, "seq", None),
        P("seq", "head"),
        P("seq", "head"),
        P("seq", "head"),
        P("head", "seq"),
        P("seq", "head"),
        P("head", "seq"),
        P("seq"),
        P("seq"),
        P("head", None),
        P("head"),
        P(),
    )
    return jax.shard_map(
        per_device, mesh=mesh, in_specs=in_specs, out_specs=out_specs, check_vma=False
    )
```

```python
import functools
import math
import types

import jax
import jax.numpy as jnp
import numpy as np
from jax import lax
from jax.experimental import pallas as pl
from jax.experimental.pallas import tpu as pltpu
from jax.sharding import PartitionSpec as P

W = 512
eps = 1e-06
exact_span = 16
far_distance = 128
highest = lax.Precision.HIGHEST
f32 = jnp.float32
bf16 = jnp.bfloat16
NEG = -1e30
MIB = 2**20


def bucket_table(key_span, bucket_total):
    found = []
    for distance in range(key_span):
        if distance < exact_span:
            found.append(distance)
        else:
            scaled = math.log(distance / exact_span) / math.log(far_distance / exact_span)
            found.append(
                min(bucket_total - 1, exact_span + math.floor(scaled * (bucket_total - exact_span)))
            )
    return np.asarray(found)


def diagonal_buckets(block_len, bucket_total):
    span = W + block_len
    table = bucket_table(W, bucket_total)
    hot = np.zeros((bucket_total, span), np.float32)
    for u in range(1, W + 1):
        hot[table[W - u], u] = 1.0
    outside = np.where(hot.sum(0) > 0, 0.0, NEG).astype(np.float32)
    return hot, outside


def nt(a, b):
    return lax.dot_general(a, b, (((1,), (1,)), ((), ())), preferred_element_type=f32)


def nn(a, b):
    return lax.dot_general(a, b, (((1,), (0,)), ((), ())), preferred_element_type=f32)


def tn(a, b):
    return lax.dot_general(a, b, (((0,), (0,)), ((), ())), preferred_element_type=f32)


def widen_kernel(table_hbm, wide_hbm, buf, out, sem, out_sem, *, chunk, part):
    chunks = table_hbm.shape[0] // chunk

    def fetch(i):
        return pltpu.make_async_copy(
            table_hbm.at[pl.ds(i * chunk, chunk)], buf.at[i % 2], sem.at[i % 2]
        )

    def store(i):
        return pltpu.make_async_copy(
            out.at[i % 2], wide_hbm.at[:, pl.ds(2 * i * chunk, 2 * chunk)], out_sem.at[i % 2]
        )

    fetch(0).start()
    for i in range(chunks):
        fetch(i).wait()
        if i + 1 < chunks:
            fetch(i + 1).start()
        if i > 1:
            store(i - 2).wait()

        def widen(q, carry, i=i):
            x = buf[i % 2, pl.ds(q * part, part)].astype(f32)
            for r in range(part):
                for h in range(2):
                    place = pl.ds(2 * (q * part + r), 1)
                    out[i % 2, h, place, :] = x[r, h : h + 1, 0:128]
                    place = pl.ds(2 * (q * part + r) + 1, 1)
                    out[i % 2, h, place, :] = x[r, h : h + 1, 128:256]
            return carry

        lax.fori_loop(0, chunk // part, widen, 0)
        store(i).start()
    for i in range(max(0, chunks - 2), chunks):
        store(i).wait()


def widen(table):
    total = table.shape[0]
    chunk = min(1024, total)
    hbm = pl.BlockSpec(memory_space=pltpu.HBM)
    dma = pltpu.SemaphoreType.DMA
    return pl.pallas_call(
        functools.partial(widen_kernel, chunk=chunk, part=32),
        out_shape=jax.ShapeDtypeStruct((2, 2 * total, 128), f32),
        in_specs=[hbm],
        out_specs=hbm,
        scratch_shapes=[
            pltpu.VMEM((2, chunk, 2, 256), bf16),
            pltpu.VMEM((2, 2, 2 * chunk, 128), f32),
            dma((2,)),
            dma((2,)),
        ],
        compiler_params=pltpu.CompilerParams(vmem_limit_bytes=58 * MIB),
        cost_estimate=pl.CostEstimate(flops=0, bytes_accessed=40 * MIB, transcendentals=0),
        name="widen",
    )(table)


def gather_kernel(at_ref, wide_hbm, out_hbm, wide, buf, low, wide_sem, out_sem, *, unroll, group):
    parts, rows = out_hbm.shape[0], out_hbm.shape[2]

    def fetch(h):
        return pltpu.make_async_copy(wide_hbm.at[h], wide.at[h], wide_sem.at[h])

    def store(j, h, slot):
        return pltpu.make_async_copy(low.at[slot], out_hbm.at[j, h], out_sem.at[slot])

    for h in range(2):
        fetch(h).start()
    for h in range(2):
        fetch(h).wait()

        def one(j, carry, h=h):
            slot = lax.rem(j, 2)
            first = (2 * j + h) * rows

            def copy_rows(q, carry):
                base = q * unroll
                for g in range(0, unroll, group):
                    found = [
                        wide[h, pl.ds(at_ref[first + base + g + u], 2), :] for u in range(group)
                    ]
                    for u in range(group):
                        buf[pl.ds(2 * (base + g + u), 2), :] = found[u]
                return carry

            lax.fori_loop(0, rows // unroll, copy_rows, 0)

            if h == 0:

                @pl.when(j > 1)
                def _():
                    store(j, h, slot).wait()

            else:
                store(j, h, slot).wait()

            low[slot, :, 0:128] = buf[pl.ds(0, rows, 2), :].astype(bf16)
            low[slot, :, 128:256] = buf[pl.ds(1, rows, 2), :].astype(bf16)
            store(j, h, slot).start()
            return carry

        lax.fori_loop(0, parts, one, 0)
    store(0, 1, 0).wait()
    store(1, 1, 1).wait()


def gather_rows(places, wide):
    parts, heads, rows = places.shape
    unroll = min(64, rows)
    hbm = pl.BlockSpec(memory_space=pltpu.HBM)
    dma = pltpu.SemaphoreType.DMA
    return pl.pallas_call(
        functools.partial(gather_kernel, unroll=unroll, group=unroll // 2),
        out_shape=jax.ShapeDtypeStruct((parts, heads, rows, 256), bf16),
        in_specs=[pl.BlockSpec(memory_space=pltpu.SMEM), hbm],
        out_specs=hbm,
        scratch_shapes=[
            pltpu.VMEM(wide.shape, f32),
            pltpu.VMEM((2 * rows, 128), f32),
            pltpu.VMEM((2, rows, 256), bf16),
            dma((2,)),
            dma((2,)),
        ],
        compiler_params=pltpu.CompilerParams(vmem_limit_bytes=58 * MIB),
        cost_estimate=pl.CostEstimate(flops=0, bytes_accessed=100 * MIB, transcendentals=0),
        name="gather_rows",
    )(places.reshape(-1), wide)


MESH = pl.DeviceIdType.MESH


def greet(**counts):
    barrier = pltpu.get_barrier_semaphore()
    for axis, count in counts.items():
        me = lax.axis_index(axis)

        def call(d, carry, axis=axis, count=count, me=me):
            peer = lax.rem(me + d, count)
            pl.semaphore_signal(barrier, inc=1, device_id={axis: peer}, device_id_type=MESH)
            return carry

        lax.fori_loop(1, count, call, 0)
    pl.semaphore_wait(barrier, sum(counts.values()) - len(counts))


def send(src, dst, send_sem, recv_sem, axis, peer):
    return pltpu.make_async_remote_copy(
        src_ref=src,
        dst_ref=dst,
        send_sem=send_sem,
        recv_sem=recv_sem,
        device_id={axis: peer},
        device_id_type=MESH,
    )


def doc_starts(lengths_ref, first, count):
    place = first + lax.broadcasted_iota(jnp.int32, (count, 1), 0)
    start = jnp.zeros((count, 1), jnp.int32)
    end = jnp.int32(0)
    for c in range(lengths_ref.shape[0]):
        end = end + lengths_ref[c]
        start = jnp.where(end <= place, end, start)
    return start


def head_cols(h):
    return slice(h * 128, h * 128 + 128)


def row_form(columns, count):
    lane = lax.broadcasted_iota(jnp.int32, (count, 128), 1)
    wide = jnp.zeros((count, 128), f32)
    for i, column in enumerate(columns):
        wide = jnp.where(lane == i, column, wide)
    return wide


def request_kernel(codes_ref, place_ref, tok_ref, got, own_sem, ss, rs, *, parts, slots, tokens):
    rows = codes_ref.shape[1] // parts
    me = lax.axis_index("seq")

    def part(owner):
        return codes_ref.at[:, pl.ds(pl.multiple_of(owner * rows, 128), rows)]

    keep = pltpu.make_async_copy(part(me), got.at[0], own_sem)
    keep.start()
    greet(seq=parts)

    def ask(d):
        peer = lax.rem(me + d, parts)
        return send(part(peer), got.at[d], ss.at[d], rs.at[d], "seq", peer)

    def start(d, carry):
        ask(d).start()
        return carry

    lax.fori_loop(1, parts, start, 0)
    shift = slots.bit_length() - 1

    def read(d, j):
        code = got[d]
        place_ref[j] = (code & (slots - 1)) * 2
        tok_ref[j] = (code >> shift) & (tokens - 1)

    keep.wait()
    read(0, me)

    def arrive(d, carry):
        ask(d).wait()
        read(d, lax.rem(me + parts - d, parts))
        return carry

    lax.fori_loop(1, parts, arrive, 0)


def request(codes, parts, slots, tokens):
    rows = codes.shape[1] // parts
    vmem = pl.BlockSpec(memory_space=pltpu.VMEM)
    dma = pltpu.SemaphoreType.DMA
    shape = (parts, 2, rows)
    return pl.pallas_call(
        functools.partial(request_kernel, parts=parts, slots=slots, tokens=tokens),
        out_shape=(jax.ShapeDtypeStruct(shape, jnp.int32),) * 2,
        in_specs=[vmem],
        out_specs=(vmem,) * 2,
        scratch_shapes=[pltpu.VMEM(shape, jnp.int32), dma, dma((parts,)), dma((parts,))],
        compiler_params=pltpu.CompilerParams(
            vmem_limit_bytes=8 * MIB, collective_id=6, has_side_effects=True
        ),
        name="request",
    )(codes)


class HeadSum:
    def __init__(self, src, scratch, sems, full=None, full_sems=None):
        self.src, self.full = src, full
        self.core_recv, self.side_send, self.side_recv = scratch
        self.core_ss, self.core_rs, self.side_ss, self.side_rs = sems
        self.full_sems = full_sems
        head = lax.axis_index("head")
        self.y, self.c = head // 2, lax.rem(head, 2)
        self.share = src.shape[0] // 4
        self.core = 2 * self.y + 1 - self.c
        self.side = 2 * (1 - self.y) + self.c
        self.mine = self.rows_of(head)

    def rows_of(self, place):
        return pl.ds(pl.multiple_of(place * self.share, self.share), self.share)

    def to_core(self, i):
        y = self.y if i == 0 else 1 - self.y
        src = self.src.at[self.rows_of(2 * y + 1 - self.c)]
        return send(src, self.core_recv.at[i], self.core_ss.at[i], self.core_rs.at[i], "head", self.core)

    def to_side(self):
        return send(self.side_send, self.side_recv, self.side_ss, self.side_rs, "head", self.side)

    def start(self):
        self.to_core(1).start()
        self.to_core(0).start()

    def relay(self):
        self.to_core(1).wait()
        other = self.src[self.rows_of(self.side), :].astype(f32)
        self.side_send[...] = (other + self.core_recv[1].astype(f32)).astype(bf16)
        self.to_side().start()

    def total(self):
        self.to_core(0).wait()
        found = self.src[self.mine, :].astype(f32) + self.core_recv[0].astype(f32)
        self.to_side().wait()
        return found + self.side_recv[...].astype(f32)

    def back(self, i):
        rows = self.rows_of(self.side) if i == 2 else self.mine
        peer = self.side if i == 1 else self.core
        ss, rs = self.full_sems
        return send(self.full.at[rows], self.full.at[rows], ss.at[i], rs.at[i], "head", peer)

    def spread(self, value):
        self.full[self.mine, :] = value.astype(self.full.dtype)
        self.back(1).start()
        self.back(0).start()

    def forward(self):
        self.back(1).wait()
        self.back(2).start()

    def settle(self):
        self.back(0).wait()
        self.back(2).wait()

    @staticmethod
    def scratch(count, width):
        piece = (count // 4, width)
        return [pltpu.VMEM((2,) + piece, bf16), pltpu.VMEM(piece, bf16), pltpu.VMEM(piece, bf16)]

    @staticmethod
    def sems():
        dma = pltpu.SemaphoreType.DMA
        return [dma((2,)), dma((2,)), dma, dma]

    @staticmethod
    def full_scratch():
        return [pltpu.SemaphoreType.DMA((3,))] * 2


class Held:
    def __init__(self, arrays, parts):
        self.arrays, self.parts = arrays, parts
        self.all = arrays[0][1].shape[0] == parts

    def fetch(self, i, j):
        hbm, place, sem = self.arrays[i]
        slot = j if self.all else 0
        return pltpu.make_async_copy(hbm.at[j], place.at[slot], sem.at[slot])

    def ahead(self):
        if self.all:

            def start(j, carry):
                for i in range(len(self.arrays)):
                    self.fetch(i, j).start()
                return carry

            lax.fori_loop(0, self.parts, start, 0)

    def get(self, j, again=False):
        for i in range(len(self.arrays)):
            if not self.all:
                self.fetch(i, j).start()
            if not (self.all and again):
                self.fetch(i, j).wait()
        return [place.at[j if self.all else 0] for _, place, _ in self.arrays]

    @staticmethod
    def scratch(arrays, parts):
        slots = parts if parts <= 8 else 1
        places = [pltpu.VMEM((slots,) + a.shape[1:], a.dtype) for a in arrays]
        return places + [pltpu.SemaphoreType.DMA((slots,))] * len(arrays)


class ScatterSum:
    def __init__(self, grads, sems, parts):
        self.grads, self.sems = grads, sems
        self.quarter = parts // 4
        self.own = grads[0][0].shape[0] // parts
        me = lax.axis_index("seq")
        self.x, self.b, self.a = lax.rem(me, 2), lax.rem(me // 2, 2), me // 4

    def place(self, da, side, x):
        b = self.b if side == 1 else 1 - self.b
        return 4 * lax.rem(self.a + da, self.quarter) + 2 * b + x

    def rows_of(self, place):
        return pl.ds(pl.multiple_of(place * self.own, self.own), self.own)

    def send_x(self, k, da, side):
        ss, rs = self.sems[0:2]
        return send(
            self.grads[k][0].at[self.rows_of(self.place(da, side, 1 - self.x))],
            self.grads[k][1].at[side, da],
            ss.at[k, side, da],
            rs.at[k, side, da],
            "seq",
            self.place(0, 1, 1 - self.x),
        )

    def send_pair(self, k, da):
        ss, rs = self.sems[2:4]
        grads, peer = self.grads[k], self.place(0, 0, self.x)
        return send(grads[2].at[da], grads[3].at[da], ss.at[k, da], rs.at[k, da], "seq", peer)

    def send_far(self, k, da):
        ss, rs = self.sems[4:6]
        grads, peer = self.grads[k], self.place(da, 1, self.x)
        return send(grads[4].at[da], grads[5].at[da], ss.at[k, da], rs.at[k, da], "seq", peer)

    def loop(self, first, last, step):
        def body(da, carry):
            for k in range(len(self.grads)):
                step(k, da)
            return carry

        lax.fori_loop(first, last, body, 0)

    def span(self, far):
        return (1, self.quarter) if far else (0, 1)

    def start(self, far, side):
        self.loop(*self.span(far), lambda k, da: self.send_x(k, da, side).start())

    def start_one(self, k):
        for far in (True, False):
            for side in range(2):

                def body(da, carry, side=side):
                    self.send_x(k, da, side).start()
                    return carry

                lax.fori_loop(*self.span(far), body, 0)

    def column(self, k, da, side):
        self.send_x(k, da, side).wait()
        mine = self.grads[k][0][self.rows_of(self.place(da, side, self.x)), :]
        return mine.astype(f32) + self.grads[k][1][side, da].astype(f32)

    def pair(self, far):
        def step(k, da):
            self.grads[k][2][da] = self.column(k, da, 0).astype(bf16)
            self.send_pair(k, da).start()

        self.loop(*self.span(far), step)

    def both(self, k, da):
        found = self.column(k, da, 1)
        self.send_pair(k, da).wait()
        return found + self.grads[k][3][da].astype(f32)

    def far(self):
        def step(k, da):
            self.grads[k][4][da] = self.both(k, da).astype(bf16)
            self.send_far(k, da).start()

        self.loop(*self.span(True), step)

    def settle(self, outs):
        for k, out in enumerate(outs):
            out[...] = self.both(k, 0)

        def step(k, da):
            self.send_far(k, da).wait()
            outs[k][...] += self.grads[k][5][da].astype(f32)

        self.loop(*self.span(True), step)

    @staticmethod
    def scratch(shapes, parts):
        quarter = parts // 4
        slots = []
        for rows, columns in shapes:
            piece = (rows // parts, columns)
            slots.append(pltpu.VMEM((2, quarter) + piece, bf16))
            slots += [pltpu.VMEM((quarter,) + piece, bf16)] * 4
        dma = pltpu.SemaphoreType.DMA
        count = len(shapes)
        return slots, [dma((count, 2, quarter))] * 2 + [dma((count, quarter))] * 4


def row_mean(x):
    return jnp.mean(x, axis=1, keepdims=True)


def col_sum(x):
    return jnp.sum(x, axis=0, keepdims=True)


def folded(line):
    return jnp.concatenate([line[:, 128 * i : 128 * i + 128] for i in range(8)], axis=0)


def fold_sum(line):
    return col_sum(folded(line))


class JoinedSum(ScatterSum):
    def __init__(self, grads, sems, parts, first):
        super().__init__([(g[0], *g[4:]) for g in grads], sems, parts)
        self.own = grads[0][0].shape[1] // parts
        self.operands = [g[0:4] for g in grads]
        self.first = first

    def side_of(self, first, second):
        return 2 * first + second if self.first == "z" else 2 * second + first

    def mine(self):
        return (self.b, self.x) if self.first == "z" else (self.x, self.b)

    def place(self, da, side, flip=0):
        first, second = self.mine()
        first = 1 - first if flip else first
        second = second if side == 1 else 1 - second
        return 4 * lax.rem(self.a + da, self.quarter) + self.side_of(first, second)

    def partner(self):
        return self.place(0, 1, 1)

    def columns(self, place):
        return pl.ds(pl.multiple_of(place * self.own, self.own), self.own)

    def cross_blocks(self, k, sems):
        left, slots = self.operands[k][0:2]
        first, _ = self.mine()
        copies = []
        for block in range(2 * self.quarter):
            place = 4 * (block // 2) + self.side_of(1 - first, block % 2)
            copies.append(
                send(
                    left.at[:, self.columns(place)],
                    slots.at[:, pl.ds(block * self.own, self.own)],
                    sems[0].at[block],
                    sems[1].at[block],
                    "seq",
                    self.partner(),
                )
            )
        return copies

    def cross(self, k, sems):
        right, slots = self.operands[k][2:4]
        return [send(right, slots, sems[0].at[0], sems[1].at[0], "seq", self.partner())]

    def send_pair(self, k, da):
        ss, rs = self.sems[0:2]
        grads, peer = self.grads[k], self.place(0, 0)
        return send(grads[1].at[da], grads[2].at[da], ss.at[k, da], rs.at[k, da], "seq", peer)

    def send_far(self, k, da):
        ss, rs = self.sems[2:4]
        grads, peer = self.grads[k], self.place(da, 1)
        return send(grads[3].at[da], grads[4].at[da], ss.at[k, da], rs.at[k, da], "seq", peer)

    def column(self, k, da, side):
        left, left_other, right, right_other = self.operands[k]
        _, second = self.mine()
        second = second if side == 1 else 1 - second
        block = 2 * lax.rem(self.a + da, self.quarter) + second
        found = tn(left[:, self.columns(self.place(da, side))], right[...])
        return found + tn(left_other[:, self.columns(block)], right_other[...])

    def pair(self, far):
        def step(k, da):
            self.grads[k][1][da] = self.column(k, da, 0).astype(bf16)
            self.send_pair(k, da).start()

        self.loop(*self.span(far), step)

    def both(self, k, da):
        found = self.column(k, da, 1)
        self.send_pair(k, da).wait()
        return found + self.grads[k][2][da].astype(f32)

    def far(self):
        def step(k, da):
            self.grads[k][3][da] = self.both(k, da).astype(bf16)
            self.send_far(k, da).start()

        self.loop(*self.span(True), step)

    def settle(self, outs):
        for k, out in enumerate(outs):
            out[...] = self.both(k, 0)

        def step(k, da):
            self.send_far(k, da).wait()
            outs[k][...] += self.grads[k][4][da].astype(f32)

        self.loop(*self.span(True), step)

    @staticmethod
    def scratch(shapes, parts):
        quarter = parts // 4
        slots = []
        for rows, columns in shapes:
            slots += [pltpu.VMEM((quarter, rows // parts, columns), bf16)] * 4
        return slots, [pltpu.SemaphoreType.DMA((len(shapes), quarter))] * 4


class Product:
    def __init__(self, r, name, left, right, parts, first, left_other=None, right_other=None):
        self.left, self.right = left, right
        self.joined = left.shape[1] // parts % 128 == 0

        def own(part):
            return getattr(r, f"{name}_{part}")

        if self.joined:
            left_slots = own("left") if left_other is None else left_other
            right_slots = own("right") if right_other is None else right_other
            grads = (left, left_slots, right, right_slots, *(own(i) for i in range(4)))
            self.sum = JoinedSum([grads], [own(f"sem_{i}") for i in range(4)], parts, first)
            self.lefts, self.rights = [], []
            if left_other is None:
                self.lefts = self.sum.cross_blocks(0, (own("left_ss"), own("left_rs")))
            if right_other is None:
                self.rights = self.sum.cross(0, (own("right_ss"), own("right_rs")))
        else:
            self.whole = own("whole")
            grads = (self.whole, *(own(i) for i in range(5)))
            self.sum = ScatterSum([grads], [own(f"sem_{i}") for i in range(6)], parts)
        self.pair, self.far = self.sum.pair, self.sum.far

    def begin_left(self):
        if self.joined:
            for copy in self.lefts:
                copy.start()

    def begin(self):
        if self.joined:
            for copy in self.rights:
                copy.start()
        else:
            for b in range(self.left.shape[1] // 256):
                block = slice(256 * b, 256 * b + 256)
                self.whole[block, :] = tn(self.left[:, block], self.right[...]).astype(bf16)
            self.sum.start_one(0)

    def ready(self):
        if self.joined:
            for copy in self.lefts + self.rights:
                copy.wait()

    def settle(self, out):
        self.sum.settle((out,))

    @staticmethod
    def scratch(name, count, model, columns, parts, left=True, right=True):
        own, dma = model // parts, pltpu.SemaphoreType.DMA
        found = {}
        if own % 128 == 0:
            slots, sems = JoinedSum.scratch([(model, columns)], parts)
            if left:
                found["left"] = pltpu.VMEM((count, model // 2), bf16)
                found |= {f"left_{end}": dma((parts // 2,)) for end in ("ss", "rs")}
            if right:
                found["right"] = pltpu.VMEM((count, columns), bf16)
                found |= {f"right_{end}": dma((1,)) for end in ("ss", "rs")}
        else:
            slots, sems = ScatterSum.scratch([(model, columns)], parts)
            found["whole"] = pltpu.VMEM((model, columns), bf16)
        found |= {str(i): s for i, s in enumerate(slots)}
        found |= {f"sem_{i}": s for i, s in enumerate(sems)}
        return {f"{name}_{part}": spec for part, spec in found.items()}


def layer_kernel(*refs, names, parts, peers, scale):
    r = types.SimpleNamespace(**dict(zip(names, refs, strict=True)))
    count, width = r.q.shape
    span, model = r.pair.shape[1], r.inputs.shape[1]
    per = r.tok.shape[2]
    half = parts // 2
    me = lax.axis_index("seq")
    x, z = lax.rem(me, 2), me // 2
    partner = me + 1 - 2 * x

    def at(o, c):
        return 2 * o + (x if c == 0 else 1 - x)

    def reader(c, dz):
        return at(lax.rem(z + half - dz, half), c)

    held = Held(((r.q_all_hbm, r.q_all, r.q_sem), (r.rows_hbm, r.rows, r.rows_sem)), parts)
    held.ahead()

    def fetch(i):
        name = FETCHED[i]
        return pltpu.make_async_copy(
            getattr(r, name + "_hbm"), getattr(r, name), r.fetch_sem.at[i]
        )

    def fetch_late(i):
        place = r.w_up.at[:, pl.ds(i * width, width)]
        return pltpu.make_async_copy(
            getattr(r, LATE[i] + "_hbm"), place, r.fetch_sem.at[len(FETCHED) + i]
        )

    for i in range(len(FETCHED)):
        fetch(i).start()

    def head_sum(name, slots, source, full):
        return HeadSum(
            source,
            [getattr(r, f"{slots}_{i}") for i in range(3)],
            [getattr(r, f"{name}_sem_{i}") for i in range(4)],
            full,
            [getattr(r, f"{name}_full_{i}") for i in range(2)],
        )

    sums = head_sum("sum", "turn", r.partial, r.branch)
    feeds = head_sum("feed", "feed", r.feed_in, r.layer)
    attn = head_sum("attn", "turn", r.partial, r.normed_two)
    cot_other = getattr(r, "cot_other", None)
    normed_other = getattr(r, "normed_other", None)
    mixed_other = getattr(r, "mixed_other", None)
    p_down = Product(r, "down", r.cot, r.hidden, parts, "z", left_other=cot_other)
    p_up = Product(r, "up", r.normed_two, r.grad_upward, parts, "x")
    p_o = Product(r, "o", r.branch, r.mixed, parts, "x", right_other=mixed_other)
    p_kv = Product(r, "kv", r.normed, r.d_kv, parts, "x", left_other=normed_other)
    p_q = Product(r, "q", r.normed, r.d_q, parts, "x", left_other=normed_other)
    ids = lax.broadcasted_iota(jnp.int32, (count, per), 0)

    own_pair = [
        pltpu.make_async_copy(source, r.pair.at[i, pl.ds(W, count)], r.own_sem.at[i])
        for i, source in enumerate((r.k_hbm, r.v_hbm))
    ]
    for copy in own_pair:
        copy.start()
    @pl.when(z == 0)
    def _():
        r.pair[:, :count] = jnp.zeros_like(r.pair[:, :count])

    @pl.when(me == 0)
    def _():
        r.pair[:, count:W] = jnp.zeros_like(r.pair[:, count:W])


    for copy in own_pair:
        copy.wait()
    greet(seq=parts, head=peers)

    def pair_rows(first):
        return r.pair.at[:, pl.ds(first, count)]

    def hand_on(i, source, target, peer):
        return send(
            pair_rows(source), pair_rows(target), r.next_ss.at[i], r.next_rs.at[i], "seq", peer
        )

    next_one = hand_on(0, W, count, partner)
    next_two = hand_on(1, W, 0, me + 2)
    passed_on = hand_on(2, 0, count, partner)

    @pl.when(z < half - 1)
    def _():
        next_two.start()

    @pl.when(x == 0)
    def _():
        next_one.start()

    def recall_part(j):
        q_at, rows_at = held.get(j)
        outs, logs = [], []
        for h in range(2):
            cols = head_cols(h)
            keep = r.tok[j, h : h + 1, :] == ids
            s = jnp.where(keep, nt(q_at[:, cols], rows_at[h, :, 0:128]), NEG)
            top = jnp.max(s, axis=1, keepdims=True)
            p = jnp.where(keep, jnp.exp((s - top) * scale), 0.0)
            total = jnp.sum(p, axis=1, keepdims=True)
            some = total > 0.0
            safe = jnp.where(some, total, 1.0)
            outs.append(nn(p.astype(bf16), rows_at[h, :, 128:256]) / safe)
            logs.append(jnp.where(some, top * scale + jnp.log(safe), NEG))
        return outs, logs

    def out_x(dz):
        return (
            send(r.log_xs.at[dz], r.log_xr.at[dz], r.lx_ss.at[dz], r.lx_rs.at[dz], "seq", partner),
            send(r.dq_xs.at[dz], r.dq_xr.at[dz], r.ox_ss.at[dz], r.ox_rs.at[dz], "seq", partner),
        )

    def log_z(dz):
        return send(
            r.log_zs.at[dz], r.log_zr.at[dz], r.lz_ss.at[dz], r.lz_rs.at[dz], "seq", reader(0, dz)
        )

    def out_z(dz):
        return send(
            r.dq_zs.at[dz], r.dq_zr.at[dz], r.oz_ss.at[dz], r.oz_rs.at[dz], "seq", reader(0, dz)
        )

    def lend(dz):
        outs, logs = recall_part(reader(1, dz))
        for h in range(2):
            r.dq_xs[dz, h] = outs[h].astype(bf16)
        r.log_xs[dz] = row_form(logs, count).T[0:8]
        for copy in out_x(dz):
            copy.start()

    def unite(outs, logs, dz):
        for copy in out_x(dz):
            copy.wait()
        other = r.log_xr[dz].T
        joined = []
        for h in range(2):
            theirs = other[:, h : h + 1]
            top = jnp.maximum(logs[h], theirs)
            a, b = jnp.exp(logs[h] - top), jnp.exp(theirs - top)
            total = a + b
            outs[h] = outs[h] * (a / total) + r.dq_xr[dz, h].astype(f32) * (b / total)
            joined.append(top + jnp.log(total))
        return outs, joined

    def lend_step(dz, carry):
        lend(dz)
        return carry

    lax.fori_loop(1, half, lend_step, 0)
    lend(0)

    @pl.when(z > 0)
    def _():
        hand_on(1, W, 0, partner).wait_recv()

        @pl.when(x == 1)
        def _():
            passed_on.start()

    def keep_step(dz, carry):
        outs, logs = recall_part(reader(0, dz))
        outs, logs = unite(outs, logs, dz)
        for h in range(2):
            r.dq_zs[dz, h] = outs[h].astype(bf16)
        r.log_zs[dz] = row_form(logs, count).T[0:8]
        log_z(dz).start()
        out_z(dz).start()
        return carry

    lax.fori_loop(1, half, keep_step, 0)
    outs, logs = recall_part(me)
    outs, logs = unite(outs, logs, 0)
    r.log_zr[0] = row_form(logs, count).T[0:8]
    for h in range(2):
        r.recalled[:, head_cols(h)] = outs[h]

    @pl.when(x == 0)
    def _():
        next_one.wait_send()

        @pl.when(z > 0)
        def _():
            passed_on.wait_recv()

    @pl.when(x == 1)
    def _():
        next_one.wait_recv()

        @pl.when(z > 0)
        def _():
            passed_on.wait_send()

    @pl.when(z < half - 1)
    def _():
        next_two.wait_send()

    first = me * count
    start = doc_starts(r.lengths, first, count)
    key_place = first - W + lax.broadcasted_iota(jnp.int32, (count, span), 1)
    seen = key_place >= start
    for h in range(2):
        cols = head_cols(h)
        bias = pltpu.roll(
            jnp.broadcast_to(r.bias[h : h + 1, :], (count, span)), 0, 1, stride=1, stride_axis=0
        )
        s = nt(r.q[:, cols], r.pair[0, :, cols]) * scale + bias
        s = jnp.where(seen, s, NEG)
        raised = jnp.exp(s - jnp.max(s, axis=1, keepdims=True))
        p = raised / jnp.sum(raised, axis=1, keepdims=True)
        r.p[h] = p
        r.local[:, cols] = nn(p.astype(bf16), r.pair[1, :, cols])

    def wait_log(dz, top):
        log_z(dz).wait()
        return jnp.maximum(top, r.log_zr[dz])

    top = lax.fori_loop(1, half, wait_log, r.log_zr[0])

    def add_to(dz, total):
        return total + jnp.exp(r.log_zr[dz] - top)

    logs = top + jnp.log(lax.fori_loop(0, half, add_to, jnp.zeros_like(top)))
    r.logs[...] = logs
    share = jnp.exp(r.log_zr[0] - logs).T
    for h in range(2):
        r.recalled[:, head_cols(h)] *= share[:, h : h + 1]

    def gather_out(dz, carry):
        share = jnp.exp(r.log_zr[dz] - logs).T
        out_z(dz).wait()
        for h in range(2):
            r.recalled[:, head_cols(h)] += share[:, h : h + 1] * r.dq_zr[dz, h].astype(f32)
        return carry

    lax.fori_loop(1, half, gather_out, 0)
    for h in range(2):
        cols = head_cols(h)
        gate = r.gate[h]
        mixed = gate * r.recalled[:, cols] + (1.0 - gate) * r.local[:, cols]
        r.mixed[:, cols] = mixed.astype(bf16)


    for i in range(len(FETCHED)):
        fetch(i).wait()
    for b in range(model // 256):
        block = slice(256 * b, 256 * b + 256)
        r.partial[:, block] = nn(r.mixed[...], r.w_o[:, block]).astype(bf16)
    attn.start()
    crossing = []
    if cot_other is not None:
        for name, first, left, other in (("cot", "z", r.cot, cot_other), ("normed", "x", r.normed, normed_other)):
            joined = JoinedSum([(left, other, left, left)], [None] * 4, parts, first)
            sems = getattr(r, f"{name}_ss"), getattr(r, f"{name}_rs")
            crossing += joined.cross_blocks(0, sems)
        joined = JoinedSum([(r.normed, r.normed, r.mixed, mixed_other)], [None] * 4, parts, "x")
        crossing += joined.cross(0, (r.mixed_ss, r.mixed_rs))
        for copy in crossing:
            copy.start()
    attn.relay()
    branch = attn.total()
    middle = r.inputs[attn.mine, :].astype(f32) + branch
    r.middle[...] = middle
    row_scale = lax.rsqrt(row_mean(middle * middle) + eps)
    hat = middle * row_scale
    attn.spread(hat * r.gain_two[...])
    r.small_send[17:18] = fold_sum(col_sum(branch * branch))
    attn.forward()
    attn.settle()

    p_up.begin_left()
    for b in range(r.hidden.shape[1] // 256):
        block = slice(256 * b, 256 * b + 256)
        up = nn(r.normed_two[...], r.w_up[:, block])
        square = up * up
        bent = jnp.tanh(GELU * (up + 0.044715 * up * square))
        rise = 0.5 * (1.0 + bent)
        r.hidden[:, block] = (up * rise).astype(bf16)
        steep = (0.5 * GELU) * up * (1.0 - bent * bent) * (1.0 + (3 * 0.044715) * square)
        r.slope[:, block] = rise + steep
    p_down.begin()
    for b in range(r.hidden.shape[1] // 256):
        block = slice(256 * b, 256 * b + 256)
        back = nt(r.cot[...], r.w_down[block, :])
        r.grad_upward[:, block] = (r.slope[:, block] * back).astype(bf16)
    p_up.begin()
    for b in range(model // 256):
        block = slice(256 * b, 256 * b + 256)
        r.partial[:, block] = nt(r.grad_upward[...], r.w_up[block, :]).astype(bf16)

    sums.start()
    for i in range(len(LATE)):
        fetch_late(i).start()
    sums.relay()
    for b in range(model // 256):
        block = slice(256 * b, 256 * b + 256)
        r.feed_in[:, block] = nn(r.hidden[...], r.w_down[:, block]).astype(bf16)
    feeds.start()
    grad_normed = sums.total()
    scaled = grad_normed * r.gain_two[...]
    grad_middle = r.cot[sums.mine, :].astype(f32) + row_scale * (
        scaled - hat * row_mean(scaled * hat)
    )
    sums.spread(grad_middle)
    r.grad_middle[...] = grad_middle
    r.small_send[8:16] = folded(col_sum(grad_normed * hat))
    feeds.relay()
    sums.forward()
    sums.settle()
    g_own = nt(r.branch[...], r.w_o[...]).astype(bf16)
    r.g_all[0, z] = g_own

    deltas = []
    for h in range(2):
        cols = head_cols(h)
        g = g_own[:, cols].astype(f32)
        r.small_send[19 + h : 20 + h] = col_sum(g * (r.recalled[:, cols] - r.local[:, cols]))
        both = jnp.sum(g * r.recalled[:, cols], axis=1, keepdims=True)
        deltas.append(both * r.gate[h])
    turned = row_form([jnp.zeros_like(deltas[0])] * 2 + deltas, count).T[0:8]
    row = lax.broadcasted_iota(jnp.int32, (8, count), 0)
    r.st_all[0, z] = jnp.where(row < 2, r.logs[...], turned)

    def ask(c, o, way, peer):
        return (
            send(
                r.st_all.at[0, o], r.st_all.at[c, o], r.st_ss.at[way, o], r.st_rs.at[c, o], "seq", peer
            ),
            send(r.g_all.at[0, o], r.g_all.at[c, o], r.g_ss.at[way, o], r.g_rs.at[c, o], "seq", peer),
        )

    def start(copies):
        for copy in copies:
            copy.start()

    def up(o):
        return ask(0, o, 0, me + 2)

    def down(o):
        return ask(0, o, 1, me - 2)

    def across(o):
        return ask(1, o, 2, partner)

    def arrived(c, o):
        for copy in ask(c, o, 2, partner):
            copy.wait_recv()

    def sent(copies):
        for copy in copies:
            copy.wait_send()

    @pl.when(z < half - 1)
    def _():
        start(up(z))

    @pl.when(z > 0)
    def _():
        start(down(z))

    start(across(z))
    for copy in crossing:
        copy.wait_recv()
    p_down.ready()
    p_down.pair(True)

    for h in range(2):
        cols = head_cols(h)
        rest = 1.0 - r.gate[h]
        g = r.g_all[0, z, :, cols]
        p = r.p[h]
        e = nt(g, r.pair[1, :, cols])
        delta = jnp.sum(p * e, axis=1, keepdims=True)
        ds = (p * ((e - delta) * rest)).astype(bf16)
        r.dq_sum[:, cols] = nn(ds, r.pair[0, :, cols]) * scale
        dk = tn(ds, r.q[:, cols]) * scale
        dv = tn(p.astype(bf16), g) * rest
        r.pair_sum[0, :, cols] = dk[W:]
        r.pair_sum[1, :, cols] = dv[W:]
        r.pair_send[0, :, cols] = dk[:W].astype(bf16)
        r.pair_send[1, :, cols] = dv[:W].astype(bf16)
        low = ds.astype(f32)
        acc = low[0:8]
        for a in range(1, count // 8):
            acc = acc + pltpu.roll(low[8 * a : 8 * a + 8], (span - 8 * a) % span, 1)
        line = acc[0:1]
        for b in range(1, 8):
            line = line + pltpu.roll(acc[b : b + 1], span - b, 1)
        lines = span // 128
        for i in range(lines):
            r.small_send[24 + h * lines + i : 25 + h * lines + i] = line[:, 128 * i : 128 * i + 128]

    halo_x = send(
        r.pair_send.at[:, pl.ds(count, count)], r.halo_x, r.halo_ss.at[0], r.halo_rs.at[0], "seq", partner
    )
    halo_z = send(r.halo_send, r.halo_z, r.halo_ss.at[1], r.halo_rs.at[1], "seq", me - 2)

    def owner_part(c, o):
        j = at(o, c)
        q_at, rows_at = held.get(j, again=True)
        stats = r.st_all[c, o].T
        found = []
        for h in range(2):
            cols = head_cols(h)
            keep = r.tok[j, h : h + 1, :] == ids
            s = nt(q_at[:, cols], rows_at[h, :, 0:128]) * scale
            p = jnp.exp(jnp.where(keep, s - stats[:, h : h + 1], NEG))
            e = nt(r.g_all[c, o, :, cols], rows_at[h, :, 128:256]) * r.gate[h]
            ds = (p * (e - stats[:, 2 + h : 3 + h])).astype(bf16)
            found.append(nn(ds, rows_at[h, :, 0:128]) * scale)
        return found

    own = owner_part(0, z)
    for h in range(2):
        r.dq_sum[:, head_cols(h)] += own[h]

    def give_x(o):
        return send(r.dq_xs.at[o], r.dq_xr.at[o], r.dx_ss.at[o], r.dx_rs.at[o], "seq", partner)

    def give_z(o):
        return send(r.dq_zs.at[o], r.dq_zr.at[z], r.dz_ss.at[o], r.dz_rs.at[z], "seq", at(o, 0))

    def got_z(o):
        return send(r.dq_zs.at[o], r.dq_zr.at[o], r.dz_ss.at[o], r.dz_rs.at[o], "seq", partner)

    def neighbour(o):
        arrived(1, o)
        found = owner_part(1, o)
        for h in range(2):
            r.dq_xs[o, h] = found[h].astype(bf16)
        give_x(o).start()

    def column(o):
        found = owner_part(0, o)
        for h in range(2):
            r.dq_zs[o, h] = found[h].astype(bf16)

    def near(body):
        def step(t, carry):
            @pl.when(z - t >= 0)
            def _():
                body(z - t, True)

            @pl.when(z + t < half)
            def _():
                body(z + t, False)

            return carry

        lax.fori_loop(1, half, step, 0)

    neighbour(z)

    def relay(o, below):
        arrived(0, o)
        start(across(o))
        if below:

            @pl.when(z < half - 1)
            def _():
                start(up(o))

        else:

            @pl.when(z > 0)
            def _():
                start(down(o))

    def relay_step(t, carry):
        @pl.when(z - t >= 0)
        def _():
            relay(z - t, True)

        @pl.when(z + t < half)
        def _():
            relay(z + t, False)

        @pl.when(z - t >= 0)
        def _():
            column(z - t)

        @pl.when(z + t < half)
        def _():
            column(z + t)

        return carry

    lax.fori_loop(1, half, relay_step, 0)
    p_up.ready()
    p_up.pair(True)
    feed_sum = feeds.total()
    layer = r.middle[...] + feed_sum
    feeds.spread(layer)
    r.small_send[16:17] = fold_sum(col_sum(layer * layer))
    r.small_send[18:19] = fold_sum(col_sum(feed_sum * feed_sum))
    near(lambda o, below: neighbour(o))
    halo_x.start()
    p_down.pair(False)
    p_o.begin_left()
    p_o.begin()
    p_up.pair(False)

    def join(o, below):
        give_x(o).wait()
        for h in range(2):
            both = r.dq_zs[o, h].astype(f32) + r.dq_xr[o, h].astype(f32)
            r.dq_zs[o, h] = both.astype(bf16)
        give_z(o).start()

    near(join)
    halo_x.wait()
    passing = x.astype(f32)
    r.halo_send[...] = (
        r.pair_send[:, :count].astype(f32) + r.halo_x[...].astype(f32) * passing
    ).astype(bf16)
    r.pair_sum[...] += r.halo_x[...].astype(f32) * (1.0 - passing)

    @pl.when(z > 0)
    def _():
        halo_z.start()

    feeds.forward()
    give_x(z).wait()
    for h in range(2):
        r.dq_sum[:, head_cols(h)] += r.dq_xr[z, h].astype(f32)

    def merge(o, below):
        got_z(o).wait_recv()
        for h in range(2):
            r.dq_sum[:, head_cols(h)] += r.dq_zr[o, h].astype(f32)

    near(merge)

    r.d_q[...] = r.dq_sum[...].astype(bf16)
    p_q.begin()
    p_down.far()
    p_up.far()
    @pl.when(z > 0)
    def _():
        halo_z.wait_send()

    @pl.when(z < half - 1)
    def _():
        send(r.halo_send, r.halo_z, r.halo_ss.at[1], r.halo_rs.at[1], "seq", partner).wait_recv()
        r.pair_sum[...] += r.halo_z[...].astype(f32)

    r.d_kv[:, :width] = r.pair_sum[0].astype(bf16)
    r.d_kv[:, width:] = r.pair_sum[1].astype(bf16)
    p_kv.begin()
    for i in range(len(LATE)):
        fetch_late(i).wait()
    for b in range(model // 256):
        block = slice(256 * b, 256 * b + 256)
        r.partial[:, block] = (
            nt(r.d_q[...], r.w_up[block, :width])
            + nt(r.d_kv[...], r.w_up[block, width : 3 * width])
        ).astype(bf16)
    backs = head_sum("back", "turn", r.partial, r.input_grad)
    backs.start()
    backs.relay()
    p_o.ready()
    p_o.pair(True)
    p_kv.ready()
    p_kv.pair(True)
    tokens = r.inputs[backs.mine, :].astype(f32)
    in_scale = lax.rsqrt(row_mean(tokens * tokens) + eps)
    in_hat = tokens * in_scale
    back_sum = backs.total()
    g = back_sum * r.gain_one[...]
    backs.spread(r.grad_middle[...] + in_scale * (g - in_hat * row_mean(g * in_hat)))
    r.small_send[0:8] = folded(col_sum(back_sum * in_hat))
    r.small_send[21:24] = jnp.zeros((3, 128), f32)
    r.small_send[36:40] = jnp.zeros((4, 128), f32)

    def small_heads(d):
        peer = lax.rem(lax.axis_index("head") + d, peers)
        return send(r.small_send, r.small_head.at[d], r.sh_ss.at[d], r.sh_rs.at[d], "head", peer)

    for d in range(1, peers):
        small_heads(d).start()
    p_q.ready()
    p_q.pair(True)
    backs.forward()
    p_o.far()
    p_kv.far()

    kept = lax.broadcasted_iota(jnp.int32, r.small_send.shape, 0) < 19
    found = r.small_send[...]
    for d in range(1, peers):
        small_heads(d).wait()
        found = found + jnp.where(kept, r.small_head[d], 0.0)
    r.small_seq[0] = found

    def small_seqs(d):
        peer = lax.rem(me + d, parts)
        return send(r.small_seq.at[0], r.small_seq.at[d], r.sq_ss.at[d], r.sq_rs.at[d], "seq", peer)

    def small_start(d, carry):
        small_seqs(d).start()
        return carry

    lax.fori_loop(1, parts, small_start, 0)
    p_o.pair(False)
    p_kv.pair(False)
    p_q.far()
    p_q.pair(False)
    p_down.settle(r.down_sum)
    r.down_out[...] = r.down_sum[...].T
    p_up.settle(r.up_out)
    p_o.settle(r.o_sum)
    p_kv.settle(r.kv_sum)
    r.k_out[...] = r.kv_sum[:, :width]
    r.v_out[...] = r.kv_sum[:, width:]
    r.o_out[...] = r.o_sum[...].T
    p_q.settle(r.q_out)
    r.small[...] = r.small_seq[0]

    def small_add(d, carry):
        small_seqs(d).wait()
        r.small[...] += r.small_seq[d]
        return carry

    lax.fori_loop(1, parts, small_add, 0)
    feeds.settle()
    backs.settle()

    sent(across(z))

    @pl.when(z < half - 1)
    def _():
        sent(up(z))

    @pl.when(z > 0)
    def _():
        sent(down(z))

    def drain(o, below):
        sent(across(o))
        give_z(o).wait_send()
        if below:

            @pl.when(z < half - 1)
            def _():
                sent(up(o))

        else:

            @pl.when(z > 0)
            def _():
                sent(down(o))

    near(drain)
    for copy in crossing:
        copy.wait_send()


FETCHED = ("cot", "w_o", "w_up", "w_down")
LATE = ("w_q", "w_k", "w_v")
GELU = math.sqrt(2 / math.pi)


def layer(inputs, parts, peers):
    count, width = inputs["q"].shape
    model, span = inputs["inputs"].shape[1], W + count
    half, own = parts // 2, model // parts
    smem = pl.BlockSpec(memory_space=pltpu.SMEM)
    vmem = pl.BlockSpec(memory_space=pltpu.VMEM)
    hbm = pl.BlockSpec(memory_space=pltpu.HBM)
    dma = pltpu.SemaphoreType.DMA
    wide = inputs["w_up_hbm"].shape[1]
    outputs = dict(
        input_grad=((count, model), bf16),
        layer=((count, model), bf16),
        q_out=((own, width), f32),
        k_out=((own, width), f32),
        v_out=((own, width), f32),
        o_out=((width, own), f32),
        up_out=((own, wide), f32),
        down_out=((wide, own), f32),
        small=((40, 128), f32),
    )
    outputs = {name: jax.ShapeDtypeStruct(*spec) for name, spec in outputs.items()}
    held = Held.scratch((inputs["q_all_hbm"], inputs["rows_hbm"]), parts)
    scratch = dict(zip(("q_all", "rows", "q_sem", "rows_sem"), held, strict=True))
    scratch |= {name: pltpu.VMEM(inputs[name + "_hbm"].shape, bf16) for name in FETCHED}
    for name, spec in dict(
        recalled=((count, width), f32),
        local=((count, width), f32),
        mixed=((count, width), bf16),
        logs=((8, count), f32),
        p=((2, count, span), f32),
        pair=((2, span, width), bf16),
        log_xs=((half, 8, count), f32),
        log_xr=((half, 8, count), f32),
        log_zs=((half, 8, count), f32),
        log_zr=((half, 8, count), f32),
        normed_two=((count, model), bf16),
        middle=((count // peers, model), f32),
        hidden=((count, wide), bf16),
        slope=((count, wide), f32),
        grad_upward=((count, wide), bf16),
        partial=((count, model), bf16),
        feed_in=((count, model), bf16),
        branch=((count, model), bf16),
        grad_middle=((count // peers, model), f32),
        g_all=((2, half, count, width), bf16),
        st_all=((2, half, 8, count), f32),
        dq_xs=((half, 2, count, 128), bf16),
        dq_xr=((half, 2, count, 128), bf16),
        dq_zs=((half, 2, count, 128), bf16),
        dq_zr=((half, 2, count, 128), bf16),
        pair_send=((2, W, width), bf16),
        pair_sum=((2, count, width), f32),
        halo_x=((2, count, width), bf16),
        halo_send=((2, count, width), bf16),
        halo_z=((2, count, width), bf16),
        dq_sum=((count, width), f32),
        d_kv=((count, 2 * width), bf16),
        d_q=((count, width), bf16),
        kv_sum=((own, 2 * width), f32),
        o_sum=((own, width), f32),
        down_sum=((own, wide), f32),
        small_send=((40, 128), f32),
        small_head=((peers, 40, 128), f32),
        small_seq=((parts, 40, 128), f32),
    ).items():
        scratch[name] = pltpu.VMEM(*spec)
    for name, shape in dict(
        fetch_sem=(len(FETCHED) + len(LATE),),
        own_sem=(2,),
        next_ss=(3,),
        next_rs=(3,),
        ox_ss=(half,),
        ox_rs=(half,),
        oz_ss=(half,),
        oz_rs=(half,),
        lx_ss=(half,),
        lx_rs=(half,),
        lz_ss=(half,),
        lz_rs=(half,),
        st_ss=(3, half),
        st_rs=(2, half),
        g_ss=(3, half),
        g_rs=(2, half),
        dx_ss=(half,),
        dx_rs=(half,),
        dz_ss=(half,),
        dz_rs=(half,),
        halo_ss=(2,),
        halo_rs=(2,),
        sh_ss=(peers,),
        sh_rs=(peers,),
        sq_ss=(parts,),
        sq_rs=(parts,),
    ).items():
        scratch[name] = dma(shape)
    for name in ("turn", "feed"):
        scratch |= {f"{name}_{i}": s for i, s in enumerate(HeadSum.scratch(count, model))}
    for name in ("attn", "sum", "feed", "back"):
        scratch |= {f"{name}_sem_{i}": s for i, s in enumerate(HeadSum.sems())}
        scratch |= {f"{name}_full_{i}": s for i, s in enumerate(HeadSum.full_scratch())}
    if own % 128 == 0:
        for name in ("cot", "normed"):
            scratch[f"{name}_other"] = pltpu.VMEM((count, model // 2), bf16)
            scratch |= {f"{name}_{end}": dma((half,)) for end in ("ss", "rs")}
        scratch["mixed_other"] = pltpu.VMEM((count, width), bf16)
        scratch |= {f"mixed_{end}": dma((1,)) for end in ("ss", "rs")}
    for name, columns, left, right in (
        ("down", wide, False, True),
        ("up", wide, True, True),
        ("o", width, True, False),
        ("kv", 2 * width, False, True),
        ("q", width, False, True),
    ):
        scratch |= Product.scratch(name, count, model, columns, parts, left, right)
    spaces = dict(gate=smem, lengths=smem)
    spaces |= {name: hbm for name in inputs if name.endswith("_hbm")}
    found = pl.pallas_call(
        functools.partial(
            layer_kernel,
            names=(*inputs, *outputs, *scratch),
            parts=parts,
            peers=peers,
            scale=128**-0.5,
        ),
        out_shape=tuple(outputs.values()),
        in_specs=[spaces.get(name, vmem) for name in inputs],
        out_specs=(vmem,) * len(outputs),
        scratch_shapes=list(scratch.values()),
        compiler_params=pltpu.CompilerParams(
            vmem_limit_bytes=(58 if parts <= 8 else 63) * MIB, collective_id=2, has_side_effects=True
        ),
        cost_estimate=pl.CostEstimate(
            flops=4 * 10**9, bytes_accessed=150 * MIB, transcendentals=5 * 10**6
        ),
        name="layer",
    )(*inputs.values())
    return dict(zip(outputs, found, strict=True))


def hand_out_kernel(*refs, copied, entries):
    count = len(copied)
    sources, (input_grad, small, gate, hot), outs = refs[:count], refs[count : count + 4], refs[count + 4 :]
    grad_out, gains_out, position_out, gate_out, rms_out = outs[count : count + 5]
    for source, out in zip(sources, outs):
        out[...] = source[...]
    grad_out[...] = input_grad[...].astype(f32)
    me = lax.axis_index("seq")
    if gains_out.shape[1] == 128:
        gains_out[0:1, :] = small[pl.ds(me, 1), :]
        gains_out[1:2, :] = small[pl.ds(me + 8, 1), :]
    else:
        gains_out[...] = small[0:16, :]
    lines = hot.shape[0] // 128
    for h in range(2):
        found = jnp.zeros((1, hot.shape[1]), f32)
        for i in range(lines):
            line = small[24 + h * lines + i : 25 + h * lines + i, :]
            found = found + lax.dot_general(
                line,
                hot[128 * i : 128 * i + 128, :],
                (((1,), (0,)), ((), ())),
                precision=highest,
                preferred_element_type=f32,
            )
        position_out[h : h + 1, :] = found
    sums = jnp.sum(small[16:24, :], axis=1, keepdims=True)
    lane = lax.broadcasted_iota(jnp.int32, (1, 2), 1)
    steep = jnp.where(lane == 0, gate[0] * (1.0 - gate[0]), gate[1] * (1.0 - gate[1]))
    gate_out[...] = jnp.where(lane == 0, sums[3:4], sums[4:5]) * steep
    lane = lax.broadcasted_iota(jnp.int32, (1, 3), 1)
    squares = jnp.where(lane == 0, sums[0:1], jnp.where(lane == 1, sums[1:2], sums[2:3]))
    rms_out[...] = jnp.sqrt(squares / entries)


def hand_out(done, gate, hot, entries, parts):
    copied = ("layer", "q_out", "k_out", "v_out", "o_out", "up_out", "down_out")
    smem = pl.BlockSpec(memory_space=pltpu.SMEM)
    vmem = pl.BlockSpec(memory_space=pltpu.VMEM)
    model = done["input_grad"].shape[1]
    own = model // parts
    shapes = [jax.ShapeDtypeStruct(done[name].shape, done[name].dtype) for name in copied]
    shapes += [
        jax.ShapeDtypeStruct(shape, f32)
        for shape in (
            done["input_grad"].shape,
            (2, 128) if own == 128 else (16, 128),
            (2, hot.shape[1]),
            (1, 2),
            (1, 3),
        )
    ]
    found = pl.pallas_call(
        functools.partial(hand_out_kernel, copied=copied, entries=entries),
        out_shape=tuple(shapes),
        in_specs=[vmem] * len(copied) + [vmem, vmem, smem, vmem],
        out_specs=(vmem,) * (len(copied) + 5),
        compiler_params=pltpu.CompilerParams(vmem_limit_bytes=62 * MIB),
        name="hand_out",
    )(*(done[name] for name in copied), done["input_grad"], done["small"], gate, hot)
    named = dict(zip(copied, found))
    named |= dict(zip(("input_grad", "gains", "position", "gate", "rms"), found[len(copied) :]))
    return named


def norm_stats(values):
    row_scale = lax.rsqrt(jnp.mean(values * values, axis=-1, keepdims=True) + eps)
    return (values * row_scale, row_scale)


def per_device(
    inputs,
    cotangent,
    query_weight,
    key_weight,
    value_weight,
    output_weight,
    up_weight,
    down_weight,
    first_gain,
    second_gain,
    position_bias,
    gate_bias,
    memory_table,
    retrieved,
    lengths,
):
    _, block_len, model_width = inputs.shape
    bucket_total = position_bias.shape[1]
    seq_count = lax.axis_size("seq")
    slot_count = memory_table.shape[0]

    wanted = jnp.transpose(retrieved[0], (1, 0, 2))
    token = jnp.arange(block_len, dtype=jnp.int32)[None, :, None]
    codes = (wanted // slot_count) * (block_len * slot_count) + token * slot_count + wanted % slot_count
    codes = lax.sort(codes.reshape(2, -1), dimension=1, is_stable=False)
    places, tok = request(codes, seq_count, slot_count, block_len)
    rows = gather_rows(places, widen(memory_table))

    hot, outside = diagonal_buckets(block_len, bucket_total)
    bias_row = jnp.dot(position_bias, hot, precision=highest) + outside[None]

    x, cot = inputs[0], cotangent[0]
    peers = lax.axis_size("head")
    gate_flat = jax.nn.sigmoid(gate_bias)
    hat_one, _ = norm_stats(x.astype(f32))
    normed_one = (hat_one * first_gain).astype(bf16)
    queries = nn(normed_one, query_weight).astype(bf16)
    keys = nn(normed_one, key_weight).astype(bf16)
    values = nn(normed_one, value_weight).astype(bf16)
    q_all = lax.all_gather(queries, "seq", axis=0)

    done = layer(
        dict(
            lengths=lengths[0],
            gate=gate_flat,
            q=queries,
            k_hbm=keys,
            v_hbm=values,
            bias=bias_row,
            tok=tok,
            inputs=x,
            normed=normed_one,
            gain_one=first_gain[None],
            gain_two=second_gain[None],
            q_all_hbm=q_all,
            rows_hbm=rows,
            cot_hbm=cot,
            w_o_hbm=output_weight,
            w_up_hbm=up_weight,
            w_down_hbm=down_weight,
            w_q_hbm=query_weight,
            w_k_hbm=key_weight,
            w_v_hbm=value_weight,
        ),
        seq_count,
        peers,
    )
    entries = float(block_len * model_width * seq_count)
    out = hand_out(done, gate_flat, jnp.asarray(hot.T), entries, seq_count)
    share = model_width // seq_count
    gains = out["gains"]
    if share != 128:
        start = lax.axis_index("seq") * share
        gains = lax.dynamic_slice_in_dim(gains.reshape(2, model_width), start, share, 1)
    return (
        out["layer"][None],
        out["input_grad"][None],
        out["q_out"],
        out["k_out"],
        out["v_out"],
        out["o_out"],
        out["up_out"],
        out["down_out"],
        gains[0],
        gains[1],
        out["position"],
        out["gate"][0],
        out["rms"][0],
    )


def solution(mesh):
    in_specs = (
        P(None, "seq", None),
        P(None, "seq", None),
        P(None, "head"),
        P(None, "head"),
        P(None, "head"),
        P("head", None),
        P(None, "head"),
        P("head", None),
        P(),
        P(),
        P("head", None),
        P("head"),
        P("seq", "head", None),
        P(None, "seq", "head", None),
        P(),
    )
    out_specs = (
        P(None, "seq", None),
        P(None, "seq", None),
        P("seq", "head"),
        P("seq", "head"),
        P("seq", "head"),
        P("head", "seq"),
        P("seq", "head"),
        P("head", "seq"),
        P("seq"),
        P("seq"),
        P("head", None),
        P("head"),
        P(),
    )
    return jax.shard_map(
        per_device, mesh=mesh, in_specs=in_specs, out_specs=out_specs, check_vma=False
    )
```

```python
import functools
import math
import types

import jax
import jax.numpy as jnp
import numpy as np
from jax import lax
from jax.experimental import pallas as pl
from jax.experimental.pallas import tpu as pltpu
from jax.sharding import PartitionSpec as P

W = 512
eps = 1e-06
exact_span = 16
far_distance = 128
highest = lax.Precision.HIGHEST
f32 = jnp.float32
bf16 = jnp.bfloat16
NEG = -1e30
MIB = 2**20


def bucket_table(key_span, bucket_total):
    found = []
    for distance in range(key_span):
        if distance < exact_span:
            found.append(distance)
        else:
            scaled = math.log(distance / exact_span) / math.log(far_distance / exact_span)
            found.append(
                min(bucket_total - 1, exact_span + math.floor(scaled * (bucket_total - exact_span)))
            )
    return np.asarray(found)


def diagonal_buckets(block_len, bucket_total):
    span = W + block_len
    table = bucket_table(W, bucket_total)
    hot = np.zeros((bucket_total, span), np.float32)
    for u in range(1, W + 1):
        hot[table[W - u], u] = 1.0
    outside = np.where(hot.sum(0) > 0, 0.0, NEG).astype(np.float32)
    return hot, outside


def nt(a, b):
    return lax.dot_general(a, b, (((1,), (1,)), ((), ())), preferred_element_type=f32)


def nn(a, b):
    return lax.dot_general(a, b, (((1,), (0,)), ((), ())), preferred_element_type=f32)


def tn(a, b):
    return lax.dot_general(a, b, (((0,), (0,)), ((), ())), preferred_element_type=f32)


def widen_kernel(table_hbm, wide_hbm, buf, out, sem, out_sem, *, chunk, part):
    chunks = table_hbm.shape[0] // chunk

    def fetch(i):
        return pltpu.make_async_copy(
            table_hbm.at[pl.ds(i * chunk, chunk)], buf.at[i % 2], sem.at[i % 2]
        )

    def store(i):
        return pltpu.make_async_copy(
            out.at[i % 2], wide_hbm.at[:, pl.ds(2 * i * chunk, 2 * chunk)], out_sem.at[i % 2]
        )

    fetch(0).start()
    for i in range(chunks):
        fetch(i).wait()
        if i + 1 < chunks:
            fetch(i + 1).start()
        if i > 1:
            store(i - 2).wait()

        def widen(q, carry, i=i):
            x = buf[i % 2, pl.ds(q * part, part)].astype(f32)
            for r in range(part):
                for h in range(2):
                    place = pl.ds(2 * (q * part + r), 1)
                    out[i % 2, h, place, :] = x[r, h : h + 1, 0:128]
                    place = pl.ds(2 * (q * part + r) + 1, 1)
                    out[i % 2, h, place, :] = x[r, h : h + 1, 128:256]
            return carry

        lax.fori_loop(0, chunk // part, widen, 0)
        store(i).start()
    for i in range(max(0, chunks - 2), chunks):
        store(i).wait()


def widen(table):
    total = table.shape[0]
    chunk = min(1024, total)
    hbm = pl.BlockSpec(memory_space=pltpu.HBM)
    dma = pltpu.SemaphoreType.DMA
    return pl.pallas_call(
        functools.partial(widen_kernel, chunk=chunk, part=32),
        out_shape=jax.ShapeDtypeStruct((2, 2 * total, 128), f32),
        in_specs=[hbm],
        out_specs=hbm,
        scratch_shapes=[
            pltpu.VMEM((2, chunk, 2, 256), bf16),
            pltpu.VMEM((2, 2, 2 * chunk, 128), f32),
            dma((2,)),
            dma((2,)),
        ],
        compiler_params=pltpu.CompilerParams(vmem_limit_bytes=58 * MIB),
        cost_estimate=pl.CostEstimate(flops=0, bytes_accessed=40 * MIB, transcendentals=0),
        name="widen",
    )(table)


def gather_kernel(at_ref, wide_hbm, out_hbm, wide, buf, low, wide_sem, out_sem, *, unroll, group):
    parts, rows = out_hbm.shape[0], out_hbm.shape[2]

    def fetch(h):
        return pltpu.make_async_copy(wide_hbm.at[h], wide.at[h], wide_sem.at[h])

    def store(j, h, slot):
        return pltpu.make_async_copy(low.at[slot], out_hbm.at[j, h], out_sem.at[slot])

    for h in range(2):
        fetch(h).start()
    for h in range(2):
        fetch(h).wait()

        def one(j, carry, h=h):
            slot = lax.rem(j, 2)
            first = (2 * j + h) * rows

            def copy_rows(q, carry):
                base = q * unroll
                for g in range(0, unroll, group):
                    found = [
                        wide[h, pl.ds(at_ref[first + base + g + u], 2), :] for u in range(group)
                    ]
                    for u in range(group):
                        buf[pl.ds(2 * (base + g + u), 2), :] = found[u]
                return carry

            lax.fori_loop(0, rows // unroll, copy_rows, 0)

            if h == 0:

                @pl.when(j > 1)
                def _():
                    store(j, h, slot).wait()

            else:
                store(j, h, slot).wait()

            low[slot, :, 0:128] = buf[pl.ds(0, rows, 2), :].astype(bf16)
            low[slot, :, 128:256] = buf[pl.ds(1, rows, 2), :].astype(bf16)
            store(j, h, slot).start()
            return carry

        lax.fori_loop(0, parts, one, 0)
    store(0, 1, 0).wait()
    store(1, 1, 1).wait()


def gather_rows(places, wide):
    parts, heads, rows = places.shape
    unroll = min(64, rows)
    hbm = pl.BlockSpec(memory_space=pltpu.HBM)
    dma = pltpu.SemaphoreType.DMA
    return pl.pallas_call(
        functools.partial(gather_kernel, unroll=unroll, group=unroll // 2),
        out_shape=jax.ShapeDtypeStruct((parts, heads, rows, 256), bf16),
        in_specs=[pl.BlockSpec(memory_space=pltpu.SMEM), hbm],
        out_specs=hbm,
        scratch_shapes=[
            pltpu.VMEM(wide.shape, f32),
            pltpu.VMEM((2 * rows, 128), f32),
            pltpu.VMEM((2, rows, 256), bf16),
            dma((2,)),
            dma((2,)),
        ],
        compiler_params=pltpu.CompilerParams(vmem_limit_bytes=58 * MIB),
        cost_estimate=pl.CostEstimate(flops=0, bytes_accessed=100 * MIB, transcendentals=0),
        name="gather_rows",
    )(places.reshape(-1), wide)


MESH = pl.DeviceIdType.MESH


def greet(meanwhile=None, **counts):
    barrier = pltpu.get_barrier_semaphore()
    for axis, count in counts.items():
        me = lax.axis_index(axis)

        def call(d, carry, axis=axis, count=count, me=me):
            peer = lax.rem(me + d, count)
            pl.semaphore_signal(barrier, inc=1, device_id={axis: peer}, device_id_type=MESH)
            return carry

        lax.fori_loop(1, count, call, 0)
    if meanwhile is not None:
        meanwhile()
    pl.semaphore_wait(barrier, sum(counts.values()) - len(counts))


def send(src, dst, send_sem, recv_sem, axis, peer):
    return pltpu.make_async_remote_copy(
        src_ref=src,
        dst_ref=dst,
        send_sem=send_sem,
        recv_sem=recv_sem,
        device_id={axis: peer},
        device_id_type=MESH,
    )


def doc_starts(lengths_ref, first, count):
    place = first + lax.broadcasted_iota(jnp.int32, (count, 1), 0)
    start = jnp.zeros((count, 1), jnp.int32)
    end = jnp.int32(0)
    for c in range(lengths_ref.shape[0]):
        end = end + lengths_ref[c]
        start = jnp.where(end <= place, end, start)
    return start


def head_cols(h):
    return slice(h * 128, h * 128 + 128)


def row_form(columns, count):
    lane = lax.broadcasted_iota(jnp.int32, (count, 128), 1)
    wide = jnp.zeros((count, 128), f32)
    for i, column in enumerate(columns):
        wide = jnp.where(lane == i, column, wide)
    return wide


def request_kernel(
    codes_ref,
    normed_ref,
    wk_ref,
    wv_ref,
    place_ref,
    tok_ref,
    k_ref,
    v_ref,
    got,
    own_sem,
    ss,
    rs,
    *,
    parts,
    slots,
    tokens,
):
    rows = codes_ref.shape[1] // parts
    me = lax.axis_index("seq")

    def part(owner):
        return codes_ref.at[:, pl.ds(pl.multiple_of(owner * rows, 128), rows)]

    keep = pltpu.make_async_copy(part(me), got.at[0], own_sem)
    keep.start()

    def project():
        k_ref[...] = nn(normed_ref[...], wk_ref[...]).astype(bf16)
        v_ref[...] = nn(normed_ref[...], wv_ref[...]).astype(bf16)

    greet(project, seq=parts)

    def ask(d):
        peer = lax.rem(me + d, parts)
        return send(part(peer), got.at[d], ss.at[d], rs.at[d], "seq", peer)

    def start(d, carry):
        ask(d).start()
        return carry

    lax.fori_loop(1, parts, start, 0)
    shift = slots.bit_length() - 1

    def read(d, j):
        code = got[d]
        place_ref[j] = (code & (slots - 1)) * 2
        tok_ref[j] = (code >> shift) & (tokens - 1)

    keep.wait()
    read(0, me)

    def arrive(d, carry):
        ask(d).wait()
        read(d, lax.rem(me + parts - d, parts))
        return carry

    lax.fori_loop(1, parts, arrive, 0)


def request(codes, normed, wk, wv, parts, slots, tokens):
    rows = codes.shape[1] // parts
    vmem = pl.BlockSpec(memory_space=pltpu.VMEM)
    dma = pltpu.SemaphoreType.DMA
    shape = (parts, 2, rows)
    return pl.pallas_call(
        functools.partial(request_kernel, parts=parts, slots=slots, tokens=tokens),
        out_shape=(jax.ShapeDtypeStruct(shape, jnp.int32),) * 2
        + (jax.ShapeDtypeStruct((tokens, wk.shape[1]), bf16),) * 2,
        in_specs=[vmem] * 4,
        out_specs=(vmem,) * 4,
        scratch_shapes=[pltpu.VMEM(shape, jnp.int32), dma, dma((parts,)), dma((parts,))],
        compiler_params=pltpu.CompilerParams(
            vmem_limit_bytes=16 * MIB, collective_id=6, has_side_effects=True
        ),
        name="request",
    )(codes, normed, wk, wv)


class HeadSum:
    def __init__(self, src, scratch, sems, full=None, full_sems=None):
        self.src, self.full = src, full
        self.core_recv, self.side_send, self.side_recv = scratch
        self.core_ss, self.core_rs, self.side_ss, self.side_rs = sems
        self.full_sems = full_sems
        head = lax.axis_index("head")
        self.y, self.c = head // 2, lax.rem(head, 2)
        self.share = src.shape[0] // 4
        self.core = 2 * self.y + 1 - self.c
        self.side = 2 * (1 - self.y) + self.c
        self.mine = self.rows_of(head)

    def rows_of(self, place):
        return pl.ds(pl.multiple_of(place * self.share, self.share), self.share)

    def to_core(self, i):
        y = self.y if i == 0 else 1 - self.y
        src = self.src.at[self.rows_of(2 * y + 1 - self.c)]
        return send(src, self.core_recv.at[i], self.core_ss.at[i], self.core_rs.at[i], "head", self.core)

    def to_side(self):
        return send(self.side_send, self.side_recv, self.side_ss, self.side_rs, "head", self.side)

    def start(self):
        self.to_core(1).start()
        self.to_core(0).start()

    def relay(self):
        self.to_core(1).wait()
        other = self.src[self.rows_of(self.side), :].astype(f32)
        self.side_send[...] = (other + self.core_recv[1].astype(f32)).astype(bf16)
        self.to_side().start()

    def total(self):
        self.to_core(0).wait()
        found = self.src[self.mine, :].astype(f32) + self.core_recv[0].astype(f32)
        self.to_side().wait()
        return found + self.side_recv[...].astype(f32)

    def back(self, i):
        rows = self.rows_of(self.side) if i == 2 else self.mine
        peer = self.side if i == 1 else self.core
        ss, rs = self.full_sems
        return send(self.full.at[rows], self.full.at[rows], ss.at[i], rs.at[i], "head", peer)

    def spread(self, value):
        self.full[self.mine, :] = value.astype(self.full.dtype)
        self.back(1).start()
        self.back(0).start()

    def forward(self):
        self.back(1).wait()
        self.back(2).start()

    def settle(self):
        self.back(0).wait()
        self.back(2).wait()

    @staticmethod
    def scratch(count, width):
        piece = (count // 4, width)
        return [pltpu.VMEM((2,) + piece, bf16), pltpu.VMEM(piece, bf16), pltpu.VMEM(piece, bf16)]

    @staticmethod
    def sems():
        dma = pltpu.SemaphoreType.DMA
        return [dma((2,)), dma((2,)), dma, dma]

    @staticmethod
    def full_scratch():
        return [pltpu.SemaphoreType.DMA((3,))] * 2


class Held:
    def __init__(self, arrays, parts):
        self.arrays, self.parts = arrays, parts
        self.all = arrays[0][1].shape[0] == parts

    def fetch(self, i, j):
        hbm, place, sem = self.arrays[i]
        slot = j if self.all else 0
        return pltpu.make_async_copy(hbm.at[j], place.at[slot], sem.at[slot])

    def ahead(self):
        if self.all:

            def start(j, carry):
                for i in range(len(self.arrays)):
                    self.fetch(i, j).start()
                return carry

            lax.fori_loop(0, self.parts, start, 0)

    def get(self, j, again=False):
        for i in range(len(self.arrays)):
            if not self.all:
                self.fetch(i, j).start()
            if not (self.all and again):
                self.fetch(i, j).wait()
        return [place.at[j if self.all else 0] for _, place, _ in self.arrays]

    @staticmethod
    def scratch(arrays, parts):
        slots = parts if parts <= 8 else 1
        places = [pltpu.VMEM((slots,) + a.shape[1:], a.dtype) for a in arrays]
        return places + [pltpu.SemaphoreType.DMA((slots,))] * len(arrays)


class ScatterSum:
    def __init__(self, grads, sems, parts):
        self.grads, self.sems = grads, sems
        self.quarter = parts // 4
        self.own = grads[0][0].shape[0] // parts
        me = lax.axis_index("seq")
        self.x, self.b, self.a = lax.rem(me, 2), lax.rem(me // 2, 2), me // 4

    def place(self, da, side, x):
        b = self.b if side == 1 else 1 - self.b
        return 4 * lax.rem(self.a + da, self.quarter) + 2 * b + x

    def rows_of(self, place):
        return pl.ds(pl.multiple_of(place * self.own, self.own), self.own)

    def send_x(self, k, da, side):
        ss, rs = self.sems[0:2]
        return send(
            self.grads[k][0].at[self.rows_of(self.place(da, side, 1 - self.x))],
            self.grads[k][1].at[side, da],
            ss.at[k, side, da],
            rs.at[k, side, da],
            "seq",
            self.place(0, 1, 1 - self.x),
        )

    def send_pair(self, k, da):
        ss, rs = self.sems[2:4]
        grads, peer = self.grads[k], self.place(0, 0, self.x)
        return send(grads[2].at[da], grads[3].at[da], ss.at[k, da], rs.at[k, da], "seq", peer)

    def send_far(self, k, da):
        ss, rs = self.sems[4:6]
        grads, peer = self.grads[k], self.place(da, 1, self.x)
        return send(grads[4].at[da], grads[5].at[da], ss.at[k, da], rs.at[k, da], "seq", peer)

    def loop(self, first, last, step):
        def body(da, carry):
            for k in range(len(self.grads)):
                step(k, da)
            return carry

        lax.fori_loop(first, last, body, 0)

    def span(self, far):
        return (1, self.quarter) if far else (0, 1)

    def start(self, far, side):
        self.loop(*self.span(far), lambda k, da: self.send_x(k, da, side).start())

    def start_one(self, k):
        for far in (True, False):
            for side in range(2):

                def body(da, carry, side=side):
                    self.send_x(k, da, side).start()
                    return carry

                lax.fori_loop(*self.span(far), body, 0)

    def column(self, k, da, side):
        self.send_x(k, da, side).wait()
        mine = self.grads[k][0][self.rows_of(self.place(da, side, self.x)), :]
        return mine.astype(f32) + self.grads[k][1][side, da].astype(f32)

    def pair(self, far):
        def step(k, da):
            self.grads[k][2][da] = self.column(k, da, 0).astype(bf16)
            self.send_pair(k, da).start()

        self.loop(*self.span(far), step)

    def both(self, k, da):
        found = self.column(k, da, 1)
        self.send_pair(k, da).wait()
        return found + self.grads[k][3][da].astype(f32)

    def far(self):
        def step(k, da):
            self.grads[k][4][da] = self.both(k, da).astype(bf16)
            self.send_far(k, da).start()

        self.loop(*self.span(True), step)

    def settle(self, outs):
        for k, out in enumerate(outs):
            out[...] = self.both(k, 0)

        def step(k, da):
            self.send_far(k, da).wait()
            outs[k][...] += self.grads[k][5][da].astype(f32)

        self.loop(*self.span(True), step)

    @staticmethod
    def scratch(shapes, parts):
        quarter = parts // 4
        slots = []
        for rows, columns in shapes:
            piece = (rows // parts, columns)
            slots.append(pltpu.VMEM((2, quarter) + piece, bf16))
            slots += [pltpu.VMEM((quarter,) + piece, bf16)] * 4
        dma = pltpu.SemaphoreType.DMA
        count = len(shapes)
        return slots, [dma((count, 2, quarter))] * 2 + [dma((count, quarter))] * 4


def row_mean(x):
    return jnp.mean(x, axis=1, keepdims=True)


def col_sum(x):
    return jnp.sum(x, axis=0, keepdims=True)


def folded(line):
    return jnp.concatenate([line[:, 128 * i : 128 * i + 128] for i in range(8)], axis=0)


def fold_sum(line):
    return col_sum(folded(line))


class JoinedSum(ScatterSum):
    def __init__(self, grads, sems, parts, first):
        super().__init__([(g[0], *g[4:]) for g in grads], sems, parts)
        self.own = grads[0][0].shape[1] // parts
        self.operands = [g[0:4] for g in grads]
        self.first = first

    def side_of(self, first, second):
        return 2 * first + second if self.first == "z" else 2 * second + first

    def mine(self):
        return (self.b, self.x) if self.first == "z" else (self.x, self.b)

    def place(self, da, side, flip=0):
        first, second = self.mine()
        first = 1 - first if flip else first
        second = second if side == 1 else 1 - second
        return 4 * lax.rem(self.a + da, self.quarter) + self.side_of(first, second)

    def partner(self):
        return self.place(0, 1, 1)

    def columns(self, place):
        return pl.ds(pl.multiple_of(place * self.own, self.own), self.own)

    def cross_blocks(self, k, sems):
        left, slots = self.operands[k][0:2]
        first, _ = self.mine()
        copies = []
        for block in range(2 * self.quarter):
            place = 4 * (block // 2) + self.side_of(1 - first, block % 2)
            copies.append(
                send(
                    left.at[:, self.columns(place)],
                    slots.at[:, pl.ds(block * self.own, self.own)],
                    sems[0].at[block],
                    sems[1].at[block],
                    "seq",
                    self.partner(),
                )
            )
        return copies

    def cross(self, k, sems):
        right, slots = self.operands[k][2:4]
        return [send(right, slots, sems[0].at[0], sems[1].at[0], "seq", self.partner())]

    def send_pair(self, k, da):
        ss, rs = self.sems[0:2]
        grads, peer = self.grads[k], self.place(0, 0)
        return send(grads[1].at[da], grads[2].at[da], ss.at[k, da], rs.at[k, da], "seq", peer)

    def send_far(self, k, da):
        ss, rs = self.sems[2:4]
        grads, peer = self.grads[k], self.place(da, 1)
        return send(grads[3].at[da], grads[4].at[da], ss.at[k, da], rs.at[k, da], "seq", peer)

    def column(self, k, da, side):
        left, left_other, right, right_other = self.operands[k]
        _, second = self.mine()
        second = second if side == 1 else 1 - second
        block = 2 * lax.rem(self.a + da, self.quarter) + second
        found = tn(left[:, self.columns(self.place(da, side))], right[...])
        return found + tn(left_other[:, self.columns(block)], right_other[...])

    def pair(self, far):
        def step(k, da):
            self.grads[k][1][da] = self.column(k, da, 0).astype(bf16)
            self.send_pair(k, da).start()

        self.loop(*self.span(far), step)

    def both(self, k, da):
        found = self.column(k, da, 1)
        self.send_pair(k, da).wait()
        return found + self.grads[k][2][da].astype(f32)

    def far(self):
        def step(k, da):
            self.grads[k][3][da] = self.both(k, da).astype(bf16)
            self.send_far(k, da).start()

        self.loop(*self.span(True), step)

    def settle(self, outs):
        for k, out in enumerate(outs):
            out[...] = self.both(k, 0)

        def step(k, da):
            self.send_far(k, da).wait()
            outs[k][...] += self.grads[k][4][da].astype(f32)

        self.loop(*self.span(True), step)

    @staticmethod
    def scratch(shapes, parts):
        quarter = parts // 4
        slots = []
        for rows, columns in shapes:
            slots += [pltpu.VMEM((quarter, rows // parts, columns), bf16)] * 4
        return slots, [pltpu.SemaphoreType.DMA((len(shapes), quarter))] * 4


class Product:
    def __init__(self, r, name, left, right, parts, first, left_other=None, right_other=None):
        self.left, self.right = left, right
        self.joined = left.shape[1] // parts % 128 == 0

        def own(part):
            return getattr(r, f"{name}_{part}")

        if self.joined:
            left_slots = own("left") if left_other is None else left_other
            right_slots = own("right") if right_other is None else right_other
            grads = (left, left_slots, right, right_slots, *(own(i) for i in range(4)))
            self.sum = JoinedSum([grads], [own(f"sem_{i}") for i in range(4)], parts, first)
            self.lefts, self.rights = [], []
            if left_other is None:
                self.lefts = self.sum.cross_blocks(0, (own("left_ss"), own("left_rs")))
            if right_other is None:
                self.rights = self.sum.cross(0, (own("right_ss"), own("right_rs")))
        else:
            self.whole = own("whole")
            grads = (self.whole, *(own(i) for i in range(5)))
            self.sum = ScatterSum([grads], [own(f"sem_{i}") for i in range(6)], parts)
        self.pair, self.far = self.sum.pair, self.sum.far

    def begin_left(self):
        if self.joined:
            for copy in self.lefts:
                copy.start()

    def begin(self):
        if self.joined:
            for copy in self.rights:
                copy.start()
        else:
            for b in range(self.left.shape[1] // 256):
                block = slice(256 * b, 256 * b + 256)
                self.whole[block, :] = tn(self.left[:, block], self.right[...]).astype(bf16)
            self.sum.start_one(0)

    def ready(self):
        if self.joined:
            for copy in self.lefts + self.rights:
                copy.wait()

    def settle(self, out):
        self.sum.settle((out,))

    @staticmethod
    def scratch(name, count, model, columns, parts, left=True, right=True):
        own, dma = model // parts, pltpu.SemaphoreType.DMA
        found = {}
        if own % 128 == 0:
            slots, sems = JoinedSum.scratch([(model, columns)], parts)
            if left:
                found["left"] = pltpu.VMEM((count, model // 2), bf16)
                found |= {f"left_{end}": dma((parts // 2,)) for end in ("ss", "rs")}
            if right:
                found["right"] = pltpu.VMEM((count, columns), bf16)
                found |= {f"right_{end}": dma((1,)) for end in ("ss", "rs")}
        else:
            slots, sems = ScatterSum.scratch([(model, columns)], parts)
            found["whole"] = pltpu.VMEM((model, columns), bf16)
        found |= {str(i): s for i, s in enumerate(slots)}
        found |= {f"sem_{i}": s for i, s in enumerate(sems)}
        return {f"{name}_{part}": spec for part, spec in found.items()}


def layer_kernel(*refs, names, parts, peers, scale):
    r = types.SimpleNamespace(**dict(zip(names, refs, strict=True)))
    count, width = r.q.shape
    span, model = r.pair.shape[1], r.inputs.shape[1]
    per = r.tok.shape[2]
    half = parts // 2
    me = lax.axis_index("seq")
    x, z = lax.rem(me, 2), me // 2
    partner = me + 1 - 2 * x

    def at(o, c):
        return 2 * o + (x if c == 0 else 1 - x)

    def reader(c, dz):
        return at(lax.rem(z + half - dz, half), c)

    held = Held(((r.q_all_hbm, r.q_all, r.q_sem), (r.rows_hbm, r.rows, r.rows_sem)), parts)
    held.ahead()

    def fetch(i):
        name = FETCHED[i]
        return pltpu.make_async_copy(
            getattr(r, name + "_hbm"), getattr(r, name), r.fetch_sem.at[i]
        )

    def fetch_late(i):
        place = r.w_up.at[:, pl.ds(i * width, width)]
        return pltpu.make_async_copy(
            getattr(r, LATE[i] + "_hbm"), place, r.fetch_sem.at[len(FETCHED) + i]
        )

    for i in range(len(FETCHED)):
        fetch(i).start()

    def head_sum(name, slots, source, full):
        return HeadSum(
            source,
            [getattr(r, f"{slots}_{i}") for i in range(3)],
            [getattr(r, f"{name}_sem_{i}") for i in range(4)],
            full,
            [getattr(r, f"{name}_full_{i}") for i in range(2)],
        )

    sums = head_sum("sum", "turn", r.partial, r.branch)
    feeds = head_sum("feed", "feed", r.feed_in, r.layer)
    attn = head_sum("attn", "turn", r.partial, r.normed_two)
    cot_other = getattr(r, "cot_other", None)
    normed_other = getattr(r, "normed_other", None)
    mixed_other = getattr(r, "mixed_other", None)
    p_down = Product(r, "down", r.cot, r.hidden, parts, "z", left_other=cot_other)
    p_up = Product(r, "up", r.normed_two, r.grad_upward, parts, "x")
    p_o = Product(r, "o", r.branch, r.mixed, parts, "x", right_other=mixed_other)
    p_kv = Product(r, "kv", r.normed, r.d_kv, parts, "x", left_other=normed_other)
    p_q = Product(r, "q", r.normed, r.d_q, parts, "x", left_other=normed_other)
    ids = lax.broadcasted_iota(jnp.int32, (count, per), 0)

    own_pair = [
        pltpu.make_async_copy(source, r.pair.at[i, pl.ds(W, count)], r.own_sem.at[i])
        for i, source in enumerate((r.k_hbm, r.v_hbm))
    ]
    for copy in own_pair:
        copy.start()
    @pl.when(z == 0)
    def _():
        r.pair[:, :count] = jnp.zeros_like(r.pair[:, :count])

    @pl.when(me == 0)
    def _():
        r.pair[:, count:W] = jnp.zeros_like(r.pair[:, count:W])


    for copy in own_pair:
        copy.wait()
    greet(seq=parts, head=peers)

    def pair_rows(first):
        return r.pair.at[:, pl.ds(first, count)]

    def hand_on(i, source, target, peer):
        return send(
            pair_rows(source), pair_rows(target), r.next_ss.at[i], r.next_rs.at[i], "seq", peer
        )

    next_one = hand_on(0, W, count, partner)
    next_two = hand_on(1, W, 0, me + 2)
    passed_on = hand_on(2, 0, count, partner)

    @pl.when(z < half - 1)
    def _():
        next_two.start()

    @pl.when(x == 0)
    def _():
        next_one.start()

    def recall_part(j):
        q_at, rows_at = held.get(j)
        outs, logs = [], []
        for h in range(2):
            cols = head_cols(h)
            keep = r.tok[j, h : h + 1, :] == ids
            s = jnp.where(keep, nt(q_at[:, cols], rows_at[h, :, 0:128]), NEG)
            top = jnp.max(s, axis=1, keepdims=True)
            p = jnp.exp((s - top) * scale)
            total = jnp.sum(p, axis=1, keepdims=True)
            some = top > 0.5 * NEG
            outs.append(
                nn(p.astype(bf16), rows_at[h, :, 128:256]) * jnp.where(some, 1.0 / total, 0.0)
            )
            logs.append(jnp.where(some, top * scale + jnp.log(total), NEG))
        return outs, logs

    def out_x(dz):
        return (
            send(r.log_xs.at[dz], r.log_xr.at[dz], r.lx_ss.at[dz], r.lx_rs.at[dz], "seq", partner),
            send(r.dq_xs.at[dz], r.dq_xr.at[dz], r.ox_ss.at[dz], r.ox_rs.at[dz], "seq", partner),
        )

    def log_z(dz):
        return send(
            r.log_zs.at[dz], r.log_zr.at[dz], r.lz_ss.at[dz], r.lz_rs.at[dz], "seq", reader(0, dz)
        )

    def out_z(dz):
        return send(
            r.dq_zs.at[dz], r.dq_zr.at[dz], r.oz_ss.at[dz], r.oz_rs.at[dz], "seq", reader(0, dz)
        )

    def lend(dz):
        outs, logs = recall_part(reader(1, dz))
        for h in range(2):
            r.dq_xs[dz, h] = outs[h].astype(bf16)
        r.log_xs[dz] = row_form(logs, count).T[0:8]
        for copy in out_x(dz):
            copy.start()

    def unite(outs, logs, dz):
        for copy in out_x(dz):
            copy.wait()
        other = r.log_xr[dz].T
        joined = []
        for h in range(2):
            theirs = other[:, h : h + 1]
            top = jnp.maximum(logs[h], theirs)
            a, b = jnp.exp(logs[h] - top), jnp.exp(theirs - top)
            total = a + b
            outs[h] = outs[h] * (a / total) + r.dq_xr[dz, h].astype(f32) * (b / total)
            joined.append(top + jnp.log(total))
        return outs, joined

    def lend_step(dz, carry):
        lend(dz)
        return carry

    lax.fori_loop(1, half, lend_step, 0)
    lend(0)

    @pl.when(z > 0)
    def _():
        hand_on(1, W, 0, partner).wait_recv()

        @pl.when(x == 1)
        def _():
            passed_on.start()

    def keep_step(dz, carry):
        outs, logs = recall_part(reader(0, dz))
        outs, logs = unite(outs, logs, dz)
        for h in range(2):
            r.dq_zs[dz, h] = outs[h].astype(bf16)
        r.log_zs[dz] = row_form(logs, count).T[0:8]
        log_z(dz).start()
        out_z(dz).start()
        return carry

    lax.fori_loop(1, half, keep_step, 0)
    outs, logs = recall_part(me)
    outs, logs = unite(outs, logs, 0)
    r.log_zr[0] = row_form(logs, count).T[0:8]
    for h in range(2):
        r.recalled[:, head_cols(h)] = outs[h]

    @pl.when(x == 0)
    def _():
        next_one.wait_send()

        @pl.when(z > 0)
        def _():
            passed_on.wait_recv()

    @pl.when(x == 1)
    def _():
        next_one.wait_recv()

        @pl.when(z > 0)
        def _():
            passed_on.wait_send()

    @pl.when(z < half - 1)
    def _():
        next_two.wait_send()

    first = me * count
    start = doc_starts(r.lengths, first, count)
    key_place = first - W + lax.broadcasted_iota(jnp.int32, (count, span), 1)
    seen = key_place >= start
    for h in range(2):
        cols = head_cols(h)
        bias = pltpu.roll(
            jnp.broadcast_to(r.bias[h : h + 1, :], (count, span)), 0, 1, stride=1, stride_axis=0
        )
        s = nt(r.q[:, cols], r.pair[0, :, cols]) * scale + bias
        s = jnp.where(seen, s, NEG)
        raised = jnp.exp(s - jnp.max(s, axis=1, keepdims=True))
        p = raised / jnp.sum(raised, axis=1, keepdims=True)
        r.p[h] = p
        r.local[:, cols] = nn(p.astype(bf16), r.pair[1, :, cols])

    def wait_log(dz, top):
        log_z(dz).wait()
        return jnp.maximum(top, r.log_zr[dz])

    top = lax.fori_loop(1, half, wait_log, r.log_zr[0])

    def add_to(dz, total):
        return total + jnp.exp(r.log_zr[dz] - top)

    logs = top + jnp.log(lax.fori_loop(0, half, add_to, jnp.zeros_like(top)))
    r.logs[...] = logs
    share = jnp.exp(r.log_zr[0] - logs).T
    for h in range(2):
        r.recalled[:, head_cols(h)] *= share[:, h : h + 1]

    def gather_out(dz, carry):
        share = jnp.exp(r.log_zr[dz] - logs).T
        out_z(dz).wait()
        for h in range(2):
            r.recalled[:, head_cols(h)] += share[:, h : h + 1] * r.dq_zr[dz, h].astype(f32)
        return carry

    lax.fori_loop(1, half, gather_out, 0)
    for h in range(2):
        cols = head_cols(h)
        gate = r.gate[h]
        mixed = gate * r.recalled[:, cols] + (1.0 - gate) * r.local[:, cols]
        r.mixed[:, cols] = mixed.astype(bf16)


    for i in range(len(FETCHED)):
        fetch(i).wait()
    for b in range(model // 256):
        block = slice(256 * b, 256 * b + 256)
        r.partial[:, block] = nn(r.mixed[...], r.w_o[:, block]).astype(bf16)
    attn.start()
    crossing = []
    if cot_other is not None:
        for name, first, left, other in (("cot", "z", r.cot, cot_other), ("normed", "x", r.normed, normed_other)):
            joined = JoinedSum([(left, other, left, left)], [None] * 4, parts, first)
            sems = getattr(r, f"{name}_ss"), getattr(r, f"{name}_rs")
            crossing += joined.cross_blocks(0, sems)
        joined = JoinedSum([(r.normed, r.normed, r.mixed, mixed_other)], [None] * 4, parts, "x")
        crossing += joined.cross(0, (r.mixed_ss, r.mixed_rs))
        for copy in crossing:
            copy.start()
    attn.relay()
    branch = attn.total()
    middle = r.inputs[attn.mine, :].astype(f32) + branch
    r.middle[...] = middle
    row_scale = lax.rsqrt(row_mean(middle * middle) + eps)
    hat = middle * row_scale
    attn.spread(hat * r.gain_two[...])
    r.small_send[17:18] = fold_sum(col_sum(branch * branch))
    attn.forward()
    attn.settle()

    p_up.begin_left()
    for b in range(r.hidden.shape[1] // 256):
        block = slice(256 * b, 256 * b + 256)
        up = nn(r.normed_two[...], r.w_up[:, block])
        square = up * up
        bent = jnp.tanh(GELU * (up + 0.044715 * up * square))
        rise = 0.5 * (1.0 + bent)
        r.hidden[:, block] = (up * rise).astype(bf16)
        steep = (0.5 * GELU) * up * (1.0 - bent * bent) * (1.0 + (3 * 0.044715) * square)
        r.slope[:, block] = rise + steep
    p_down.begin()
    for b in range(r.hidden.shape[1] // 256):
        block = slice(256 * b, 256 * b + 256)
        back = nt(r.cot[...], r.w_down[block, :])
        r.grad_upward[:, block] = (r.slope[:, block] * back).astype(bf16)
    p_up.begin()
    for b in range(model // 256):
        block = slice(256 * b, 256 * b + 256)
        r.partial[:, block] = nt(r.grad_upward[...], r.w_up[block, :]).astype(bf16)

    sums.start()
    for i in range(len(LATE)):
        fetch_late(i).start()
    sums.relay()
    for b in range(model // 256):
        block = slice(256 * b, 256 * b + 256)
        r.feed_in[:, block] = nn(r.hidden[...], r.w_down[:, block]).astype(bf16)
    feeds.start()
    grad_normed = sums.total()
    scaled = grad_normed * r.gain_two[...]
    grad_middle = r.cot[sums.mine, :].astype(f32) + row_scale * (
        scaled - hat * row_mean(scaled * hat)
    )
    sums.spread(grad_middle)
    r.grad_middle[...] = grad_middle
    r.small_send[8:16] = folded(col_sum(grad_normed * hat))
    feeds.relay()
    sums.forward()
    sums.settle()
    g_own = nt(r.branch[...], r.w_o[...]).astype(bf16)
    r.g_all[0, z] = g_own

    deltas = []
    for h in range(2):
        cols = head_cols(h)
        g = g_own[:, cols].astype(f32)
        r.small_send[19 + h : 20 + h] = col_sum(g * (r.recalled[:, cols] - r.local[:, cols]))
        both = jnp.sum(g * r.recalled[:, cols], axis=1, keepdims=True)
        deltas.append(both * r.gate[h])
    turned = row_form([jnp.zeros_like(deltas[0])] * 2 + deltas, count).T[0:8]
    row = lax.broadcasted_iota(jnp.int32, (8, count), 0)
    r.st_all[0, z] = jnp.where(row < 2, r.logs[...], turned)

    def ask(c, o, way, peer):
        return (
            send(
                r.st_all.at[0, o], r.st_all.at[c, o], r.st_ss.at[way, o], r.st_rs.at[c, o], "seq", peer
            ),
            send(r.g_all.at[0, o], r.g_all.at[c, o], r.g_ss.at[way, o], r.g_rs.at[c, o], "seq", peer),
        )

    def start(copies):
        for copy in copies:
            copy.start()

    def up(o):
        return ask(0, o, 0, me + 2)

    def down(o):
        return ask(0, o, 1, me - 2)

    def across(o):
        return ask(1, o, 2, partner)

    def arrived(c, o):
        for copy in ask(c, o, 2, partner):
            copy.wait_recv()

    def sent(copies):
        for copy in copies:
            copy.wait_send()

    @pl.when(z < half - 1)
    def _():
        start(up(z))

    @pl.when(z > 0)
    def _():
        start(down(z))

    start(across(z))
    for copy in crossing:
        copy.wait_recv()
    p_down.ready()
    p_down.pair(True)

    for h in range(2):
        cols = head_cols(h)
        rest = 1.0 - r.gate[h]
        g = r.g_all[0, z, :, cols]
        p = r.p[h]
        e = nt(g, r.pair[1, :, cols])
        delta = jnp.sum(p * e, axis=1, keepdims=True)
        ds = (p * ((e - delta) * rest)).astype(bf16)
        r.dq_sum[:, cols] = nn(ds, r.pair[0, :, cols]) * scale
        dk = tn(ds, r.q[:, cols]) * scale
        dv = tn(p.astype(bf16), g) * rest
        r.pair_sum[0, :, cols] = dk[W:]
        r.pair_sum[1, :, cols] = dv[W:]
        r.pair_send[0, :, cols] = dk[:W].astype(bf16)
        r.pair_send[1, :, cols] = dv[:W].astype(bf16)
        low = ds.astype(f32)
        acc = low[0:8]
        for a in range(1, count // 8):
            acc = acc + pltpu.roll(low[8 * a : 8 * a + 8], (span - 8 * a) % span, 1)
        line = acc[0:1]
        for b in range(1, 8):
            line = line + pltpu.roll(acc[b : b + 1], span - b, 1)
        lines = span // 128
        for i in range(lines):
            r.small_send[24 + h * lines + i : 25 + h * lines + i] = line[:, 128 * i : 128 * i + 128]

    halo_x = send(
        r.pair_send.at[:, pl.ds(count, count)], r.halo_x, r.halo_ss.at[0], r.halo_rs.at[0], "seq", partner
    )
    halo_z = send(r.halo_send, r.halo_z, r.halo_ss.at[1], r.halo_rs.at[1], "seq", me - 2)

    def owner_part(c, o):
        j = at(o, c)
        q_at, rows_at = held.get(j, again=True)
        stats = r.st_all[c, o].T
        found = []
        for h in range(2):
            cols = head_cols(h)
            keep = r.tok[j, h : h + 1, :] == ids
            s = nt(q_at[:, cols], rows_at[h, :, 0:128]) * scale
            p = jnp.exp(jnp.where(keep, s - stats[:, h : h + 1], NEG))
            e = nt(r.g_all[c, o, :, cols], rows_at[h, :, 128:256]) * r.gate[h]
            ds = (p * (e - stats[:, 2 + h : 3 + h])).astype(bf16)
            found.append(nn(ds, rows_at[h, :, 0:128]) * scale)
        return found

    own = owner_part(0, z)
    for h in range(2):
        r.dq_sum[:, head_cols(h)] += own[h]

    def give_x(o):
        return send(r.dq_xs.at[o], r.dq_xr.at[o], r.dx_ss.at[o], r.dx_rs.at[o], "seq", partner)

    def give_z(o):
        return send(r.dq_zs.at[o], r.dq_zr.at[z], r.dz_ss.at[o], r.dz_rs.at[z], "seq", at(o, 0))

    def got_z(o):
        return send(r.dq_zs.at[o], r.dq_zr.at[o], r.dz_ss.at[o], r.dz_rs.at[o], "seq", partner)

    def neighbour(o):
        arrived(1, o)
        found = owner_part(1, o)
        for h in range(2):
            r.dq_xs[o, h] = found[h].astype(bf16)
        give_x(o).start()

    def column(o):
        found = owner_part(0, o)
        for h in range(2):
            r.dq_zs[o, h] = found[h].astype(bf16)

    def near(body):
        def step(t, carry):
            @pl.when(z - t >= 0)
            def _():
                body(z - t, True)

            @pl.when(z + t < half)
            def _():
                body(z + t, False)

            return carry

        lax.fori_loop(1, half, step, 0)

    neighbour(z)

    def relay(o, below):
        arrived(0, o)
        start(across(o))
        if below:

            @pl.when(z < half - 1)
            def _():
                start(up(o))

        else:

            @pl.when(z > 0)
            def _():
                start(down(o))

    def relay_step(t, carry):
        @pl.when(z - t >= 0)
        def _():
            relay(z - t, True)

        @pl.when(z + t < half)
        def _():
            relay(z + t, False)

        @pl.when(z - t >= 0)
        def _():
            column(z - t)

        @pl.when(z + t < half)
        def _():
            column(z + t)

        return carry

    lax.fori_loop(1, half, relay_step, 0)
    p_up.ready()
    p_up.pair(True)
    feed_sum = feeds.total()
    layer = r.middle[...] + feed_sum
    feeds.spread(layer)
    r.small_send[16:17] = fold_sum(col_sum(layer * layer))
    r.small_send[18:19] = fold_sum(col_sum(feed_sum * feed_sum))
    near(lambda o, below: neighbour(o))
    halo_x.start()
    p_o.begin_left()
    p_o.begin()

    def join(o, below):
        give_x(o).wait()
        for h in range(2):
            both = r.dq_zs[o, h].astype(f32) + r.dq_xr[o, h].astype(f32)
            r.dq_zs[o, h] = both.astype(bf16)
        give_z(o).start()

    near(join)
    halo_x.wait()
    passing = x.astype(f32)
    r.halo_send[...] = (
        r.pair_send[:, :count].astype(f32) + r.halo_x[...].astype(f32) * passing
    ).astype(bf16)
    r.pair_sum[...] += r.halo_x[...].astype(f32) * (1.0 - passing)

    @pl.when(z > 0)
    def _():
        halo_z.start()

    feeds.forward()
    give_x(z).wait()
    for h in range(2):
        r.dq_sum[:, head_cols(h)] += r.dq_xr[z, h].astype(f32)

    def merge(o, below):
        got_z(o).wait_recv()
        for h in range(2):
            r.dq_sum[:, head_cols(h)] += r.dq_zr[o, h].astype(f32)

    near(merge)
    p_up.pair(False)
    p_down.pair(False)

    r.d_q[...] = r.dq_sum[...].astype(bf16)
    p_q.begin()
    p_down.far()
    p_up.far()
    @pl.when(z > 0)
    def _():
        halo_z.wait_send()

    @pl.when(z < half - 1)
    def _():
        send(r.halo_send, r.halo_z, r.halo_ss.at[1], r.halo_rs.at[1], "seq", partner).wait_recv()
        r.pair_sum[...] += r.halo_z[...].astype(f32)

    r.d_kv[:, :width] = r.pair_sum[0].astype(bf16)
    r.d_kv[:, width:] = r.pair_sum[1].astype(bf16)
    p_kv.begin()
    for i in range(len(LATE)):
        fetch_late(i).wait()
    for b in range(model // 256):
        block = slice(256 * b, 256 * b + 256)
        r.partial[:, block] = (
            nt(r.d_q[...], r.w_up[block, :width])
            + nt(r.d_kv[...], r.w_up[block, width : 3 * width])
        ).astype(bf16)
    backs = head_sum("back", "turn", r.partial, r.input_grad)
    backs.start()
    backs.relay()
    p_o.ready()
    p_o.pair(True)
    p_kv.ready()
    p_kv.pair(True)
    tokens = r.inputs[backs.mine, :].astype(f32)
    in_scale = lax.rsqrt(row_mean(tokens * tokens) + eps)
    in_hat = tokens * in_scale
    back_sum = backs.total()
    g = back_sum * r.gain_one[...]
    backs.spread(r.grad_middle[...] + in_scale * (g - in_hat * row_mean(g * in_hat)))
    r.small_send[0:8] = folded(col_sum(back_sum * in_hat))
    r.small_send[21:24] = jnp.zeros((3, 128), f32)
    r.small_send[36:40] = jnp.zeros((4, 128), f32)

    def small_heads(d):
        peer = lax.rem(lax.axis_index("head") + d, peers)
        return send(r.small_send, r.small_head.at[d], r.sh_ss.at[d], r.sh_rs.at[d], "head", peer)

    for d in range(1, peers):
        small_heads(d).start()
    p_q.ready()
    p_q.pair(True)
    backs.forward()
    p_o.far()
    p_kv.far()

    kept = lax.broadcasted_iota(jnp.int32, r.small_send.shape, 0) < 19
    found = r.small_send[...]
    for d in range(1, peers):
        small_heads(d).wait()
        found = found + jnp.where(kept, r.small_head[d], 0.0)
    r.small_seq[0] = found

    def small_seqs(d):
        peer = lax.rem(me + d, parts)
        return send(r.small_seq.at[0], r.small_seq.at[d], r.sq_ss.at[d], r.sq_rs.at[d], "seq", peer)

    def small_start(d, carry):
        small_seqs(d).start()
        return carry

    lax.fori_loop(1, parts, small_start, 0)
    p_o.pair(False)
    p_kv.pair(False)
    p_q.far()
    p_q.pair(False)
    p_down.settle(r.down_sum)
    r.down_out[...] = r.down_sum[...].T
    p_up.settle(r.up_out)
    p_o.settle(r.o_sum)
    p_kv.settle(r.kv_sum)
    r.k_out[...] = r.kv_sum[:, :width]
    r.v_out[...] = r.kv_sum[:, width:]
    r.o_out[...] = r.o_sum[...].T
    p_q.settle(r.q_out)
    r.small[...] = r.small_seq[0]

    def small_add(d, carry):
        small_seqs(d).wait()
        r.small[...] += r.small_seq[d]
        return carry

    lax.fori_loop(1, parts, small_add, 0)
    feeds.settle()
    backs.settle()

    sent(across(z))

    @pl.when(z < half - 1)
    def _():
        sent(up(z))

    @pl.when(z > 0)
    def _():
        sent(down(z))

    def drain(o, below):
        sent(across(o))
        give_z(o).wait_send()
        if below:

            @pl.when(z < half - 1)
            def _():
                sent(up(o))

        else:

            @pl.when(z > 0)
            def _():
                sent(down(o))

    near(drain)
    for copy in crossing:
        copy.wait_send()


FETCHED = ("cot", "w_o", "w_up", "w_down")
LATE = ("w_q", "w_k", "w_v")
GELU = math.sqrt(2 / math.pi)


def layer(inputs, parts, peers):
    count, width = inputs["q"].shape
    model, span = inputs["inputs"].shape[1], W + count
    half, own = parts // 2, model // parts
    smem = pl.BlockSpec(memory_space=pltpu.SMEM)
    vmem = pl.BlockSpec(memory_space=pltpu.VMEM)
    hbm = pl.BlockSpec(memory_space=pltpu.HBM)
    dma = pltpu.SemaphoreType.DMA
    wide = inputs["w_up_hbm"].shape[1]
    outputs = dict(
        input_grad=((count, model), bf16),
        layer=((count, model), bf16),
        q_out=((own, width), f32),
        k_out=((own, width), f32),
        v_out=((own, width), f32),
        o_out=((width, own), f32),
        up_out=((own, wide), f32),
        down_out=((wide, own), f32),
        small=((40, 128), f32),
    )
    outputs = {name: jax.ShapeDtypeStruct(*spec) for name, spec in outputs.items()}
    held = Held.scratch((inputs["q_all_hbm"], inputs["rows_hbm"]), parts)
    scratch = dict(zip(("q_all", "rows", "q_sem", "rows_sem"), held, strict=True))
    scratch |= {name: pltpu.VMEM(inputs[name + "_hbm"].shape, bf16) for name in FETCHED}
    for name, spec in dict(
        recalled=((count, width), f32),
        local=((count, width), f32),
        mixed=((count, width), bf16),
        logs=((8, count), f32),
        p=((2, count, span), f32),
        pair=((2, span, width), bf16),
        log_xs=((half, 8, count), f32),
        log_xr=((half, 8, count), f32),
        log_zs=((half, 8, count), f32),
        log_zr=((half, 8, count), f32),
        normed_two=((count, model), bf16),
        middle=((count // peers, model), f32),
        hidden=((count, wide), bf16),
        slope=((count, wide), f32),
        grad_upward=((count, wide), bf16),
        partial=((count, model), bf16),
        feed_in=((count, model), bf16),
        branch=((count, model), bf16),
        grad_middle=((count // peers, model), f32),
        g_all=((2, half, count, width), bf16),
        st_all=((2, half, 8, count), f32),
        dq_xs=((half, 2, count, 128), bf16),
        dq_xr=((half, 2, count, 128), bf16),
        dq_zs=((half, 2, count, 128), bf16),
        dq_zr=((half, 2, count, 128), bf16),
        pair_send=((2, W, width), bf16),
        pair_sum=((2, count, width), f32),
        halo_x=((2, count, width), bf16),
        halo_send=((2, count, width), bf16),
        halo_z=((2, count, width), bf16),
        dq_sum=((count, width), f32),
        d_kv=((count, 2 * width), bf16),
        d_q=((count, width), bf16),
        kv_sum=((own, 2 * width), f32),
        o_sum=((own, width), f32),
        down_sum=((own, wide), f32),
        small_send=((40, 128), f32),
        small_head=((peers, 40, 128), f32),
        small_seq=((parts, 40, 128), f32),
    ).items():
        scratch[name] = pltpu.VMEM(*spec)
    for name, shape in dict(
        fetch_sem=(len(FETCHED) + len(LATE),),
        own_sem=(2,),
        next_ss=(3,),
        next_rs=(3,),
        ox_ss=(half,),
        ox_rs=(half,),
        oz_ss=(half,),
        oz_rs=(half,),
        lx_ss=(half,),
        lx_rs=(half,),
        lz_ss=(half,),
        lz_rs=(half,),
        st_ss=(3, half),
        st_rs=(2, half),
        g_ss=(3, half),
        g_rs=(2, half),
        dx_ss=(half,),
        dx_rs=(half,),
        dz_ss=(half,),
        dz_rs=(half,),
        halo_ss=(2,),
        halo_rs=(2,),
        sh_ss=(peers,),
        sh_rs=(peers,),
        sq_ss=(parts,),
        sq_rs=(parts,),
    ).items():
        scratch[name] = dma(shape)
    for name in ("turn", "feed"):
        scratch |= {f"{name}_{i}": s for i, s in enumerate(HeadSum.scratch(count, model))}
    for name in ("attn", "sum", "feed", "back"):
        scratch |= {f"{name}_sem_{i}": s for i, s in enumerate(HeadSum.sems())}
        scratch |= {f"{name}_full_{i}": s for i, s in enumerate(HeadSum.full_scratch())}
    if own % 128 == 0:
        for name in ("cot", "normed"):
            scratch[f"{name}_other"] = pltpu.VMEM((count, model // 2), bf16)
            scratch |= {f"{name}_{end}": dma((half,)) for end in ("ss", "rs")}
        scratch["mixed_other"] = pltpu.VMEM((count, width), bf16)
        scratch |= {f"mixed_{end}": dma((1,)) for end in ("ss", "rs")}
    for name, columns, left, right in (
        ("down", wide, False, True),
        ("up", wide, True, True),
        ("o", width, True, False),
        ("kv", 2 * width, False, True),
        ("q", width, False, True),
    ):
        scratch |= Product.scratch(name, count, model, columns, parts, left, right)
    spaces = dict(gate=smem, lengths=smem)
    spaces |= {name: hbm for name in inputs if name.endswith("_hbm")}
    found = pl.pallas_call(
        functools.partial(
            layer_kernel,
            names=(*inputs, *outputs, *scratch),
            parts=parts,
            peers=peers,
            scale=128**-0.5,
        ),
        out_shape=tuple(outputs.values()),
        in_specs=[spaces.get(name, vmem) for name in inputs],
        out_specs=(vmem,) * len(outputs),
        scratch_shapes=list(scratch.values()),
        compiler_params=pltpu.CompilerParams(
            vmem_limit_bytes=(58 if parts <= 8 else 63) * MIB, collective_id=2, has_side_effects=True
        ),
        cost_estimate=pl.CostEstimate(
            flops=4 * 10**9, bytes_accessed=150 * MIB, transcendentals=5 * 10**6
        ),
        name="layer",
    )(*inputs.values())
    return dict(zip(outputs, found, strict=True))


def hand_out_kernel(*refs, copied, entries):
    count = len(copied)
    sources, (input_grad, small, gate, hot), outs = refs[:count], refs[count : count + 4], refs[count + 4 :]
    grad_out, one_out, two_out, position_out, gate_out, rms_out = outs[count : count + 6]
    for source, out in zip(sources, outs):
        out[...] = source[...]
    grad_out[...] = input_grad[...].astype(f32)
    me = lax.axis_index("seq")
    if one_out.shape[0] == 1:
        one_out[...] = small[pl.ds(me, 1), :]
        two_out[...] = small[pl.ds(me + 8, 1), :]
    else:
        one_out[...] = small[0:8, :]
        two_out[...] = small[8:16, :]
    lines = hot.shape[0] // 128
    for h in range(2):
        found = jnp.zeros((1, hot.shape[1]), f32)
        for i in range(lines):
            line = small[24 + h * lines + i : 25 + h * lines + i, :]
            found = found + lax.dot_general(
                line,
                hot[128 * i : 128 * i + 128, :],
                (((1,), (0,)), ((), ())),
                precision=highest,
                preferred_element_type=f32,
            )
        position_out[h : h + 1, :] = found
    sums = jnp.sum(small[16:24, :], axis=1, keepdims=True)
    lane = lax.broadcasted_iota(jnp.int32, (1, 2), 1)
    steep = jnp.where(lane == 0, gate[0] * (1.0 - gate[0]), gate[1] * (1.0 - gate[1]))
    gate_out[...] = jnp.where(lane == 0, sums[3:4], sums[4:5]) * steep
    lane = lax.broadcasted_iota(jnp.int32, (1, 3), 1)
    squares = jnp.where(lane == 0, sums[0:1], jnp.where(lane == 1, sums[1:2], sums[2:3]))
    rms_out[...] = jnp.sqrt(squares / entries)


def hand_out(done, gate, hot, entries, parts):
    copied = ("layer", "q_out", "k_out", "v_out", "o_out", "up_out", "down_out")
    smem = pl.BlockSpec(memory_space=pltpu.SMEM)
    vmem = pl.BlockSpec(memory_space=pltpu.VMEM)
    model = done["input_grad"].shape[1]
    own = model // parts
    shapes = [jax.ShapeDtypeStruct(done[name].shape, done[name].dtype) for name in copied]
    shapes += [
        jax.ShapeDtypeStruct(shape, f32)
        for shape in (
            done["input_grad"].shape,
            *[(1 if own == 128 else 8, 128)] * 2,
            (2, hot.shape[1]),
            (1, 2),
            (1, 3),
        )
    ]
    found = pl.pallas_call(
        functools.partial(hand_out_kernel, copied=copied, entries=entries),
        out_shape=tuple(shapes),
        in_specs=[vmem] * len(copied) + [vmem, vmem, smem, vmem],
        out_specs=(vmem,) * (len(copied) + 6),
        compiler_params=pltpu.CompilerParams(vmem_limit_bytes=62 * MIB),
        name="hand_out",
    )(*(done[name] for name in copied), done["input_grad"], done["small"], gate, hot)
    named = dict(zip(copied, found))
    named |= dict(zip(("input_grad", "gain_one", "gain_two", "position", "gate", "rms"), found[len(copied) :]))
    return named


def norm_stats(values):
    row_scale = lax.rsqrt(jnp.mean(values * values, axis=-1, keepdims=True) + eps)
    return (values * row_scale, row_scale)


def per_device(
    inputs,
    cotangent,
    query_weight,
    key_weight,
    value_weight,
    output_weight,
    up_weight,
    down_weight,
    first_gain,
    second_gain,
    position_bias,
    gate_bias,
    memory_table,
    retrieved,
    lengths,
):
    _, block_len, model_width = inputs.shape
    bucket_total = position_bias.shape[1]
    seq_count = lax.axis_size("seq")
    slot_count = memory_table.shape[0]

    wanted = jnp.transpose(retrieved[0], (1, 0, 2))
    token = jnp.arange(block_len, dtype=jnp.int32)[None, :, None]
    codes = (wanted // slot_count) * (block_len * slot_count) + token * slot_count + wanted % slot_count
    codes = lax.sort(codes.reshape(2, -1), dimension=1, is_stable=False)
    hot, outside = diagonal_buckets(block_len, bucket_total)
    bias_row = jnp.dot(position_bias, hot, precision=highest) + outside[None]

    x, cot = inputs[0], cotangent[0]
    peers = lax.axis_size("head")
    gate_flat = jax.nn.sigmoid(gate_bias)
    hat_one, _ = norm_stats(x.astype(f32))
    normed_one = (hat_one * first_gain).astype(bf16)
    queries = nn(normed_one, query_weight).astype(bf16)
    places, tok, keys, values = request(
        codes, normed_one, key_weight, value_weight, seq_count, slot_count, block_len
    )
    rows = gather_rows(places, widen(memory_table))
    q_all = lax.all_gather(queries, "seq", axis=0)

    done = layer(
        dict(
            lengths=lengths[0],
            gate=gate_flat,
            q=queries,
            k_hbm=keys,
            v_hbm=values,
            bias=bias_row,
            tok=tok,
            inputs=x,
            normed=normed_one,
            gain_one=first_gain[None],
            gain_two=second_gain[None],
            q_all_hbm=q_all,
            rows_hbm=rows,
            cot_hbm=cot,
            w_o_hbm=output_weight,
            w_up_hbm=up_weight,
            w_down_hbm=down_weight,
            w_q_hbm=query_weight,
            w_k_hbm=key_weight,
            w_v_hbm=value_weight,
        ),
        seq_count,
        peers,
    )
    entries = float(block_len * model_width * seq_count)
    out = hand_out(done, gate_flat, jnp.asarray(hot.T), entries, seq_count)
    share = model_width // seq_count
    gains = [out["gain_one"].reshape(-1), out["gain_two"].reshape(-1)]
    if share != 128:
        start = lax.axis_index("seq") * share
        gains = [lax.dynamic_slice_in_dim(gain, start, share) for gain in gains]
    return (
        out["layer"][None],
        out["input_grad"][None],
        out["q_out"],
        out["k_out"],
        out["v_out"],
        out["o_out"],
        out["up_out"],
        out["down_out"],
        gains[0],
        gains[1],
        out["position"],
        out["gate"][0],
        out["rms"][0],
    )


def solution(mesh):
    in_specs = (
        P(None, "seq", None),
        P(None, "seq", None),
        P(None, "head"),
        P(None, "head"),
        P(None, "head"),
        P("head", None),
        P(None, "head"),
        P("head", None),
        P(),
        P(),
        P("head", None),
        P("head"),
        P("seq", "head", None),
        P(None, "seq", "head", None),
        P(),
    )
    out_specs = (
        P(None, "seq", None),
        P(None, "seq", None),
        P("seq", "head"),
        P("seq", "head"),
        P("seq", "head"),
        P("head", "seq"),
        P("seq", "head"),
        P("head", "seq"),
        P("seq"),
        P("seq"),
        P("head", None),
        P("head"),
        P(),
    )
    return jax.shard_map(
        per_device, mesh=mesh, in_specs=in_specs, out_specs=out_specs, check_vma=False
    )
```

```python
import functools
import math
import types

import jax
import jax.numpy as jnp
import numpy as np
from jax import lax
from jax.experimental import pallas as pl
from jax.experimental.pallas import tpu as pltpu
from jax.sharding import PartitionSpec as P

W = 512
eps = 1e-06
exact_span = 16
far_distance = 128
highest = lax.Precision.HIGHEST
f32 = jnp.float32
bf16 = jnp.bfloat16
NEG = -1e30
MIB = 2**20


def bucket_table(key_span, bucket_total):
    found = []
    for distance in range(key_span):
        if distance < exact_span:
            found.append(distance)
        else:
            scaled = math.log(distance / exact_span) / math.log(far_distance / exact_span)
            found.append(
                min(bucket_total - 1, exact_span + math.floor(scaled * (bucket_total - exact_span)))
            )
    return np.asarray(found)


def diagonal_buckets(block_len, bucket_total):
    span = W + block_len
    table = bucket_table(W, bucket_total)
    hot = np.zeros((bucket_total, span), np.float32)
    for u in range(1, W + 1):
        hot[table[W - u], u] = 1.0
    outside = np.where(hot.sum(0) > 0, 0.0, NEG).astype(np.float32)
    return hot, outside


def nt(a, b):
    return lax.dot_general(a, b, (((1,), (1,)), ((), ())), preferred_element_type=f32)


def nn(a, b):
    return lax.dot_general(a, b, (((1,), (0,)), ((), ())), preferred_element_type=f32)


def tn(a, b):
    return lax.dot_general(a, b, (((0,), (0,)), ((), ())), preferred_element_type=f32)


def widen_kernel(table_hbm, wide_hbm, buf, out, sem, out_sem, *, chunk, part):
    chunks = table_hbm.shape[0] // chunk

    def fetch(i):
        return pltpu.make_async_copy(
            table_hbm.at[pl.ds(i * chunk, chunk)], buf.at[i % 2], sem.at[i % 2]
        )

    def store(i):
        return pltpu.make_async_copy(
            out.at[i % 2], wide_hbm.at[:, pl.ds(2 * i * chunk, 2 * chunk)], out_sem.at[i % 2]
        )

    fetch(0).start()
    for i in range(chunks):
        fetch(i).wait()
        if i + 1 < chunks:
            fetch(i + 1).start()
        if i > 1:
            store(i - 2).wait()

        def widen(q, carry, i=i):
            x = buf[i % 2, pl.ds(q * part, part)].astype(f32)
            for r in range(part):
                for h in range(2):
                    place = pl.ds(2 * (q * part + r), 1)
                    out[i % 2, h, place, :] = x[r, h : h + 1, 0:128]
                    place = pl.ds(2 * (q * part + r) + 1, 1)
                    out[i % 2, h, place, :] = x[r, h : h + 1, 128:256]
            return carry

        lax.fori_loop(0, chunk // part, widen, 0)
        store(i).start()
    for i in range(max(0, chunks - 2), chunks):
        store(i).wait()


def widen(table):
    total = table.shape[0]
    chunk = min(1024, total)
    hbm = pl.BlockSpec(memory_space=pltpu.HBM)
    dma = pltpu.SemaphoreType.DMA
    return pl.pallas_call(
        functools.partial(widen_kernel, chunk=chunk, part=32),
        out_shape=jax.ShapeDtypeStruct((2, 2 * total, 128), f32),
        in_specs=[hbm],
        out_specs=hbm,
        scratch_shapes=[
            pltpu.VMEM((2, chunk, 2, 256), bf16),
            pltpu.VMEM((2, 2, 2 * chunk, 128), f32),
            dma((2,)),
            dma((2,)),
        ],
        compiler_params=pltpu.CompilerParams(vmem_limit_bytes=58 * MIB),
        cost_estimate=pl.CostEstimate(flops=0, bytes_accessed=40 * MIB, transcendentals=0),
        name="widen",
    )(table)


def gather_kernel(at_ref, wide_hbm, out_hbm, wide, buf, low, wide_sem, out_sem, *, unroll, group):
    parts, rows = out_hbm.shape[0], out_hbm.shape[2]

    def fetch(h):
        return pltpu.make_async_copy(wide_hbm.at[h], wide.at[h], wide_sem.at[h])

    def store(j, h, slot):
        return pltpu.make_async_copy(low.at[slot], out_hbm.at[j, h], out_sem.at[slot])

    for h in range(2):
        fetch(h).start()
    for h in range(2):
        fetch(h).wait()

        def one(j, carry, h=h):
            slot = lax.rem(j, 2)
            first = (2 * j + h) * rows

            def copy_rows(q, carry):
                base = q * unroll
                for g in range(0, unroll, group):
                    found = [
                        wide[h, pl.ds(at_ref[first + base + g + u], 2), :] for u in range(group)
                    ]
                    for u in range(group):
                        buf[pl.ds(2 * (base + g + u), 2), :] = found[u]
                return carry

            lax.fori_loop(0, rows // unroll, copy_rows, 0)

            if h == 0:

                @pl.when(j > 1)
                def _():
                    store(j, h, slot).wait()

            else:
                store(j, h, slot).wait()

            low[slot, :, 0:128] = buf[pl.ds(0, rows, 2), :].astype(bf16)
            low[slot, :, 128:256] = buf[pl.ds(1, rows, 2), :].astype(bf16)
            store(j, h, slot).start()
            return carry

        lax.fori_loop(0, parts, one, 0)
    store(0, 1, 0).wait()
    store(1, 1, 1).wait()


def gather_rows(places, wide, shape):
    parts, heads, rows = shape
    unroll = min(64, rows)
    hbm = pl.BlockSpec(memory_space=pltpu.HBM)
    dma = pltpu.SemaphoreType.DMA
    return pl.pallas_call(
        functools.partial(gather_kernel, unroll=unroll, group=unroll // 2),
        out_shape=jax.ShapeDtypeStruct((parts, heads, rows, 256), bf16),
        in_specs=[pl.BlockSpec(memory_space=pltpu.SMEM), hbm],
        out_specs=hbm,
        scratch_shapes=[
            pltpu.VMEM(wide.shape, f32),
            pltpu.VMEM((2 * rows, 128), f32),
            pltpu.VMEM((2, rows, 256), bf16),
            dma((2,)),
            dma((2,)),
        ],
        compiler_params=pltpu.CompilerParams(vmem_limit_bytes=58 * MIB),
        cost_estimate=pl.CostEstimate(flops=0, bytes_accessed=100 * MIB, transcendentals=0),
        name="gather_rows",
    )(places.reshape(-1), wide)


MESH = pl.DeviceIdType.MESH


def greet(meanwhile=None, **counts):
    barrier = pltpu.get_barrier_semaphore()
    for axis, count in counts.items():
        me = lax.axis_index(axis)

        def call(d, carry, axis=axis, count=count, me=me):
            peer = lax.rem(me + d, count)
            pl.semaphore_signal(barrier, inc=1, device_id={axis: peer}, device_id_type=MESH)
            return carry

        lax.fori_loop(1, count, call, 0)
    if meanwhile is not None:
        meanwhile()
    pl.semaphore_wait(barrier, sum(counts.values()) - len(counts))


def send(src, dst, send_sem, recv_sem, axis, peer):
    return pltpu.make_async_remote_copy(
        src_ref=src,
        dst_ref=dst,
        send_sem=send_sem,
        recv_sem=recv_sem,
        device_id={axis: peer},
        device_id_type=MESH,
    )


def doc_starts(lengths_ref, first, count):
    place = first + lax.broadcasted_iota(jnp.int32, (count, 1), 0)
    start = jnp.zeros((count, 1), jnp.int32)
    end = jnp.int32(0)
    for c in range(lengths_ref.shape[0]):
        end = end + lengths_ref[c]
        start = jnp.where(end <= place, end, start)
    return start


def head_cols(h):
    return slice(h * 128, h * 128 + 128)


def row_form(columns, count):
    lane = lax.broadcasted_iota(jnp.int32, (count, 128), 1)
    wide = jnp.zeros((count, 128), f32)
    for i, column in enumerate(columns):
        wide = jnp.where(lane == i, column, wide)
    return wide


def request_kernel(
    codes_ref,
    normed_ref,
    wk_ref,
    wv_ref,
    place_ref,
    tok_ref,
    k_ref,
    v_ref,
    got,
    own_sem,
    ss,
    rs,
    *,
    parts,
    slots,
    tokens,
):
    rows = codes_ref.shape[1] // parts
    me = lax.axis_index("seq")

    def part(owner):
        return codes_ref.at[:, pl.ds(pl.multiple_of(owner * rows, 128), rows)]

    keep = pltpu.make_async_copy(part(me), got.at[0], own_sem)
    keep.start()

    def project():
        k_ref[...] = nn(normed_ref[...], wk_ref[...]).astype(bf16)
        v_ref[...] = nn(normed_ref[...], wv_ref[...]).astype(bf16)

    greet(project, seq=parts)

    def ask(d):
        peer = lax.rem(me + d, parts)
        return send(part(peer), got.at[d], ss.at[d], rs.at[d], "seq", peer)

    def start(d, carry):
        ask(d).start()
        return carry

    lax.fori_loop(1, parts, start, 0)
    shift = slots.bit_length() - 1
    lines = rows // 128

    def read(d, j):
        code = got[d]
        for h in range(2):
            found = (code[h : h + 1] & (slots - 1)) * 2
            pieces = [found[:, 128 * i : 128 * i + 128] for i in range(lines)]
            at = pl.ds(pl.multiple_of((2 * j + h) * lines, lines), lines)
            place_ref[at, :] = jnp.concatenate(pieces, axis=0)
        tok_ref[j] = (code >> shift) & (tokens - 1)

    keep.wait()
    read(0, me)

    def arrive(d, carry):
        ask(d).wait()
        read(d, lax.rem(me + parts - d, parts))
        return carry

    lax.fori_loop(1, parts, arrive, 0)


def request(codes, normed, wk, wv, parts, slots, tokens):
    rows = codes.shape[1] // parts
    vmem = pl.BlockSpec(memory_space=pltpu.VMEM)
    dma = pltpu.SemaphoreType.DMA
    shape = (parts, 2, rows)
    return pl.pallas_call(
        functools.partial(request_kernel, parts=parts, slots=slots, tokens=tokens),
        out_shape=(
            jax.ShapeDtypeStruct((parts * 2 * rows // 128, 128), jnp.int32),
            jax.ShapeDtypeStruct(shape, jnp.int32),
        )
        + (jax.ShapeDtypeStruct((tokens, wk.shape[1]), bf16),) * 2,
        in_specs=[vmem] * 4,
        out_specs=(vmem,) * 4,
        scratch_shapes=[pltpu.VMEM(shape, jnp.int32), dma, dma((parts,)), dma((parts,))],
        compiler_params=pltpu.CompilerParams(
            vmem_limit_bytes=16 * MIB, collective_id=6, has_side_effects=True
        ),
        name="request",
    )(codes, normed, wk, wv)


class HeadSum:
    def __init__(self, src, scratch, sems, full=None, full_sems=None):
        self.src, self.full = src, full
        self.core_recv, self.side_send, self.side_recv = scratch
        self.core_ss, self.core_rs, self.side_ss, self.side_rs = sems
        self.full_sems = full_sems
        head = lax.axis_index("head")
        self.y, self.c = head // 2, lax.rem(head, 2)
        self.share = src.shape[0] // 4
        self.core = 2 * self.y + 1 - self.c
        self.side = 2 * (1 - self.y) + self.c
        self.mine = self.rows_of(head)

    def rows_of(self, place):
        return pl.ds(pl.multiple_of(place * self.share, self.share), self.share)

    def to_core(self, i):
        y = self.y if i == 0 else 1 - self.y
        src = self.src.at[self.rows_of(2 * y + 1 - self.c)]
        return send(src, self.core_recv.at[i], self.core_ss.at[i], self.core_rs.at[i], "head", self.core)

    def to_side(self):
        return send(self.side_send, self.side_recv, self.side_ss, self.side_rs, "head", self.side)

    def start(self):
        self.to_core(1).start()
        self.to_core(0).start()

    def relay(self):
        self.to_core(1).wait()
        other = self.src[self.rows_of(self.side), :].astype(f32)
        self.side_send[...] = (other + self.core_recv[1].astype(f32)).astype(bf16)
        self.to_side().start()

    def total(self):
        self.to_core(0).wait()
        found = self.src[self.mine, :].astype(f32) + self.core_recv[0].astype(f32)
        self.to_side().wait()
        return found + self.side_recv[...].astype(f32)

    def back(self, i):
        rows = self.rows_of(self.side) if i == 2 else self.mine
        peer = self.side if i == 1 else self.core
        ss, rs = self.full_sems
        return send(self.full.at[rows], self.full.at[rows], ss.at[i], rs.at[i], "head", peer)

    def spread(self, value):
        self.full[self.mine, :] = value.astype(self.full.dtype)
        self.back(1).start()
        self.back(0).start()

    def forward(self):
        self.back(1).wait()
        self.back(2).start()

    def settle(self):
        self.back(0).wait()
        self.back(2).wait()

    @staticmethod
    def scratch(count, width):
        piece = (count // 4, width)
        return [pltpu.VMEM((2,) + piece, bf16), pltpu.VMEM(piece, bf16), pltpu.VMEM(piece, bf16)]

    @staticmethod
    def sems():
        dma = pltpu.SemaphoreType.DMA
        return [dma((2,)), dma((2,)), dma, dma]

    @staticmethod
    def full_scratch():
        return [pltpu.SemaphoreType.DMA((3,))] * 2


class Held:
    def __init__(self, arrays, parts):
        self.arrays, self.parts = arrays, parts
        self.all = arrays[0][1].shape[0] == parts

    def fetch(self, i, j):
        hbm, place, sem = self.arrays[i]
        slot = j if self.all else 0
        return pltpu.make_async_copy(hbm.at[j], place.at[slot], sem.at[slot])

    def ahead(self):
        if self.all:

            def start(j, carry):
                for i in range(len(self.arrays)):
                    self.fetch(i, j).start()
                return carry

            lax.fori_loop(0, self.parts, start, 0)

    def get(self, j, again=False):
        for i in range(len(self.arrays)):
            if not self.all:
                self.fetch(i, j).start()
            if not (self.all and again):
                self.fetch(i, j).wait()
        return [place.at[j if self.all else 0] for _, place, _ in self.arrays]

    @staticmethod
    def scratch(arrays, parts):
        slots = parts if parts <= 8 else 1
        places = [pltpu.VMEM((slots,) + a.shape[1:], a.dtype) for a in arrays]
        return places + [pltpu.SemaphoreType.DMA((slots,))] * len(arrays)


class ScatterSum:
    def __init__(self, grads, sems, parts):
        self.grads, self.sems = grads, sems
        self.quarter = parts // 4
        self.own = grads[0][0].shape[0] // parts
        me = lax.axis_index("seq")
        self.x, self.b, self.a = lax.rem(me, 2), lax.rem(me // 2, 2), me // 4

    def place(self, da, side, x):
        b = self.b if side == 1 else 1 - self.b
        return 4 * lax.rem(self.a + da, self.quarter) + 2 * b + x

    def rows_of(self, place):
        return pl.ds(pl.multiple_of(place * self.own, self.own), self.own)

    def send_x(self, k, da, side):
        ss, rs = self.sems[0:2]
        return send(
            self.grads[k][0].at[self.rows_of(self.place(da, side, 1 - self.x))],
            self.grads[k][1].at[side, da],
            ss.at[k, side, da],
            rs.at[k, side, da],
            "seq",
            self.place(0, 1, 1 - self.x),
        )

    def send_pair(self, k, da):
        ss, rs = self.sems[2:4]
        grads, peer = self.grads[k], self.place(0, 0, self.x)
        return send(grads[2].at[da], grads[3].at[da], ss.at[k, da], rs.at[k, da], "seq", peer)

    def send_far(self, k, da):
        ss, rs = self.sems[4:6]
        grads, peer = self.grads[k], self.place(da, 1, self.x)
        return send(grads[4].at[da], grads[5].at[da], ss.at[k, da], rs.at[k, da], "seq", peer)

    def loop(self, first, last, step):
        def body(da, carry):
            for k in range(len(self.grads)):
                step(k, da)
            return carry

        lax.fori_loop(first, last, body, 0)

    def span(self, far):
        return (1, self.quarter) if far else (0, 1)

    def start(self, far, side):
        self.loop(*self.span(far), lambda k, da: self.send_x(k, da, side).start())

    def start_one(self, k):
        for far in (True, False):
            for side in range(2):

                def body(da, carry, side=side):
                    self.send_x(k, da, side).start()
                    return carry

                lax.fori_loop(*self.span(far), body, 0)

    def column(self, k, da, side):
        self.send_x(k, da, side).wait()
        mine = self.grads[k][0][self.rows_of(self.place(da, side, self.x)), :]
        return mine.astype(f32) + self.grads[k][1][side, da].astype(f32)

    def pair(self, far):
        def step(k, da):
            self.grads[k][2][da] = self.column(k, da, 0).astype(bf16)
            self.send_pair(k, da).start()

        self.loop(*self.span(far), step)

    def both(self, k, da):
        found = self.column(k, da, 1)
        self.send_pair(k, da).wait()
        return found + self.grads[k][3][da].astype(f32)

    def far(self):
        def step(k, da):
            self.grads[k][4][da] = self.both(k, da).astype(bf16)
            self.send_far(k, da).start()

        self.loop(*self.span(True), step)

    def settle(self, outs):
        for k, out in enumerate(outs):
            out[...] = self.both(k, 0)

        def step(k, da):
            self.send_far(k, da).wait()
            outs[k][...] += self.grads[k][5][da].astype(f32)

        self.loop(*self.span(True), step)

    @staticmethod
    def scratch(shapes, parts):
        quarter = parts // 4
        slots = []
        for rows, columns in shapes:
            piece = (rows // parts, columns)
            slots.append(pltpu.VMEM((2, quarter) + piece, bf16))
            slots += [pltpu.VMEM((quarter,) + piece, bf16)] * 4
        dma = pltpu.SemaphoreType.DMA
        count = len(shapes)
        return slots, [dma((count, 2, quarter))] * 2 + [dma((count, quarter))] * 4


def row_mean(x):
    return jnp.mean(x, axis=1, keepdims=True)


def col_sum(x):
    return jnp.sum(x, axis=0, keepdims=True)


def folded(line):
    return jnp.concatenate([line[:, 128 * i : 128 * i + 128] for i in range(8)], axis=0)


def fold_sum(line):
    return col_sum(folded(line))


class JoinedSum(ScatterSum):
    def __init__(self, grads, sems, parts, first):
        super().__init__([(g[0], *g[4:]) for g in grads], sems, parts)
        self.own = grads[0][0].shape[1] // parts
        self.operands = [g[0:4] for g in grads]
        self.first = first

    def side_of(self, first, second):
        return 2 * first + second if self.first == "z" else 2 * second + first

    def mine(self):
        return (self.b, self.x) if self.first == "z" else (self.x, self.b)

    def place(self, da, side, flip=0):
        first, second = self.mine()
        first = 1 - first if flip else first
        second = second if side == 1 else 1 - second
        return 4 * lax.rem(self.a + da, self.quarter) + self.side_of(first, second)

    def partner(self):
        return self.place(0, 1, 1)

    def columns(self, place):
        return pl.ds(pl.multiple_of(place * self.own, self.own), self.own)

    def cross_blocks(self, k, sems):
        left, slots = self.operands[k][0:2]
        first, _ = self.mine()
        copies = []
        for block in range(2 * self.quarter):
            place = 4 * (block // 2) + self.side_of(1 - first, block % 2)
            copies.append(
                send(
                    left.at[:, self.columns(place)],
                    slots.at[:, pl.ds(block * self.own, self.own)],
                    sems[0].at[block],
                    sems[1].at[block],
                    "seq",
                    self.partner(),
                )
            )
        return copies

    def cross(self, k, sems):
        right, slots = self.operands[k][2:4]
        return [send(right, slots, sems[0].at[0], sems[1].at[0], "seq", self.partner())]

    def send_pair(self, k, da):
        ss, rs = self.sems[0:2]
        grads, peer = self.grads[k], self.place(0, 0)
        return send(grads[1].at[da], grads[2].at[da], ss.at[k, da], rs.at[k, da], "seq", peer)

    def send_far(self, k, da):
        ss, rs = self.sems[2:4]
        grads, peer = self.grads[k], self.place(da, 1)
        return send(grads[3].at[da], grads[4].at[da], ss.at[k, da], rs.at[k, da], "seq", peer)

    def column(self, k, da, side):
        left, left_other, right, right_other = self.operands[k]
        _, second = self.mine()
        second = second if side == 1 else 1 - second
        block = 2 * lax.rem(self.a + da, self.quarter) + second
        found = tn(left[:, self.columns(self.place(da, side))], right[...])
        return found + tn(left_other[:, self.columns(block)], right_other[...])

    def pair(self, far):
        def step(k, da):
            self.grads[k][1][da] = self.column(k, da, 0).astype(bf16)
            self.send_pair(k, da).start()

        self.loop(*self.span(far), step)

    def both(self, k, da):
        found = self.column(k, da, 1)
        self.send_pair(k, da).wait()
        return found + self.grads[k][2][da].astype(f32)

    def far(self):
        def step(k, da):
            self.grads[k][3][da] = self.both(k, da).astype(bf16)
            self.send_far(k, da).start()

        self.loop(*self.span(True), step)

    def settle(self, outs):
        for k, out in enumerate(outs):
            out[...] = self.both(k, 0)

        def step(k, da):
            self.send_far(k, da).wait()
            outs[k][...] += self.grads[k][4][da].astype(f32)

        self.loop(*self.span(True), step)

    @staticmethod
    def scratch(shapes, parts):
        quarter = parts // 4
        slots = []
        for rows, columns in shapes:
            slots += [pltpu.VMEM((quarter, rows // parts, columns), bf16)] * 4
        return slots, [pltpu.SemaphoreType.DMA((len(shapes), quarter))] * 4


class Product:
    def __init__(self, r, name, left, right, parts, first, left_other=None, right_other=None):
        self.left, self.right = left, right
        self.joined = left.shape[1] // parts % 128 == 0

        def own(part):
            return getattr(r, f"{name}_{part}")

        if self.joined:
            left_slots = own("left") if left_other is None else left_other
            right_slots = own("right") if right_other is None else right_other
            grads = (left, left_slots, right, right_slots, *(own(i) for i in range(4)))
            self.sum = JoinedSum([grads], [own(f"sem_{i}") for i in range(4)], parts, first)
            self.lefts, self.rights = [], []
            if left_other is None:
                self.lefts = self.sum.cross_blocks(0, (own("left_ss"), own("left_rs")))
            if right_other is None:
                self.rights = self.sum.cross(0, (own("right_ss"), own("right_rs")))
        else:
            self.whole = own("whole")
            grads = (self.whole, *(own(i) for i in range(5)))
            self.sum = ScatterSum([grads], [own(f"sem_{i}") for i in range(6)], parts)
        self.pair, self.far = self.sum.pair, self.sum.far

    def begin_left(self):
        if self.joined:
            for copy in self.lefts:
                copy.start()

    def begin(self):
        if self.joined:
            for copy in self.rights:
                copy.start()
        else:
            for b in range(self.left.shape[1] // 256):
                block = slice(256 * b, 256 * b + 256)
                self.whole[block, :] = tn(self.left[:, block], self.right[...]).astype(bf16)
            self.sum.start_one(0)

    def ready(self):
        if self.joined:
            for copy in self.lefts + self.rights:
                copy.wait()

    def settle(self, out):
        self.sum.settle((out,))

    @staticmethod
    def scratch(name, count, model, columns, parts, left=True, right=True):
        own, dma = model // parts, pltpu.SemaphoreType.DMA
        found = {}
        if own % 128 == 0:
            slots, sems = JoinedSum.scratch([(model, columns)], parts)
            if left:
                found["left"] = pltpu.VMEM((count, model // 2), bf16)
                found |= {f"left_{end}": dma((parts // 2,)) for end in ("ss", "rs")}
            if right:
                found["right"] = pltpu.VMEM((count, columns), bf16)
                found |= {f"right_{end}": dma((1,)) for end in ("ss", "rs")}
        else:
            slots, sems = ScatterSum.scratch([(model, columns)], parts)
            found["whole"] = pltpu.VMEM((model, columns), bf16)
        found |= {str(i): s for i, s in enumerate(slots)}
        found |= {f"sem_{i}": s for i, s in enumerate(sems)}
        return {f"{name}_{part}": spec for part, spec in found.items()}


def layer_kernel(*refs, names, parts, peers, scale):
    r = types.SimpleNamespace(**dict(zip(names, refs, strict=True)))
    count, width = r.q.shape
    span, model = r.pair.shape[1], r.inputs.shape[1]
    per = r.tok.shape[2]
    half = parts // 2
    me = lax.axis_index("seq")
    x, z = lax.rem(me, 2), me // 2
    partner = me + 1 - 2 * x

    def at(o, c):
        return 2 * o + (x if c == 0 else 1 - x)

    def reader(c, dz):
        return at(lax.rem(z + half - dz, half), c)

    held = Held(((r.q_all_hbm, r.q_all, r.q_sem), (r.rows_hbm, r.rows, r.rows_sem)), parts)
    held.ahead()

    def fetch(i):
        name = FETCHED[i]
        return pltpu.make_async_copy(
            getattr(r, name + "_hbm"), getattr(r, name), r.fetch_sem.at[i]
        )

    def fetch_late(i):
        place = r.w_up.at[:, pl.ds(i * width, width)]
        return pltpu.make_async_copy(
            getattr(r, LATE[i] + "_hbm"), place, r.fetch_sem.at[len(FETCHED) + i]
        )

    for i in range(len(FETCHED)):
        fetch(i).start()

    def head_sum(name, slots, source, full):
        return HeadSum(
            source,
            [getattr(r, f"{slots}_{i}") for i in range(3)],
            [getattr(r, f"{name}_sem_{i}") for i in range(4)],
            full,
            [getattr(r, f"{name}_full_{i}") for i in range(2)],
        )

    sums = head_sum("sum", "turn", r.partial, r.branch)
    feeds = head_sum("feed", "feed", r.feed_in, r.layer)
    attn = head_sum("attn", "turn", r.partial, r.normed_two)
    cot_other = getattr(r, "cot_other", None)
    normed_other = getattr(r, "normed_other", None)
    mixed_other = getattr(r, "mixed_other", None)
    p_down = Product(r, "down", r.cot, r.hidden, parts, "z", left_other=cot_other)
    p_up = Product(r, "up", r.normed_two, r.grad_upward, parts, "x")
    p_o = Product(r, "o", r.branch, r.mixed, parts, "x", right_other=mixed_other)
    p_kv = Product(r, "kv", r.normed, r.d_kv, parts, "x", left_other=normed_other)
    p_q = Product(r, "q", r.normed, r.d_q, parts, "x", left_other=normed_other)
    ids = lax.broadcasted_iota(jnp.int32, (count, per), 0)

    own_pair = [
        pltpu.make_async_copy(source, r.pair.at[i, pl.ds(W, count)], r.own_sem.at[i])
        for i, source in enumerate((r.k_hbm, r.v_hbm))
    ]
    for copy in own_pair:
        copy.start()
    @pl.when(z == 0)
    def _():
        r.pair[:, :count] = jnp.zeros_like(r.pair[:, :count])

    @pl.when(me == 0)
    def _():
        r.pair[:, count:W] = jnp.zeros_like(r.pair[:, count:W])


    for copy in own_pair:
        copy.wait()
    greet(seq=parts, head=peers)

    def pair_rows(first):
        return r.pair.at[:, pl.ds(first, count)]

    def hand_on(i, source, target, peer):
        return send(
            pair_rows(source), pair_rows(target), r.next_ss.at[i], r.next_rs.at[i], "seq", peer
        )

    next_one = hand_on(0, W, count, partner)
    next_two = hand_on(1, W, 0, me + 2)
    passed_on = hand_on(2, 0, count, partner)

    @pl.when(z < half - 1)
    def _():
        next_two.start()

    @pl.when(x == 0)
    def _():
        next_one.start()

    def recall_part(j):
        q_at, rows_at = held.get(j)
        outs, logs = [], []
        for h in range(2):
            cols = head_cols(h)
            keep = r.tok[j, h : h + 1, :] == ids
            s = jnp.where(keep, nt(q_at[:, cols], rows_at[h, :, 0:128]), NEG)
            top = jnp.max(s, axis=1, keepdims=True)
            p = jnp.exp((s - top) * scale)
            total = jnp.sum(p, axis=1, keepdims=True)
            some = top > 0.5 * NEG
            outs.append(
                nn(p.astype(bf16), rows_at[h, :, 128:256]) * jnp.where(some, 1.0 / total, 0.0)
            )
            logs.append(jnp.where(some, top * scale + jnp.log(total), NEG))
        return outs, logs

    def out_x(dz):
        return (
            send(r.log_xs.at[dz], r.log_xr.at[dz], r.lx_ss.at[dz], r.lx_rs.at[dz], "seq", partner),
            send(r.dq_xs.at[dz], r.dq_xr.at[dz], r.ox_ss.at[dz], r.ox_rs.at[dz], "seq", partner),
        )

    def log_z(dz):
        return send(
            r.log_zs.at[dz], r.log_zr.at[dz], r.lz_ss.at[dz], r.lz_rs.at[dz], "seq", reader(0, dz)
        )

    def out_z(dz):
        return send(
            r.dq_zs.at[dz], r.dq_zr.at[dz], r.oz_ss.at[dz], r.oz_rs.at[dz], "seq", reader(0, dz)
        )

    def lend(dz):
        outs, logs = recall_part(reader(1, dz))
        for h in range(2):
            r.dq_xs[dz, h] = outs[h].astype(bf16)
        r.log_xs[dz] = row_form(logs, count).T[0:8]
        for copy in out_x(dz):
            copy.start()

    def unite(outs, logs, dz):
        for copy in out_x(dz):
            copy.wait()
        other = r.log_xr[dz].T
        joined = []
        for h in range(2):
            theirs = other[:, h : h + 1]
            top = jnp.maximum(logs[h], theirs)
            a, b = jnp.exp(logs[h] - top), jnp.exp(theirs - top)
            total = a + b
            outs[h] = outs[h] * (a / total) + r.dq_xr[dz, h].astype(f32) * (b / total)
            joined.append(top + jnp.log(total))
        return outs, joined

    def lend_step(dz, carry):
        lend(dz)
        return carry

    lax.fori_loop(1, half, lend_step, 0)
    lend(0)

    @pl.when(z > 0)
    def _():
        hand_on(1, W, 0, partner).wait_recv()

        @pl.when(x == 1)
        def _():
            passed_on.start()

    def keep_step(dz, carry):
        outs, logs = recall_part(reader(0, dz))
        outs, logs = unite(outs, logs, dz)
        for h in range(2):
            r.dq_zs[dz, h] = outs[h].astype(bf16)
        r.log_zs[dz] = row_form(logs, count).T[0:8]
        log_z(dz).start()
        out_z(dz).start()
        return carry

    lax.fori_loop(1, half, keep_step, 0)
    outs, logs = recall_part(me)
    outs, logs = unite(outs, logs, 0)
    r.log_zr[0] = row_form(logs, count).T[0:8]
    for h in range(2):
        r.recalled[:, head_cols(h)] = outs[h]

    @pl.when(x == 0)
    def _():
        next_one.wait_send()

        @pl.when(z > 0)
        def _():
            passed_on.wait_recv()

    @pl.when(x == 1)
    def _():
        next_one.wait_recv()

        @pl.when(z > 0)
        def _():
            passed_on.wait_send()

    @pl.when(z < half - 1)
    def _():
        next_two.wait_send()

    first = me * count
    start = doc_starts(r.lengths, first, count)
    key_place = first - W + lax.broadcasted_iota(jnp.int32, (count, span), 1)
    seen = key_place >= start
    for h in range(2):
        cols = head_cols(h)
        bias = pltpu.roll(
            jnp.broadcast_to(r.bias[h : h + 1, :], (count, span)), 0, 1, stride=1, stride_axis=0
        )
        s = nt(r.q[:, cols], r.pair[0, :, cols]) * scale + bias
        s = jnp.where(seen, s, NEG)
        raised = jnp.exp(s - jnp.max(s, axis=1, keepdims=True))
        p = raised / jnp.sum(raised, axis=1, keepdims=True)
        r.p[h] = p
        r.local[:, cols] = nn(p.astype(bf16), r.pair[1, :, cols])

    def wait_log(dz, top):
        log_z(dz).wait()
        return jnp.maximum(top, r.log_zr[dz])

    top = lax.fori_loop(1, half, wait_log, r.log_zr[0])

    def add_to(dz, total):
        return total + jnp.exp(r.log_zr[dz] - top)

    logs = top + jnp.log(lax.fori_loop(0, half, add_to, jnp.zeros_like(top)))
    r.logs[...] = logs
    share = jnp.exp(r.log_zr[0] - logs).T
    for h in range(2):
        r.recalled[:, head_cols(h)] *= share[:, h : h + 1]

    def gather_out(dz, carry):
        share = jnp.exp(r.log_zr[dz] - logs).T
        out_z(dz).wait()
        for h in range(2):
            r.recalled[:, head_cols(h)] += share[:, h : h + 1] * r.dq_zr[dz, h].astype(f32)
        return carry

    lax.fori_loop(1, half, gather_out, 0)
    for h in range(2):
        cols = head_cols(h)
        gate = r.gate[h]
        mixed = gate * r.recalled[:, cols] + (1.0 - gate) * r.local[:, cols]
        r.mixed[:, cols] = mixed.astype(bf16)


    for i in range(len(FETCHED)):
        fetch(i).wait()
    for b in range(model // 256):
        block = slice(256 * b, 256 * b + 256)
        r.partial[:, block] = nn(r.mixed[...], r.w_o[:, block]).astype(bf16)
    attn.start()
    crossing = []
    if cot_other is not None:
        for name, first, left, other in (("cot", "z", r.cot, cot_other), ("normed", "x", r.normed, normed_other)):
            joined = JoinedSum([(left, other, left, left)], [None] * 4, parts, first)
            sems = getattr(r, f"{name}_ss"), getattr(r, f"{name}_rs")
            crossing += joined.cross_blocks(0, sems)
        joined = JoinedSum([(r.normed, r.normed, r.mixed, mixed_other)], [None] * 4, parts, "x")
        crossing += joined.cross(0, (r.mixed_ss, r.mixed_rs))
        for copy in crossing:
            copy.start()
    attn.relay()
    branch = attn.total()
    middle = r.inputs[attn.mine, :].astype(f32) + branch
    r.middle[...] = middle
    row_scale = lax.rsqrt(row_mean(middle * middle) + eps)
    hat = middle * row_scale
    attn.spread(hat * r.gain_two[...])
    r.small_send[17:18] = fold_sum(col_sum(branch * branch))
    attn.forward()
    attn.settle()

    p_up.begin_left()
    for b in range(r.hidden.shape[1] // 256):
        block = slice(256 * b, 256 * b + 256)
        up = nn(r.normed_two[...], r.w_up[:, block])
        square = up * up
        bent = jnp.tanh(GELU * (up + 0.044715 * up * square))
        rise = 0.5 * (1.0 + bent)
        r.hidden[:, block] = (up * rise).astype(bf16)
        steep = (0.5 * GELU) * up * (1.0 - bent * bent) * (1.0 + (3 * 0.044715) * square)
        r.slope[:, block] = rise + steep
    p_down.begin()
    for b in range(r.hidden.shape[1] // 256):
        block = slice(256 * b, 256 * b + 256)
        back = nt(r.cot[...], r.w_down[block, :])
        r.grad_upward[:, block] = (r.slope[:, block] * back).astype(bf16)
    p_up.begin()
    for b in range(model // 256):
        block = slice(256 * b, 256 * b + 256)
        r.partial[:, block] = nt(r.grad_upward[...], r.w_up[block, :]).astype(bf16)

    sums.start()
    for i in range(len(LATE)):
        fetch_late(i).start()
    sums.relay()
    for b in range(model // 256):
        block = slice(256 * b, 256 * b + 256)
        r.feed_in[:, block] = nn(r.hidden[...], r.w_down[:, block]).astype(bf16)
    feeds.start()
    grad_normed = sums.total()
    scaled = grad_normed * r.gain_two[...]
    grad_middle = r.cot[sums.mine, :].astype(f32) + row_scale * (
        scaled - hat * row_mean(scaled * hat)
    )
    sums.spread(grad_middle)
    r.grad_middle[...] = grad_middle
    r.small_send[8:16] = folded(col_sum(grad_normed * hat))
    feeds.relay()
    sums.forward()
    sums.settle()
    g_own = nt(r.branch[...], r.w_o[...]).astype(bf16)
    r.g_all[0, z] = g_own

    deltas = []
    for h in range(2):
        cols = head_cols(h)
        g = g_own[:, cols].astype(f32)
        r.small_send[19 + h : 20 + h] = col_sum(g * (r.recalled[:, cols] - r.local[:, cols]))
        both = jnp.sum(g * r.recalled[:, cols], axis=1, keepdims=True)
        deltas.append(both * r.gate[h])
    turned = row_form([jnp.zeros_like(deltas[0])] * 2 + deltas, count).T[0:8]
    row = lax.broadcasted_iota(jnp.int32, (8, count), 0)
    r.st_all[0, z] = jnp.where(row < 2, r.logs[...], turned)

    def ask(c, o, way, peer):
        return (
            send(
                r.st_all.at[0, o], r.st_all.at[c, o], r.st_ss.at[way, o], r.st_rs.at[c, o], "seq", peer
            ),
            send(r.g_all.at[0, o], r.g_all.at[c, o], r.g_ss.at[way, o], r.g_rs.at[c, o], "seq", peer),
        )

    def start(copies):
        for copy in copies:
            copy.start()

    def up(o):
        return ask(0, o, 0, me + 2)

    def down(o):
        return ask(0, o, 1, me - 2)

    def across(o):
        return ask(1, o, 2, partner)

    def arrived(c, o):
        for copy in ask(c, o, 2, partner):
            copy.wait_recv()

    def sent(copies):
        for copy in copies:
            copy.wait_send()

    @pl.when(z < half - 1)
    def _():
        start(up(z))

    @pl.when(z > 0)
    def _():
        start(down(z))

    start(across(z))
    for copy in crossing:
        copy.wait_recv()
    p_down.ready()
    p_down.pair(True)

    for h in range(2):
        cols = head_cols(h)
        rest = 1.0 - r.gate[h]
        g = r.g_all[0, z, :, cols]
        p = r.p[h]
        e = nt(g, r.pair[1, :, cols])
        delta = jnp.sum(p * e, axis=1, keepdims=True)
        ds = (p * ((e - delta) * rest)).astype(bf16)
        r.dq_sum[:, cols] = nn(ds, r.pair[0, :, cols]) * scale
        dk = tn(ds, r.q[:, cols]) * scale
        dv = tn(p.astype(bf16), g) * rest
        r.pair_sum[0, :, cols] = dk[W:]
        r.pair_sum[1, :, cols] = dv[W:]
        r.pair_send[0, :, cols] = dk[:W].astype(bf16)
        r.pair_send[1, :, cols] = dv[:W].astype(bf16)
        low = ds.astype(f32)
        acc = low[0:8]
        for a in range(1, count // 8):
            acc = acc + pltpu.roll(low[8 * a : 8 * a + 8], (span - 8 * a) % span, 1)
        line = acc[0:1]
        for b in range(1, 8):
            line = line + pltpu.roll(acc[b : b + 1], span - b, 1)
        lines = span // 128
        for i in range(lines):
            r.small_send[24 + h * lines + i : 25 + h * lines + i] = line[:, 128 * i : 128 * i + 128]

    halo_x = send(
        r.pair_send.at[:, pl.ds(count, count)], r.halo_x, r.halo_ss.at[0], r.halo_rs.at[0], "seq", partner
    )
    halo_z = send(r.halo_send, r.halo_z, r.halo_ss.at[1], r.halo_rs.at[1], "seq", me - 2)

    def owner_part(c, o):
        j = at(o, c)
        q_at, rows_at = held.get(j, again=True)
        stats = r.st_all[c, o].T
        found = []
        for h in range(2):
            cols = head_cols(h)
            keep = r.tok[j, h : h + 1, :] == ids
            s = nt(q_at[:, cols], rows_at[h, :, 0:128]) * scale
            p = jnp.exp(jnp.where(keep, s - stats[:, h : h + 1], NEG))
            e = nt(r.g_all[c, o, :, cols], rows_at[h, :, 128:256]) * r.gate[h]
            ds = (p * (e - stats[:, 2 + h : 3 + h])).astype(bf16)
            found.append(nn(ds, rows_at[h, :, 0:128]) * scale)
        return found

    own = owner_part(0, z)
    for h in range(2):
        r.dq_sum[:, head_cols(h)] += own[h]

    def give_x(o):
        return send(r.dq_xs.at[o], r.dq_xr.at[o], r.dx_ss.at[o], r.dx_rs.at[o], "seq", partner)

    def give_z(o):
        return send(r.dq_zs.at[o], r.dq_zr.at[z], r.dz_ss.at[o], r.dz_rs.at[z], "seq", at(o, 0))

    def got_z(o):
        return send(r.dq_zs.at[o], r.dq_zr.at[o], r.dz_ss.at[o], r.dz_rs.at[o], "seq", partner)

    def neighbour(o):
        arrived(1, o)
        found = owner_part(1, o)
        for h in range(2):
            r.dq_xs[o, h] = found[h].astype(bf16)
        give_x(o).start()

    def column(o):
        found = owner_part(0, o)
        for h in range(2):
            r.dq_zs[o, h] = found[h].astype(bf16)

    def near(body):
        def step(t, carry):
            @pl.when(z - t >= 0)
            def _():
                body(z - t, True)

            @pl.when(z + t < half)
            def _():
                body(z + t, False)

            return carry

        lax.fori_loop(1, half, step, 0)

    neighbour(z)

    def relay(o, below):
        arrived(0, o)
        start(across(o))
        if below:

            @pl.when(z < half - 1)
            def _():
                start(up(o))

        else:

            @pl.when(z > 0)
            def _():
                start(down(o))

    def relay_step(t, carry):
        @pl.when(z - t >= 0)
        def _():
            relay(z - t, True)

        @pl.when(z + t < half)
        def _():
            relay(z + t, False)

        @pl.when(z - t >= 0)
        def _():
            column(z - t)

        @pl.when(z + t < half)
        def _():
            column(z + t)

        return carry

    lax.fori_loop(1, half, relay_step, 0)
    p_up.ready()
    p_up.pair(True)
    feed_sum = feeds.total()
    layer = r.middle[...] + feed_sum
    feeds.spread(layer)
    r.small_send[16:17] = fold_sum(col_sum(layer * layer))
    r.small_send[18:19] = fold_sum(col_sum(feed_sum * feed_sum))
    near(lambda o, below: neighbour(o))
    halo_x.start()
    p_o.begin_left()
    p_o.begin()

    def join(o, below):
        give_x(o).wait()
        for h in range(2):
            both = r.dq_zs[o, h].astype(f32) + r.dq_xr[o, h].astype(f32)
            r.dq_zs[o, h] = both.astype(bf16)
        give_z(o).start()

    near(join)
    halo_x.wait()
    passing = x.astype(f32)
    r.halo_send[...] = (
        r.pair_send[:, :count].astype(f32) + r.halo_x[...].astype(f32) * passing
    ).astype(bf16)
    r.pair_sum[...] += r.halo_x[...].astype(f32) * (1.0 - passing)

    @pl.when(z > 0)
    def _():
        halo_z.start()

    feeds.forward()
    give_x(z).wait()
    for h in range(2):
        r.dq_sum[:, head_cols(h)] += r.dq_xr[z, h].astype(f32)

    def merge(o, below):
        got_z(o).wait_recv()
        for h in range(2):
            r.dq_sum[:, head_cols(h)] += r.dq_zr[o, h].astype(f32)

    near(merge)
    p_up.pair(False)
    p_down.pair(False)

    r.d_q[...] = r.dq_sum[...].astype(bf16)
    p_q.begin()
    p_down.far()
    p_up.far()
    @pl.when(z > 0)
    def _():
        halo_z.wait_send()

    @pl.when(z < half - 1)
    def _():
        send(r.halo_send, r.halo_z, r.halo_ss.at[1], r.halo_rs.at[1], "seq", partner).wait_recv()
        r.pair_sum[...] += r.halo_z[...].astype(f32)

    r.d_kv[:, :width] = r.pair_sum[0].astype(bf16)
    r.d_kv[:, width:] = r.pair_sum[1].astype(bf16)
    p_kv.begin()
    for i in range(len(LATE)):
        fetch_late(i).wait()
    for b in range(model // 256):
        block = slice(256 * b, 256 * b + 256)
        r.partial[:, block] = (
            nt(r.d_q[...], r.w_up[block, :width])
            + nt(r.d_kv[...], r.w_up[block, width : 3 * width])
        ).astype(bf16)
    backs = head_sum("back", "turn", r.partial, r.input_grad)
    backs.start()
    backs.relay()
    p_o.ready()
    p_o.pair(True)
    p_kv.ready()
    p_kv.pair(True)
    tokens = r.inputs[backs.mine, :].astype(f32)
    in_scale = lax.rsqrt(row_mean(tokens * tokens) + eps)
    in_hat = tokens * in_scale
    back_sum = backs.total()
    g = back_sum * r.gain_one[...]
    backs.spread(r.grad_middle[...] + in_scale * (g - in_hat * row_mean(g * in_hat)))
    r.small_send[0:8] = folded(col_sum(back_sum * in_hat))
    r.small_send[21:24] = jnp.zeros((3, 128), f32)
    r.small_send[36:40] = jnp.zeros((4, 128), f32)

    def small_heads(d):
        peer = lax.rem(lax.axis_index("head") + d, peers)
        return send(r.small_send, r.small_head.at[d], r.sh_ss.at[d], r.sh_rs.at[d], "head", peer)

    for d in range(1, peers):
        small_heads(d).start()
    p_q.ready()
    p_q.pair(True)
    backs.forward()
    p_o.far()
    p_kv.far()

    kept = lax.broadcasted_iota(jnp.int32, r.small_send.shape, 0) < 19
    found = r.small_send[...]
    for d in range(1, peers):
        small_heads(d).wait()
        found = found + jnp.where(kept, r.small_head[d], 0.0)
    r.small_seq[0] = found

    def small_seqs(d):
        peer = lax.rem(me + d, parts)
        return send(r.small_seq.at[0], r.small_seq.at[d], r.sq_ss.at[d], r.sq_rs.at[d], "seq", peer)

    def small_start(d, carry):
        small_seqs(d).start()
        return carry

    lax.fori_loop(1, parts, small_start, 0)
    p_o.pair(False)
    p_kv.pair(False)
    p_q.far()
    p_q.pair(False)
    p_down.settle(r.down_sum)
    r.down_out[...] = r.down_sum[...].T
    p_up.settle(r.up_out)
    p_o.settle(r.o_sum)
    p_kv.settle(r.kv_sum)
    r.k_out[...] = r.kv_sum[:, :width]
    r.v_out[...] = r.kv_sum[:, width:]
    r.o_out[...] = r.o_sum[...].T
    p_q.settle(r.q_out)
    r.small[...] = r.small_seq[0]

    def small_add(d, carry):
        small_seqs(d).wait()
        r.small[...] += r.small_seq[d]
        return carry

    lax.fori_loop(1, parts, small_add, 0)
    feeds.settle()
    backs.settle()

    sent(across(z))

    @pl.when(z < half - 1)
    def _():
        sent(up(z))

    @pl.when(z > 0)
    def _():
        sent(down(z))

    def drain(o, below):
        sent(across(o))
        give_z(o).wait_send()
        if below:

            @pl.when(z < half - 1)
            def _():
                sent(up(o))

        else:

            @pl.when(z > 0)
            def _():
                sent(down(o))

    near(drain)
    for copy in crossing:
        copy.wait_send()


FETCHED = ("cot", "w_o", "w_up", "w_down")
LATE = ("w_q", "w_k", "w_v")
GELU = math.sqrt(2 / math.pi)


def layer(inputs, parts, peers):
    count, width = inputs["q"].shape
    model, span = inputs["inputs"].shape[1], W + count
    half, own = parts // 2, model // parts
    smem = pl.BlockSpec(memory_space=pltpu.SMEM)
    vmem = pl.BlockSpec(memory_space=pltpu.VMEM)
    hbm = pl.BlockSpec(memory_space=pltpu.HBM)
    dma = pltpu.SemaphoreType.DMA
    wide = inputs["w_up_hbm"].shape[1]
    outputs = dict(
        input_grad=((count, model), bf16),
        layer=((count, model), bf16),
        q_out=((own, width), f32),
        k_out=((own, width), f32),
        v_out=((own, width), f32),
        o_out=((width, own), f32),
        up_out=((own, wide), f32),
        down_out=((wide, own), f32),
        small=((40, 128), f32),
    )
    outputs = {name: jax.ShapeDtypeStruct(*spec) for name, spec in outputs.items()}
    held = Held.scratch((inputs["q_all_hbm"], inputs["rows_hbm"]), parts)
    scratch = dict(zip(("q_all", "rows", "q_sem", "rows_sem"), held, strict=True))
    scratch |= {name: pltpu.VMEM(inputs[name + "_hbm"].shape, bf16) for name in FETCHED}
    for name, spec in dict(
        recalled=((count, width), f32),
        local=((count, width), f32),
        mixed=((count, width), bf16),
        logs=((8, count), f32),
        p=((2, count, span), f32),
        pair=((2, span, width), bf16),
        log_xs=((half, 8, count), f32),
        log_xr=((half, 8, count), f32),
        log_zs=((half, 8, count), f32),
        log_zr=((half, 8, count), f32),
        normed_two=((count, model), bf16),
        middle=((count // peers, model), f32),
        hidden=((count, wide), bf16),
        slope=((count, wide), f32),
        grad_upward=((count, wide), bf16),
        partial=((count, model), bf16),
        feed_in=((count, model), bf16),
        branch=((count, model), bf16),
        grad_middle=((count // peers, model), f32),
        g_all=((2, half, count, width), bf16),
        st_all=((2, half, 8, count), f32),
        dq_xs=((half, 2, count, 128), bf16),
        dq_xr=((half, 2, count, 128), bf16),
        dq_zs=((half, 2, count, 128), bf16),
        dq_zr=((half, 2, count, 128), bf16),
        pair_send=((2, W, width), bf16),
        pair_sum=((2, count, width), f32),
        halo_x=((2, count, width), bf16),
        halo_send=((2, count, width), bf16),
        halo_z=((2, count, width), bf16),
        dq_sum=((count, width), f32),
        d_kv=((count, 2 * width), bf16),
        d_q=((count, width), bf16),
        kv_sum=((own, 2 * width), f32),
        o_sum=((own, width), f32),
        down_sum=((own, wide), f32),
        small_send=((40, 128), f32),
        small_head=((peers, 40, 128), f32),
        small_seq=((parts, 40, 128), f32),
    ).items():
        scratch[name] = pltpu.VMEM(*spec)
    for name, shape in dict(
        fetch_sem=(len(FETCHED) + len(LATE),),
        own_sem=(2,),
        next_ss=(3,),
        next_rs=(3,),
        ox_ss=(half,),
        ox_rs=(half,),
        oz_ss=(half,),
        oz_rs=(half,),
        lx_ss=(half,),
        lx_rs=(half,),
        lz_ss=(half,),
        lz_rs=(half,),
        st_ss=(3, half),
        st_rs=(2, half),
        g_ss=(3, half),
        g_rs=(2, half),
        dx_ss=(half,),
        dx_rs=(half,),
        dz_ss=(half,),
        dz_rs=(half,),
        halo_ss=(2,),
        halo_rs=(2,),
        sh_ss=(peers,),
        sh_rs=(peers,),
        sq_ss=(parts,),
        sq_rs=(parts,),
    ).items():
        scratch[name] = dma(shape)
    for name in ("turn", "feed"):
        scratch |= {f"{name}_{i}": s for i, s in enumerate(HeadSum.scratch(count, model))}
    for name in ("attn", "sum", "feed", "back"):
        scratch |= {f"{name}_sem_{i}": s for i, s in enumerate(HeadSum.sems())}
        scratch |= {f"{name}_full_{i}": s for i, s in enumerate(HeadSum.full_scratch())}
    if own % 128 == 0:
        for name in ("cot", "normed"):
            scratch[f"{name}_other"] = pltpu.VMEM((count, model // 2), bf16)
            scratch |= {f"{name}_{end}": dma((half,)) for end in ("ss", "rs")}
        scratch["mixed_other"] = pltpu.VMEM((count, width), bf16)
        scratch |= {f"mixed_{end}": dma((1,)) for end in ("ss", "rs")}
    for name, columns, left, right in (
        ("down", wide, False, True),
        ("up", wide, True, True),
        ("o", width, True, False),
        ("kv", 2 * width, False, True),
        ("q", width, False, True),
    ):
        scratch |= Product.scratch(name, count, model, columns, parts, left, right)
    spaces = dict(gate=smem, lengths=smem)
    spaces |= {name: hbm for name in inputs if name.endswith("_hbm")}
    found = pl.pallas_call(
        functools.partial(
            layer_kernel,
            names=(*inputs, *outputs, *scratch),
            parts=parts,
            peers=peers,
            scale=128**-0.5,
        ),
        out_shape=tuple(outputs.values()),
        in_specs=[spaces.get(name, vmem) for name in inputs],
        out_specs=(vmem,) * len(outputs),
        scratch_shapes=list(scratch.values()),
        compiler_params=pltpu.CompilerParams(
            vmem_limit_bytes=(58 if parts <= 8 else 63) * MIB, collective_id=2, has_side_effects=True
        ),
        cost_estimate=pl.CostEstimate(
            flops=4 * 10**9, bytes_accessed=150 * MIB, transcendentals=5 * 10**6
        ),
        name="layer",
    )(*inputs.values())
    return dict(zip(outputs, found, strict=True))


def hand_out_kernel(*refs, copied, entries):
    count = len(copied)
    sources, (input_grad, small, gate, hot), outs = refs[:count], refs[count : count + 4], refs[count + 4 :]
    grad_out, one_out, two_out, position_out, gate_out, rms_out = outs[count : count + 6]
    for source, out in zip(sources, outs):
        out[...] = source[...]
    grad_out[...] = input_grad[...].astype(f32)
    me = lax.axis_index("seq")
    if one_out.shape[0] == 1:
        one_out[...] = small[pl.ds(me, 1), :]
        two_out[...] = small[pl.ds(me + 8, 1), :]
    else:
        one_out[...] = small[0:8, :]
        two_out[...] = small[8:16, :]
    lines = hot.shape[0] // 128
    for h in range(2):
        found = jnp.zeros((1, hot.shape[1]), f32)
        for i in range(lines):
            line = small[24 + h * lines + i : 25 + h * lines + i, :]
            found = found + lax.dot_general(
                line,
                hot[128 * i : 128 * i + 128, :],
                (((1,), (0,)), ((), ())),
                precision=highest,
                preferred_element_type=f32,
            )
        position_out[h : h + 1, :] = found
    sums = jnp.sum(small[16:24, :], axis=1, keepdims=True)
    lane = lax.broadcasted_iota(jnp.int32, (1, 2), 1)
    steep = jnp.where(lane == 0, gate[0] * (1.0 - gate[0]), gate[1] * (1.0 - gate[1]))
    gate_out[...] = jnp.where(lane == 0, sums[3:4], sums[4:5]) * steep
    lane = lax.broadcasted_iota(jnp.int32, (1, 3), 1)
    squares = jnp.where(lane == 0, sums[0:1], jnp.where(lane == 1, sums[1:2], sums[2:3]))
    rms_out[...] = jnp.sqrt(squares / entries)


def hand_out(done, gate, hot, entries, parts):
    copied = ("layer", "q_out", "k_out", "v_out", "o_out", "up_out", "down_out")
    smem = pl.BlockSpec(memory_space=pltpu.SMEM)
    vmem = pl.BlockSpec(memory_space=pltpu.VMEM)
    model = done["input_grad"].shape[1]
    own = model // parts
    shapes = [jax.ShapeDtypeStruct(done[name].shape, done[name].dtype) for name in copied]
    shapes += [
        jax.ShapeDtypeStruct(shape, f32)
        for shape in (
            done["input_grad"].shape,
            *[(1 if own == 128 else 8, 128)] * 2,
            (2, hot.shape[1]),
            (1, 2),
            (1, 3),
        )
    ]
    found = pl.pallas_call(
        functools.partial(hand_out_kernel, copied=copied, entries=entries),
        out_shape=tuple(shapes),
        in_specs=[vmem] * len(copied) + [vmem, vmem, smem, vmem],
        out_specs=(vmem,) * (len(copied) + 6),
        compiler_params=pltpu.CompilerParams(vmem_limit_bytes=62 * MIB),
        name="hand_out",
    )(*(done[name] for name in copied), done["input_grad"], done["small"], gate, hot)
    named = dict(zip(copied, found))
    named |= dict(zip(("input_grad", "gain_one", "gain_two", "position", "gate", "rms"), found[len(copied) :]))
    return named


def norm_stats(values):
    row_scale = lax.rsqrt(jnp.mean(values * values, axis=-1, keepdims=True) + eps)
    return (values * row_scale, row_scale)


def per_device(
    inputs,
    cotangent,
    query_weight,
    key_weight,
    value_weight,
    output_weight,
    up_weight,
    down_weight,
    first_gain,
    second_gain,
    position_bias,
    gate_bias,
    memory_table,
    retrieved,
    lengths,
):
    _, block_len, model_width = inputs.shape
    bucket_total = position_bias.shape[1]
    seq_count = lax.axis_size("seq")
    slot_count = memory_table.shape[0]

    wanted = jnp.transpose(retrieved[0], (1, 0, 2))
    token = jnp.arange(block_len, dtype=jnp.int32)[None, :, None]
    codes = (wanted // slot_count) * (block_len * slot_count) + token * slot_count + wanted % slot_count
    codes = lax.sort(codes.reshape(2, -1), dimension=1, is_stable=False)
    hot, outside = diagonal_buckets(block_len, bucket_total)
    bias_row = jnp.dot(position_bias, hot, precision=highest) + outside[None]

    x, cot = inputs[0], cotangent[0]
    peers = lax.axis_size("head")
    gate_flat = jax.nn.sigmoid(gate_bias)
    hat_one, _ = norm_stats(x.astype(f32))
    normed_one = (hat_one * first_gain).astype(bf16)
    queries = nn(normed_one, query_weight).astype(bf16)
    places, tok, keys, values = request(
        codes, normed_one, key_weight, value_weight, seq_count, slot_count, block_len
    )
    rows = gather_rows(places, widen(memory_table), tok.shape)
    q_all = lax.all_gather(queries, "seq", axis=0)

    done = layer(
        dict(
            lengths=lengths[0],
            gate=gate_flat,
            q=queries,
            k_hbm=keys,
            v_hbm=values,
            bias=bias_row,
            tok=tok,
            inputs=x,
            normed=normed_one,
            gain_one=first_gain[None],
            gain_two=second_gain[None],
            q_all_hbm=q_all,
            rows_hbm=rows,
            cot_hbm=cot,
            w_o_hbm=output_weight,
            w_up_hbm=up_weight,
            w_down_hbm=down_weight,
            w_q_hbm=query_weight,
            w_k_hbm=key_weight,
            w_v_hbm=value_weight,
        ),
        seq_count,
        peers,
    )
    entries = float(block_len * model_width * seq_count)
    out = hand_out(done, gate_flat, jnp.asarray(hot.T), entries, seq_count)
    share = model_width // seq_count
    gains = [out["gain_one"].reshape(-1), out["gain_two"].reshape(-1)]
    if share != 128:
        start = lax.axis_index("seq") * share
        gains = [lax.dynamic_slice_in_dim(gain, start, share) for gain in gains]
    return (
        out["layer"][None],
        out["input_grad"][None],
        out["q_out"],
        out["k_out"],
        out["v_out"],
        out["o_out"],
        out["up_out"],
        out["down_out"],
        gains[0],
        gains[1],
        out["position"],
        out["gate"][0],
        out["rms"][0],
    )


def solution(mesh):
    in_specs = (
        P(None, "seq", None),
        P(None, "seq", None),
        P(None, "head"),
        P(None, "head"),
        P(None, "head"),
        P("head", None),
        P(None, "head"),
        P("head", None),
        P(),
        P(),
        P("head", None),
        P("head"),
        P("seq", "head", None),
        P(None, "seq", "head", None),
        P(),
    )
    out_specs = (
        P(None, "seq", None),
        P(None, "seq", None),
        P("seq", "head"),
        P("seq", "head"),
        P("seq", "head"),
        P("head", "seq"),
        P("seq", "head"),
        P("head", "seq"),
        P("seq"),
        P("seq"),
        P("head", None),
        P("head"),
        P(),
    )
    return jax.shard_map(
        per_device, mesh=mesh, in_specs=in_specs, out_specs=out_specs, check_vma=False
    )
```
